512 devices in a mesh: dp: 64 (over z_hi, y, core), width: 8 (over z_lo, x).
Axes of the slice: x: 4, y: 8, z: 8 (z_hi: 4, z_lo: 2; z = z_hi * 2 + z_lo), core: 2. Of those that a mesh axis runs over, the one named last changes fastest.
Arguments:
- image_emb: bfloat16 [1152, 16384], P('width', 'dp'), may hold values from -0.17675781 to 0.17675781
- text_emb: bfloat16 [1152, 16384], P('width', 'dp'), may hold values from -0.17675781 to 0.17675781
- pair_offsets: int32 [12], replicated, may hold values from 0 to 255
- log_scale: float32 [1], replicated, may hold values from 1.5 to 2.5
- bias: float32 [1], replicated, may hold values from -3 to -1
Outputs:
- image_grad: float32 [1152, 16384], P('width', 'dp')
- text_grad: float32 [1152, 16384], P('width', 'dp')
The draws below stay inside these ranges and needn't reach their ends.
All inputs are finite; a program needn't handle non-finite values.
Results may differ from the reference program's by a relative error of at most 0.0042.
Values may be sent and summed in bfloat16 or wider, within the bound.
A program may use at most 64 MiB of HBM per device.

```python
import jax
import jax.numpy as jnp
from jax import lax

D = 1152
B_DEV = 256
CYCLE = 12
PAIRS = 16384
N_DP = 64


def touch_ends(array, stream_key, smallest, high):
    dims = array.shape
    place = [jax.random.randint(jax.random.fold_in(stream_key, axis), (), 0, dims[axis]) for axis in range(len(dims))]
    array = array.at[tuple(place)].set(smallest)
    longest = dims.index(max(dims))
    place[longest] = (place[longest] + 1) % dims[longest]
    return array.at[tuple(place)].set(high)


def block_scale(own_key, dims, cuts, low, top_value):
    loudness = 1.0
    for dim, shards_of in cuts:
        steps = jax.random.uniform(jax.random.fold_in(jax.random.fold_in(own_key, 6), dim), (shards_of,), jnp.float32, low / len(cuts), top_value / len(cuts))
        loudness = loudness * jnp.repeat(jnp.exp(steps), dims[dim] // shards_of).reshape((-1,) + (1,) * (len(dims) - 1 - dim))
    return loudness


def centred(stream_key, dims, deviation, limit, split=(), kind=jnp.bfloat16):
    loudness = block_scale(stream_key, dims, split, -0.22, 0.18) if split else 1.0
    result = jax.random.normal(stream_key, dims, jnp.float32) * deviation * loudness
    return jnp.minimum(jnp.maximum(result, -limit), limit).astype(kind)


def setup_inputs(seed: int = 0) -> dict:
    streams_of = jax.random.split(jax.random.key(seed), 6)
    return {
        "image_emb": centred(streams_of[0], (D, PAIRS), (D ** -0.5), 0.17675781, ((0, 8), (1, 64))),
        "text_emb": centred(streams_of[1], (D, PAIRS), (D ** -0.5), 0.17675781, ((0, 8), (1, 64))),
        "pair_offsets": touch_ends(jax.random.randint(streams_of[2], (CYCLE,), 0, B_DEV), jax.random.fold_in(streams_of[2], 1), 0, B_DEV - 1).astype(jnp.int32),
        "log_scale": jnp.clip(jax.random.uniform(streams_of[3], (1,), jnp.float32, 1.5, 2.5), 1.5, 2.5),
        "bias": jnp.clip(jax.random.uniform(streams_of[4], (1,), jnp.float32, -3.0, -1.0), -3.0, -1.0),
    }


EPSILON = 1e-06

def normalize(embedding):
    values = embedding.astype(jnp.float32)
    inverse = lax.rsqrt(lax.optimization_barrier(jnp.sum(values * values, axis=-1, keepdims=True)) + EPSILON)
    return (values * inverse, inverse)

def reference(image_emb, text_emb, pair_offsets, log_scale, bias):
    img_unit, img_norm = normalize(image_emb.T)
    txt_unit, txt_norm = normalize(text_emb.T)
    img_low = img_unit.astype(jnp.bfloat16).reshape(N_DP, B_DEV, D)
    txt_low = txt_unit.astype(jnp.bfloat16).reshape(N_DP, B_DEV, D)
    temper = jnp.exp(log_scale[0])
    offset_bias = bias[0]
    row_ids = jnp.arange(B_DEV, dtype=jnp.int32)
    row_gap = (row_ids[:, None] - row_ids[None, :]) % B_DEV
    img_wide = img_low.astype(jnp.float32)
    unit_img_grad = jnp.zeros((N_DP, B_DEV, D), jnp.float32)
    unit_txt_grad = jnp.zeros((N_DP, B_DEV, D), jnp.float32)
    for cycle_step in range(CYCLE):
        met_text = jnp.roll(txt_low, cycle_step, axis=0)
        met_wide = met_text.astype(jnp.float32)
        logits = jnp.einsum('gnd,gmd->gnm', img_wide, met_wide)
        margin = temper * logits + offset_bias
        positive = (row_gap == pair_offsets[cycle_step]).astype(jnp.float32)
        slope = (temper * (jax.nn.sigmoid(margin) - positive[None])).astype(jnp.bfloat16)
        slope_wide = slope.astype(jnp.float32)
        unit_img_grad = unit_img_grad + jnp.einsum('gnm,gmd->gnd', slope_wide, met_wide)
        moved_grad = jnp.einsum('gnm,gnd->gmd', slope_wide, img_wide)
        unit_txt_grad = unit_txt_grad + jnp.roll(moved_grad, -cycle_step, axis=0)
    unit_img_grad = unit_img_grad.reshape(N_DP * B_DEV, D)
    unit_txt_grad = unit_txt_grad.reshape(N_DP * B_DEV, D)
    img_dot = lax.optimization_barrier(jnp.sum(img_unit * unit_img_grad, axis=-1, keepdims=True))
    txt_dot = lax.optimization_barrier(jnp.sum(txt_unit * unit_txt_grad, axis=-1, keepdims=True))
    image_grad = img_norm * (unit_img_grad - img_unit * img_dot)
    text_grad = txt_norm * (unit_txt_grad - txt_unit * txt_dot)
    return (image_grad.T, text_grad.T)
```

```python
import functools

import jax
import jax.numpy as jnp
from jax import lax
from jax.experimental import pallas as pl
from jax.experimental.pallas import tpu as pltpu
from jax.sharding import PartitionSpec as P

MESH = pl.DeviceIdType.MESH
F32 = jnp.float32
BF16 = jnp.bfloat16
EPSILON = 1e-06
CYCLE = 12
NW = 8
FEAT = 144
MAIN = 128
TAIL = FEAT - MAIN
D = NW * FEAT
COLS = 256
ROWS = COLS // NW
REACH = 6
ORDER = (0, 2, 5, 1, 3, 4, 6)
PLACE = {d: i for i, d in enumerate(ORDER)}


def rows_of(d):
    return pl.ds(PLACE[d] * ROWS, ROWS)


def kernel(
    chips,
    img_hbm,
    txt_hbm,
    offsets,
    log_scale,
    bias,
    img_out,
    txt_out,
    img_raw,
    txt_in,
    txt_wide,
    a_send,
    a_recv,
    low,
    txt,
    unit,
    tnorm,
    slopes,
    dots,
    own_grad,
    f_send,
    f_recv,
    p_send,
    p_recv,
    p_own,
    e_send,
    e_recv,
    g_send,
    g_recv,
    local_sem,
    a_ss,
    a_rs,
    b_ss,
    b_rs,
    c_ss,
    c_rs,
    f_ss,
    f_rs,
    e_ss,
    e_rs,
    g_ss,
    g_rs,
    s_ss,
    s_rs,
):
    dp = lax.axis_index("dp")
    w = lax.axis_index("width")
    chip = lax.div(dp, 2)
    core = lax.rem(dp, 2)

    def along(d):
        return (lax.rem(chip + d + chips, chips) * 2 + core, w)

    def across(j):
        return (dp, lax.rem(w + j, NW))

    other = (dp + 1 - 2 * core, w)

    def remote(src, dst, ss, rs, to):
        return pltpu.make_async_remote_copy(
            src_ref=src, dst_ref=dst, send_sem=ss, recv_sem=rs, device_id=to, device_id_type=MESH
        )

    barrier = pltpu.get_barrier_semaphore()
    peers = [across(j) for j in range(1, NW)] + [other]
    peers += [along(d) for d in range(-REACH, REACH + 1) if d != 0]
    for peer in peers:
        pl.semaphore_signal(barrier, inc=1, device_id=peer, device_id_type=MESH)

    get_txt = pltpu.make_async_copy(txt_hbm, txt_in, local_sem.at[0])
    get_img = pltpu.make_async_copy(img_hbm, img_raw.at[w], local_sem.at[1])
    get_txt.start()
    get_img.start()

    @pl.when(core == 0)
    def _():
        txt[rows_of(REACH), :] = jnp.zeros((ROWS, D), BF16)

    txt_wide[FEAT:, :] = jnp.zeros((COLS - FEAT, COLS), F32)
    dots[...] = jnp.zeros(dots.shape, F32)
    get_txt.wait()
    txt_wide[:FEAT, :] = txt_in[...].astype(F32)
    a_send[...] = txt_wide[...].T.astype(BF16).reshape(NW, ROWS, COLS)
    get_img.wait()
    pl.semaphore_wait(barrier, len(peers))

    a_copies = []
    for j in range(1, NW):
        copy = remote(a_send.at[lax.rem(w + j, NW)], a_recv.at[w], a_ss.at[j], a_rs.at[j], across(j))
        copy.start()
        a_copies.append(copy)
    b_copies = []
    for j in range(1, NW):
        copy = remote(img_raw.at[w], img_raw.at[w], b_ss.at[j], b_rs.at[j], across(j))
        copy.start()
        b_copies.append(copy)
    a_recv[w] = a_send[w]
    for copy in a_copies:
        copy.wait_recv()

    tail = jnp.zeros((ROWS, MAIN), F32)
    for v in range(NW):
        piece = a_recv[v].astype(F32)
        unit[:, v * MAIN : (v + 1) * MAIN] = piece[:, :MAIN]
        rest = piece[:, MAIN:]
        tail = tail + (pltpu.roll(rest, v * TAIL, 1) if v else rest)
    unit[:, NW * MAIN :] = tail
    raw = unit[...]
    norm = lax.rsqrt(jnp.sum(raw * raw, axis=1, keepdims=True) + EPSILON)
    scaled = raw * norm
    unit[...] = scaled
    tnorm[...] = jnp.broadcast_to(norm, tnorm.shape)
    txt[rows_of(0), :] = scaled.astype(BF16)

    def pass_text(src, dst, to):
        return remote(txt.at[rows_of(src)], txt.at[rows_of(dst)], c_ss.at[dst], c_rs.at[dst], to)

    to2 = pass_text(0, 2, along(2))
    to5 = pass_text(0, 5, along(5))
    to5.start()
    to2.start()

    total = jnp.sum(jnp.square(img_raw[w].astype(F32)), axis=0, keepdims=True)
    for j, copy in enumerate(b_copies, 1):
        copy.wait_recv()
        total = total + jnp.sum(jnp.square(img_raw[lax.rem(w - j + NW, NW)].astype(F32)), axis=0, keepdims=True)
    inorm = lax.rsqrt(total + EPSILON)
    for v in range(NW):
        scaled = (img_raw[v].astype(F32) * inorm).astype(BF16)
        low[core, v * MAIN : (v + 1) * MAIN, :] = scaled[:MAIN]
        low[core, NW * MAIN + v * TAIL : NW * MAIN + (v + 1) * TAIL, :] = scaled[MAIN:]
    share = remote(low.at[core], low.at[core], s_ss.at[0], s_rs.at[0], other)
    share.start()

    temper = jnp.exp(jnp.full((1, COLS), log_scale[0], F32))
    shift = bias[0]
    col = lax.broadcasted_iota(jnp.int32, (ROWS, COLS), 1)
    row = lax.broadcasted_iota(jnp.int32, (ROWS, COLS), 0) + w * ROWS
    gap = col - row

    def back(d):
        return remote(f_send.at[d], f_recv.at[d], f_ss.at[d], f_rs.at[d], along(-d))

    def meet(ds):
        first = PLACE[ds[0]] * ROWS
        size = len(ds) * ROWS
        here = txt[first : first + size, :]
        grad = jnp.zeros((size, D), F32)
        for i in range(2):
            logits = jnp.dot(here, low[i], preferred_element_type=F32)
            parts = []
            dot = jnp.zeros((1, COLS), F32)
            for n, d in enumerate(ds):
                step = 2 * d + i - core
                met = jnp.logical_and(step >= 0, step < CYCLE).astype(F32)
                offset = offsets[jnp.clip(step, 0, CYCLE - 1)]
                own = logits[n * ROWS : (n + 1) * ROWS]
                positive = (((gap - offset) & (COLS - 1)) == 0).astype(F32)
                slope = (temper * (jax.nn.sigmoid(temper * own + shift) - positive)) * met
                slope = slope.astype(BF16)
                dot = dot + jnp.sum(slope.astype(F32) * own, axis=0, keepdims=True)
                slopes[i, (PLACE[d]) * ROWS : (PLACE[d] + 1) * ROWS, :] = slope
                parts.append(slope)
            dots[i] = dots[i] + jnp.broadcast_to(dot, dots.shape[1:])
            grad = grad + lax.dot_general(
                slopes[i, first : first + size, :], low[i], (((1,), (1,)), ((), ())), preferred_element_type=F32
            )
        for n, d in enumerate(ds):
            part = grad[n * ROWS : (n + 1) * ROWS]
            if d == 0:
                own_grad[...] = part
            else:
                f_send[d] = part.astype(BF16)

    share.wait_recv()
    meet((0,))
    to2.wait_recv()
    to1 = pass_text(2, 1, along(-1))
    to3 = pass_text(2, 3, along(1))
    to1.start()
    to3.start()
    to5.wait_recv()
    to4 = pass_text(5, 4, along(-1))
    to6 = pass_text(5, 6, along(1))
    to4.start()

    @pl.when(core == 1)
    def _():
        to6.start()

    meet((2, 5))
    for d in (5, 2):
        back(d).start()
    to1.wait_recv()
    to3.wait_recv()
    to4.wait_recv()

    @pl.when(core == 1)
    def _():
        to6.wait_recv()

    meet((1, 3, 4, 6))
    for d in (4, 3, 1):
        back(d).start()

    @pl.when(core == 1)
    def _():
        back(6).start()

    def image_part(i, store):
        third = D // 3
        dot = dots[i][:1]
        for t in range(3):
            part = lax.dot_general(
                txt[:, t * third : (t + 1) * third], slopes[i], (((0,), (0,)), ((), ())), preferred_element_type=F32
            )
            part = part - low[i, t * third : (t + 1) * third, :].astype(F32) * dot
            for u in range(3):
                v = 3 * t + u
                chunk = part[u * MAIN : (u + 1) * MAIN]
                if v < NW:
                    store(v, 0, MAIN, chunk)
                else:
                    for q in range(NW):
                        store(q, MAIN, FEAT, chunk[q * TAIL : (q + 1) * TAIL])

    def to_other(v, lo, hi, chunk):
        p_send[v, lo:hi, :] = chunk.astype(BF16)

    def to_own(v, lo, hi, chunk):
        p_own[v, lo:hi, :] = chunk

    image_part(1 - core, to_other)
    pair = remote(p_send, p_recv, s_ss.at[1], s_rs.at[1], other)
    pair.start()
    image_part(core, to_own)
    pair.wait_recv()
    for v in range(NW):
        p_own[v] = p_own[v] + p_recv[v].astype(F32)
        e_send[v] = p_own[v].astype(BF16)
    e_copies = []
    for j in range(1, NW):
        copy = remote(e_send.at[lax.rem(w + j, NW)], e_recv.at[j], e_ss.at[j], e_rs.at[j], across(j))
        copy.start()
        e_copies.append(copy)

    grad = own_grad[...]
    for d in (2, 5, 1, 3, 4):
        back(d).wait_recv()
        grad = grad + f_recv[d].astype(F32)
    own_grad[...] = grad

    @pl.when(core == 1)
    def _():
        back(6).wait_recv()
        own_grad[...] = own_grad[...] + f_recv[6].astype(F32)

    grad = own_grad[...]
    scaled = unit[...]
    dot = jnp.sum(scaled * grad, axis=1, keepdims=True)
    final = tnorm[:, :1] * (grad - scaled * dot)
    tail = final[:, NW * MAIN :]
    for v in range(NW):
        g_send[v, :, :MAIN] = final[:, v * MAIN : (v + 1) * MAIN]
        g_send[v, :, MAIN:] = pltpu.roll(tail, MAIN - v * TAIL, 1) if v else tail
    g_copies = []
    for j in range(1, NW):
        copy = remote(g_send.at[lax.rem(w + j, NW)], g_recv.at[w], g_ss.at[j], g_rs.at[j], across(j))
        copy.start()
        g_copies.append(copy)
    g_recv[w] = g_send[w]

    grad = p_own[w]
    for j, copy in enumerate(e_copies, 1):
        copy.wait_recv()
        grad = grad + e_recv[j].astype(F32)
    img_out[...] = grad * inorm
    for copy in g_copies:
        copy.wait_recv()
    txt_out[...] = g_recv[...].reshape(COLS, COLS).T[:FEAT]

    for copy in a_copies + b_copies + e_copies + g_copies:
        copy.wait_send()
    for copy in (to1, to2, to3, to4, to5, share, pair):
        copy.wait_send()
    for d in range(1, REACH):
        back(d).wait_send()

    @pl.when(core == 1)
    def _():
        to6.wait_send()
        back(6).wait_send()


def solution(mesh):
    chips = mesh.shape["dp"] // 2
    slots = len(ORDER)
    dma = pltpu.SemaphoreType.DMA

    def body(image_emb, text_emb, pair_offsets, log_scale, bias):
        shape = jax.ShapeDtypeStruct((FEAT, COLS), F32)
        any_space = pl.BlockSpec(memory_space=pl.ANY)
        smem = pl.BlockSpec(memory_space=pltpu.SMEM)
        vmem = pl.BlockSpec(memory_space=pltpu.VMEM)
        return pl.pallas_call(
            functools.partial(kernel, chips),
            out_shape=(shape, shape),
            in_specs=[any_space, any_space, smem, smem, smem],
            out_specs=(vmem, vmem),
            scratch_shapes=[
                pltpu.VMEM((NW, FEAT, COLS), BF16),
                pltpu.VMEM((FEAT, COLS), BF16),
                pltpu.VMEM((COLS, COLS), F32),
                pltpu.VMEM((NW, ROWS, COLS), BF16),
                pltpu.VMEM((NW, ROWS, COLS), BF16),
                pltpu.VMEM((2, D, COLS), BF16),
                pltpu.VMEM((slots * ROWS, D), BF16),
                pltpu.VMEM((ROWS, D), F32),
                pltpu.VMEM((ROWS, MAIN), F32),
                pltpu.VMEM((2, slots * ROWS, COLS), BF16),
                pltpu.VMEM((2, 8, COLS), F32),
                pltpu.VMEM((ROWS, D), F32),
                pltpu.VMEM((slots, ROWS, D), BF16),
                pltpu.VMEM((slots, ROWS, D), BF16),
                pltpu.VMEM((NW, FEAT, COLS), BF16),
                pltpu.VMEM((NW, FEAT, COLS), BF16),
                pltpu.VMEM((NW, FEAT, COLS), F32),
                pltpu.VMEM((NW, FEAT, COLS), BF16),
                pltpu.VMEM((NW, FEAT, COLS), BF16),
                pltpu.VMEM((NW, ROWS, COLS), F32),
                pltpu.VMEM((NW, ROWS, COLS), F32),
                dma((2,)),
                dma((NW,)),
                dma((NW,)),
                dma((NW,)),
                dma((NW,)),
                dma((slots,)),
                dma((slots,)),
                dma((slots,)),
                dma((slots,)),
                dma((NW,)),
                dma((NW,)),
                dma((NW,)),
                dma((NW,)),
                dma((2,)),
                dma((2,)),
            ],
            compiler_params=pltpu.CompilerParams(
                collective_id=0, has_side_effects=True, vmem_limit_bytes=40 * 1024 * 1024
            ),
        )(image_emb, text_emb, pair_offsets, log_scale, bias)

    placed = (P("width", "dp"), P("width", "dp"), P(), P(), P())
    return jax.shard_map(
        body,
        mesh=mesh,
        in_specs=placed,
        out_specs=(P("width", "dp"), P("width", "dp")),
        check_vma=False,
    )
```

```python
import functools

import jax
import jax.numpy as jnp
from jax import lax
from jax.experimental import pallas as pl
from jax.experimental.pallas import tpu as pltpu
from jax.sharding import PartitionSpec as P

MESH = pl.DeviceIdType.MESH
F32 = jnp.float32
BF16 = jnp.bfloat16
EPSILON = 1e-06
CYCLE = 12
NW = 8
NX = 4
FEAT = 144
MAIN = 128
TAIL = FEAT - MAIN
D = NW * FEAT
COLS = 256
ROWS = COLS // NW
REACH = 6
ORDER = (0, 2, 5, 1, 3, 4, 6)
PLACE = {d: i for i, d in enumerate(ORDER)}


def rows_of(d):
    return pl.ds(PLACE[d] * ROWS, ROWS)


def kernel(
    chips,
    img_hbm,
    txt_hbm,
    offsets,
    log_scale,
    bias,
    img_out,
    txt_out,
    img_raw,
    txt_in,
    txt_wide,
    a_send,
    a_recv,
    low,
    txt,
    unit,
    tnorm,
    slopes,
    dots,
    f_send,
    f_recv,
    p_send,
    p_recv,
    p_own,
    e_send,
    e_recv,
    z_send,
    z_recv,
    keep,
    g_send,
    g_recv,
    local_sem,
    a_ss,
    a_rs,
    b_ss,
    b_rs,
    c_ss,
    c_rs,
    f_ss,
    f_rs,
    e_ss,
    e_rs,
    g_ss,
    g_rs,
    s_ss,
    s_rs,
    z_ss,
    z_rs,
):
    dp = lax.axis_index("dp")
    w = lax.axis_index("width")
    chip = lax.div(dp, 2)
    core = lax.rem(dp, 2)

    def along(d):
        return (lax.rem(chip + d + chips, chips) * 2 + core, w)

    def across(j):
        return (dp, lax.rem(w + j, NW))

    other = (dp + 1 - 2 * core, w)
    x = lax.rem(w, NX)
    base = w - x
    base2 = NX - base
    w2 = base2 + x
    partner = (dp, w2)

    def near(j):
        return lax.rem(x + j, NX)

    def remote(src, dst, ss, rs, to):
        return pltpu.make_async_remote_copy(
            src_ref=src, dst_ref=dst, send_sem=ss, recv_sem=rs, device_id=to, device_id_type=MESH
        )

    barrier = pltpu.get_barrier_semaphore()
    peers = [across(j) for j in range(1, NW)] + [other]
    peers += [along(d) for d in range(-REACH, REACH + 1) if d != 0]
    for peer in peers:
        pl.semaphore_signal(barrier, inc=1, device_id=peer, device_id_type=MESH)

    get_txt = pltpu.make_async_copy(txt_hbm, txt_in, local_sem.at[0])
    get_img = pltpu.make_async_copy(img_hbm, img_raw.at[w], local_sem.at[1])
    get_txt.start()
    get_img.start()

    @pl.when(core == 0)
    def _():
        txt[rows_of(REACH), :] = jnp.zeros((ROWS, D), BF16)

    txt_wide[FEAT:, :] = jnp.zeros((COLS - FEAT, COLS), F32)
    dots[...] = jnp.zeros(dots.shape, F32)
    get_txt.wait()
    txt_wide[:FEAT, :] = txt_in[...].astype(F32)
    a_send[...] = txt_wide[...].T.astype(BF16).reshape(NW, ROWS, COLS)
    get_img.wait()
    pl.semaphore_wait(barrier, len(peers))

    a_copies = []
    for j in range(1, NW):
        copy = remote(a_send.at[lax.rem(w + j, NW)], a_recv.at[w], a_ss.at[j], a_rs.at[j], across(j))
        copy.start()
        a_copies.append(copy)
    a_recv[w] = a_send[w]
    for copy in a_copies:
        copy.wait_recv()
    z_copy = remote(img_raw.at[w], img_raw.at[w], b_ss.at[0], b_rs.at[0], partner)
    z_copy.start()
    b_copies = []
    for j in (1, 3, 2):
        copy = remote(img_raw.at[w], img_raw.at[w], b_ss.at[j], b_rs.at[j], (dp, base + near(j)))
        copy.start()
        b_copies.append(copy)

    tail = jnp.zeros((ROWS, MAIN), F32)
    for v in range(NW):
        piece = a_recv[v].astype(F32)
        unit[:, v * MAIN : (v + 1) * MAIN] = piece[:, :MAIN]
        rest = piece[:, MAIN:]
        tail = tail + (pltpu.roll(rest, v * TAIL, 1) if v else rest)
    unit[:, NW * MAIN :] = tail
    raw = unit[...]
    norm = lax.rsqrt(jnp.sum(raw * raw, axis=1, keepdims=True) + EPSILON)
    scaled = raw * norm
    unit[...] = scaled
    tnorm[...] = jnp.broadcast_to(norm, tnorm.shape)
    txt[rows_of(0), :] = scaled.astype(BF16)

    def pass_text(src, dst, to):
        return remote(txt.at[rows_of(src)], txt.at[rows_of(dst)], c_ss.at[dst], c_rs.at[dst], to)

    to2 = pass_text(0, 2, along(2))
    to5 = pass_text(0, 5, along(5))
    to5.start()
    to2.start()

    z_copy.wait_recv()
    for j in (1, 3, 2):
        copy = remote(img_raw.at[w2], img_raw.at[w2], b_ss.at[NX + j], b_rs.at[NX + j], (dp, base + near(j)))
        copy.start()
        b_copies.append(copy)

    def squares(v):
        return jnp.sum(jnp.square(img_raw[v].astype(F32)), axis=0, keepdims=True)

    total = squares(w) + squares(w2)
    for n, copy in enumerate(b_copies):
        copy.wait_recv()
        j = (1, 3, 2)[n % 3]
        total = total + squares((base if n < 3 else base2) + near(NX - j))
    inorm = lax.rsqrt(total + EPSILON)
    for v in range(NW):
        scaled = (img_raw[v].astype(F32) * inorm).astype(BF16)
        low[core, v * MAIN : (v + 1) * MAIN, :] = scaled[:MAIN]
        low[core, NW * MAIN + v * TAIL : NW * MAIN + (v + 1) * TAIL, :] = scaled[MAIN:]
    share = remote(low.at[core], low.at[core], s_ss.at[0], s_rs.at[0], other)
    share.start()

    temper = jnp.exp(jnp.full((1, COLS), log_scale[0], F32))
    shift = bias[0]
    col = lax.broadcasted_iota(jnp.int32, (ROWS, COLS), 1)
    row = lax.broadcasted_iota(jnp.int32, (ROWS, COLS), 0) + w * ROWS
    gap = col - row

    home = {1: 1, 3: -1, 4: 1, 6: -1, 2: -2, 5: -5}

    def back(d):
        return remote(f_send.at[d], f_recv.at[d], f_ss.at[d], f_rs.at[d], along(home[d]))

    def meet(ds):
        first = PLACE[ds[0]] * ROWS
        size = len(ds) * ROWS
        here = txt[first : first + size, :]
        grad = jnp.zeros((size, D), F32)
        for i in range(2):
            logits = jnp.dot(here, low[i], preferred_element_type=F32)
            parts = []
            dot = jnp.zeros((1, COLS), F32)
            for n, d in enumerate(ds):
                step = 2 * d + i - core
                met = jnp.logical_and(step >= 0, step < CYCLE).astype(F32)
                offset = offsets[jnp.clip(step, 0, CYCLE - 1)]
                own = logits[n * ROWS : (n + 1) * ROWS]
                positive = (((gap - offset) & (COLS - 1)) == 0).astype(F32)
                slope = (temper * (jax.nn.sigmoid(temper * own + shift) - positive)) * met
                slope = slope.astype(BF16)
                dot = dot + jnp.sum(slope.astype(F32) * own, axis=0, keepdims=True)
                slopes[i, (PLACE[d]) * ROWS : (PLACE[d] + 1) * ROWS, :] = slope
                parts.append(slope)
            dots[i] = dots[i] + jnp.broadcast_to(dot, dots.shape[1:])
            grad = grad + lax.dot_general(
                slopes[i, first : first + size, :], low[i], (((1,), (1,)), ((), ())), preferred_element_type=F32
            )
        for n, d in enumerate(ds):
            part = grad[n * ROWS : (n + 1) * ROWS]
            if d in (0, 2, 5):
                keep[PLACE[d]] = part
            else:
                f_send[d] = part.astype(BF16)

    to2.wait_recv()
    to1 = pass_text(2, 1, along(-1))
    to3 = pass_text(2, 3, along(1))
    to1.start()
    to3.start()
    to5.wait_recv()
    to4 = pass_text(5, 4, along(-1))
    to6 = pass_text(5, 6, along(1))
    to4.start()

    @pl.when(core == 1)
    def _():
        to6.start()

    share.wait_recv()
    meet((0, 2, 5))
    to1.wait_recv()
    to3.wait_recv()
    to4.wait_recv()

    @pl.when(core == 1)
    def _():
        to6.wait_recv()

    meet((1, 3, 4, 6))
    for d in (4, 3, 1):
        back(d).start()

    @pl.when(core == 1)
    def _():
        back(6).start()

    def image_part(i, store):
        third = D // 3
        dot = dots[i][:1]
        for t in range(3):
            part = lax.dot_general(
                txt[:, t * third : (t + 1) * third], slopes[i], (((0,), (0,)), ((), ())), preferred_element_type=F32
            )
            part = part - low[i, t * third : (t + 1) * third, :].astype(F32) * dot
            for u in range(3):
                v = 3 * t + u
                chunk = part[u * MAIN : (u + 1) * MAIN]
                if v < NW:
                    store(v, 0, MAIN, chunk)
                else:
                    for q in range(NW):
                        store(q, MAIN, FEAT, chunk[q * TAIL : (q + 1) * TAIL])

    def to_other(v, lo, hi, chunk):
        p_send[v, lo:hi, :] = chunk.astype(BF16)

    def to_own(v, lo, hi, chunk):
        p_own[v, lo:hi, :] = chunk

    image_part(1 - core, to_other)
    pair = remote(p_send, p_recv, s_ss.at[1], s_rs.at[1], other)
    pair.start()
    image_part(core, to_own)
    pair.wait_recv()
    for v in range(NW):
        p_own[v] = p_own[v] + p_recv[v].astype(F32)
        e_send[v] = p_own[v].astype(BF16)
    e_copies = []
    for start in (base2, base):
        for j in (1, 3, 2):
            n = len(e_copies)
            copy = remote(
                e_send.at[start + near(j)], e_recv.at[n], e_ss.at[n], e_rs.at[n], (dp, base + near(j))
            )
            copy.start()
            e_copies.append(copy)

    back(4).wait_recv()
    keep[PLACE[5]] = keep[PLACE[5]] + f_recv[4].astype(F32)

    @pl.when(core == 1)
    def _():
        back(6).wait_recv()
        keep[PLACE[5]] = keep[PLACE[5]] + f_recv[6].astype(F32)

    f_send[5] = keep[PLACE[5]].astype(BF16)
    back(5).start()
    back(1).wait_recv()
    back(3).wait_recv()
    f_send[2] = (keep[PLACE[2]] + f_recv[1].astype(F32) + f_recv[3].astype(F32)).astype(BF16)
    back(2).start()

    grad = p_own[w2]
    for n in range(3):
        e_copies[n].wait_recv()
        grad = grad + e_recv[n].astype(F32)
    z_send[...] = grad.astype(BF16)
    z_back = remote(z_send, z_recv, z_ss.at[0], z_rs.at[0], partner)
    z_back.start()

    back(2).wait_recv()
    grad = keep[PLACE[0]] + f_recv[2].astype(F32)
    back(5).wait_recv()
    grad = grad + f_recv[5].astype(F32)
    scaled = unit[...]
    dot = jnp.sum(scaled * grad, axis=1, keepdims=True)
    final = tnorm[:, :1] * (grad - scaled * dot)
    tail = final[:, NW * MAIN :]
    for v in range(NW):
        g_send[v, :, :MAIN] = final[:, v * MAIN : (v + 1) * MAIN]
        g_send[v, :, MAIN:] = pltpu.roll(tail, MAIN - v * TAIL, 1) if v else tail
    g_copies = []
    for j in range(1, NW):
        copy = remote(g_send.at[lax.rem(w + j, NW)], g_recv.at[w], g_ss.at[j], g_rs.at[j], across(j))
        copy.start()
        g_copies.append(copy)
    g_recv[w] = g_send[w]

    grad = p_own[w]
    for n in range(3, 6):
        e_copies[n].wait_recv()
        grad = grad + e_recv[n].astype(F32)
    z_back.wait_recv()
    grad = grad + z_recv[...].astype(F32)
    img_out[...] = grad * inorm
    for copy in g_copies:
        copy.wait_recv()
    txt_out[...] = g_recv[...].reshape(COLS, COLS).T[:FEAT]

    for copy in a_copies + b_copies + e_copies + g_copies:
        copy.wait_send()
    for copy in (to1, to2, to3, to4, to5, share, pair, z_copy, z_back):
        copy.wait_send()
    for d in range(1, REACH):
        back(d).wait_send()

    @pl.when(core == 1)
    def _():
        to6.wait_send()
        back(6).wait_send()


def solution(mesh):
    chips = mesh.shape["dp"] // 2
    slots = len(ORDER)
    dma = pltpu.SemaphoreType.DMA

    def body(image_emb, text_emb, pair_offsets, log_scale, bias):
        shape = jax.ShapeDtypeStruct((FEAT, COLS), F32)
        any_space = pl.BlockSpec(memory_space=pl.ANY)
        smem = pl.BlockSpec(memory_space=pltpu.SMEM)
        vmem = pl.BlockSpec(memory_space=pltpu.VMEM)
        return pl.pallas_call(
            functools.partial(kernel, chips),
            out_shape=(shape, shape),
            in_specs=[any_space, any_space, smem, smem, smem],
            out_specs=(vmem, vmem),
            scratch_shapes=[
                pltpu.VMEM((NW, FEAT, COLS), BF16),
                pltpu.VMEM((FEAT, COLS), BF16),
                pltpu.VMEM((COLS, COLS), F32),
                pltpu.VMEM((NW, ROWS, COLS), BF16),
                pltpu.VMEM((NW, ROWS, COLS), BF16),
                pltpu.VMEM((2, D, COLS), BF16),
                pltpu.VMEM((slots * ROWS, D), BF16),
                pltpu.VMEM((ROWS, D), F32),
                pltpu.VMEM((ROWS, MAIN), F32),
                pltpu.VMEM((2, slots * ROWS, COLS), BF16),
                pltpu.VMEM((2, 8, COLS), F32),
                pltpu.VMEM((slots, ROWS, D), BF16),
                pltpu.VMEM((slots, ROWS, D), BF16),
                pltpu.VMEM((NW, FEAT, COLS), BF16),
                pltpu.VMEM((NW, FEAT, COLS), BF16),
                pltpu.VMEM((NW, FEAT, COLS), F32),
                pltpu.VMEM((NW, FEAT, COLS), BF16),
                pltpu.VMEM((6, FEAT, COLS), BF16),
                pltpu.VMEM((FEAT, COLS), BF16),
                pltpu.VMEM((FEAT, COLS), BF16),
                pltpu.VMEM((3, ROWS, D), F32),
                pltpu.VMEM((NW, ROWS, COLS), F32),
                pltpu.VMEM((NW, ROWS, COLS), F32),
                dma((2,)),
                dma((NW,)),
                dma((NW,)),
                dma((NW,)),
                dma((NW,)),
                dma((slots,)),
                dma((slots,)),
                dma((slots,)),
                dma((slots,)),
                dma((NW,)),
                dma((NW,)),
                dma((NW,)),
                dma((NW,)),
                dma((2,)),
                dma((2,)),
                dma((1,)),
                dma((1,)),
            ],
            compiler_params=pltpu.CompilerParams(
                collective_id=0, has_side_effects=True, vmem_limit_bytes=60 * 1024 * 1024
            ),
        )(image_emb, text_emb, pair_offsets, log_scale, bias)

    placed = (P("width", "dp"), P("width", "dp"), P(), P(), P())
    return jax.shard_map(
        body,
        mesh=mesh,
        in_specs=placed,
        out_specs=(P("width", "dp"), P("width", "dp")),
        check_vma=False,
    )
```

```python
import functools

import jax
import jax.numpy as jnp
from jax import lax
from jax.experimental import pallas as pl
from jax.experimental.pallas import tpu as pltpu
from jax.sharding import PartitionSpec as P

MESH = pl.DeviceIdType.MESH
F32 = jnp.float32
BF16 = jnp.bfloat16
EPSILON = 1e-06
CYCLE = 12
NW = 8
NX = 4
FEAT = 144
MAIN = 128
TAIL = FEAT - MAIN
D = NW * FEAT
COLS = 256
ROWS = COLS // NW
REACH = 6
ORDER = (0, 2, 5, 1, 3, 4, 6)
PLACE = {d: i for i, d in enumerate(ORDER)}


def rows_of(d):
    return pl.ds(PLACE[d] * ROWS, ROWS)


def kernel(
    chips,
    img_hbm,
    txt_hbm,
    offsets,
    log_scale,
    bias,
    img_out,
    txt_out,
    img_raw,
    txt_in,
    txt_wide,
    a_send,
    a_recv,
    low,
    txt,
    unit,
    tnorm,
    slopes,
    dots,
    f_send,
    f_recv,
    p_send,
    p_recv,
    p_own,
    e_send,
    e_recv,
    z_send,
    z_recv,
    keep,
    g_send,
    g_recv,
    local_sem,
    a_ss,
    a_rs,
    b_ss,
    b_rs,
    c_ss,
    c_rs,
    f_ss,
    f_rs,
    e_ss,
    e_rs,
    g_ss,
    g_rs,
    s_ss,
    s_rs,
    z_ss,
    z_rs,
):
    dp = lax.axis_index("dp")
    w = lax.axis_index("width")
    chip = lax.div(dp, 2)
    core = lax.rem(dp, 2)

    def along(d):
        return (lax.rem(chip + d + chips, chips) * 2 + core, w)

    def across(j):
        return (dp, lax.rem(w + j, NW))

    other = (dp + 1 - 2 * core, w)
    x = lax.rem(w, NX)
    base = w - x
    base2 = NX - base
    w2 = base2 + x
    partner = (dp, w2)

    def near(j):
        return lax.rem(x + j, NX)

    def remote(src, dst, ss, rs, to):
        return pltpu.make_async_remote_copy(
            src_ref=src, dst_ref=dst, send_sem=ss, recv_sem=rs, device_id=to, device_id_type=MESH
        )

    barrier = pltpu.get_barrier_semaphore()
    peers = [across(j) for j in range(1, NW)] + [other]
    peers += [along(d) for d in range(-REACH, REACH + 1) if d != 0]
    for peer in peers:
        pl.semaphore_signal(barrier, inc=1, device_id=peer, device_id_type=MESH)

    get_txt = pltpu.make_async_copy(txt_hbm, txt_in, local_sem.at[0])
    get_img = pltpu.make_async_copy(img_hbm, img_raw.at[w], local_sem.at[1])
    get_txt.start()
    get_img.start()

    @pl.when(core == 0)
    def _():
        txt[rows_of(REACH), :] = jnp.zeros((ROWS, D), BF16)

    txt_wide[FEAT:, :] = jnp.zeros((COLS - FEAT, COLS), F32)
    dots[...] = jnp.zeros(dots.shape, F32)
    get_txt.wait()
    txt_wide[:FEAT, :] = txt_in[...].astype(F32)
    a_send[...] = txt_wide[...].T.astype(BF16).reshape(NW, ROWS, COLS)
    get_img.wait()
    pl.semaphore_wait(barrier, len(peers))

    z_copy = remote(img_raw.at[w], img_raw.at[w], b_ss.at[0], b_rs.at[0], partner)
    z_copy.start()
    a_copies = []
    for j in range(1, NW):
        copy = remote(a_send.at[lax.rem(w + j, NW)], a_recv.at[w], a_ss.at[j], a_rs.at[j], across(j))
        copy.start()
        a_copies.append(copy)
    a_recv[w] = a_send[w]
    for copy in a_copies:
        copy.wait_recv()
    b_copies = []
    for j in (1, 3, 2):
        copy = remote(img_raw.at[w], img_raw.at[w], b_ss.at[j], b_rs.at[j], (dp, base + near(j)))
        copy.start()
        b_copies.append(copy)

    tail = jnp.zeros((ROWS, MAIN), F32)
    for v in range(NW):
        piece = a_recv[v].astype(F32)
        unit[:, v * MAIN : (v + 1) * MAIN] = piece[:, :MAIN]
        rest = piece[:, MAIN:]
        tail = tail + (pltpu.roll(rest, v * TAIL, 1) if v else rest)
    unit[:, NW * MAIN :] = tail
    raw = unit[...]
    norm = lax.rsqrt(jnp.sum(raw * raw, axis=1, keepdims=True) + EPSILON)
    scaled = raw * norm
    unit[...] = scaled
    tnorm[...] = jnp.broadcast_to(norm, tnorm.shape)
    txt[rows_of(0), :] = scaled.astype(BF16)

    def pass_text(src, dst, to):
        return remote(txt.at[rows_of(src)], txt.at[rows_of(dst)], c_ss.at[dst], c_rs.at[dst], to)

    to2 = pass_text(0, 2, along(2))
    to5 = pass_text(0, 5, along(5))
    to5.start()
    to2.start()

    z_copy.wait_recv()
    for j in (1, 3, 2):
        copy = remote(img_raw.at[w2], img_raw.at[w2], b_ss.at[NX + j], b_rs.at[NX + j], (dp, base + near(j)))
        copy.start()
        b_copies.append(copy)

    to2.wait_recv()
    to1 = pass_text(2, 1, along(-1))
    to3 = pass_text(2, 3, along(1))
    to1.start()
    to3.start()
    to5.wait_recv()
    to4 = pass_text(5, 4, along(-1))
    to6 = pass_text(5, 6, along(1))
    to4.start()

    @pl.when(core == 1)
    def _():
        to6.start()

    def squares(v):
        return jnp.sum(jnp.square(img_raw[v].astype(F32)), axis=0, keepdims=True)

    total = squares(w) + squares(w2)
    for n, copy in enumerate(b_copies):
        copy.wait_recv()
        j = (1, 3, 2)[n % 3]
        total = total + squares((base if n < 3 else base2) + near(NX - j))
    inorm = lax.rsqrt(total + EPSILON)
    for v in range(NW):
        scaled = (img_raw[v].astype(F32) * inorm).astype(BF16)
        low[core, v * MAIN : (v + 1) * MAIN, :] = scaled[:MAIN]
        low[core, NW * MAIN + v * TAIL : NW * MAIN + (v + 1) * TAIL, :] = scaled[MAIN:]
    share = remote(low.at[core], low.at[core], s_ss.at[0], s_rs.at[0], other)
    share.start()

    temper = jnp.exp(jnp.full((1, COLS), log_scale[0], F32))
    shift = bias[0]
    col = lax.broadcasted_iota(jnp.int32, (ROWS, COLS), 1)
    row = lax.broadcasted_iota(jnp.int32, (ROWS, COLS), 0) + w * ROWS
    gap = col - row

    home = {1: 1, 3: -1, 4: 1, 6: -1, 2: -2, 5: -5}

    def back(d):
        return remote(f_send.at[d], f_recv.at[d], f_ss.at[d], f_rs.at[d], along(home[d]))

    def meet(ds):
        first = PLACE[ds[0]] * ROWS
        size = len(ds) * ROWS
        here = txt[first : first + size, :]
        grad = jnp.zeros((size, D), F32)
        for i in range(2):
            logits = jnp.dot(here, low[i], preferred_element_type=F32)
            parts = []
            dot = jnp.zeros((1, COLS), F32)
            for n, d in enumerate(ds):
                step = 2 * d + i - core
                met = jnp.logical_and(step >= 0, step < CYCLE).astype(F32)
                offset = offsets[jnp.clip(step, 0, CYCLE - 1)]
                own = logits[n * ROWS : (n + 1) * ROWS]
                positive = (((gap - offset) & (COLS - 1)) == 0).astype(F32)
                slope = (temper * (jax.nn.sigmoid(temper * own + shift) - positive)) * met
                slope = slope.astype(BF16)
                dot = dot + jnp.sum(slope.astype(F32) * own, axis=0, keepdims=True)
                slopes[i, (PLACE[d]) * ROWS : (PLACE[d] + 1) * ROWS, :] = slope
                parts.append(slope)
            dots[i] = dots[i] + jnp.broadcast_to(dot, dots.shape[1:])
            grad = grad + lax.dot_general(
                slopes[i, first : first + size, :], low[i], (((1,), (1,)), ((), ())), preferred_element_type=F32
            )
        for n, d in enumerate(ds):
            part = grad[n * ROWS : (n + 1) * ROWS]
            if d in (0, 2, 5):
                keep[PLACE[d]] = part
            else:
                f_send[d] = part.astype(BF16)

    share.wait_recv()
    meet((0, 2, 5))
    to1.wait_recv()
    to3.wait_recv()
    to4.wait_recv()

    @pl.when(core == 1)
    def _():
        to6.wait_recv()

    meet((1, 3, 4, 6))
    for d in (4, 3, 1):
        back(d).start()

    @pl.when(core == 1)
    def _():
        back(6).start()

    def image_part(i, store):
        third = D // 3
        dot = dots[i][:1]
        for t in range(3):
            part = lax.dot_general(
                txt[:, t * third : (t + 1) * third], slopes[i], (((0,), (0,)), ((), ())), preferred_element_type=F32
            )
            part = part - low[i, t * third : (t + 1) * third, :].astype(F32) * dot
            for u in range(3):
                v = 3 * t + u
                chunk = part[u * MAIN : (u + 1) * MAIN]
                if v < NW:
                    store(v, 0, MAIN, chunk)
                else:
                    for q in range(NW):
                        store(q, MAIN, FEAT, chunk[q * TAIL : (q + 1) * TAIL])

    def to_other(v, lo, hi, chunk):
        p_send[v, lo:hi, :] = chunk.astype(BF16)

    def to_own(v, lo, hi, chunk):
        p_own[v, lo:hi, :] = chunk

    image_part(1 - core, to_other)
    pair = remote(p_send, p_recv, s_ss.at[1], s_rs.at[1], other)
    pair.start()
    image_part(core, to_own)
    pair.wait_recv()
    for v in range(NW):
        p_own[v] = p_own[v] + p_recv[v].astype(F32)
        e_send[v] = p_own[v].astype(BF16)
    e_copies = []
    for start in (base2, base):
        for j in (1, 3, 2):
            n = len(e_copies)
            copy = remote(
                e_send.at[start + near(j)], e_recv.at[n], e_ss.at[n], e_rs.at[n], (dp, base + near(j))
            )
            copy.start()
            e_copies.append(copy)

    back(4).wait_recv()
    keep[PLACE[5]] = keep[PLACE[5]] + f_recv[4].astype(F32)

    @pl.when(core == 1)
    def _():
        back(6).wait_recv()
        keep[PLACE[5]] = keep[PLACE[5]] + f_recv[6].astype(F32)

    f_send[5] = keep[PLACE[5]].astype(BF16)
    back(5).start()
    back(1).wait_recv()
    back(3).wait_recv()
    f_send[2] = (keep[PLACE[2]] + f_recv[1].astype(F32) + f_recv[3].astype(F32)).astype(BF16)
    back(2).start()

    grad = p_own[w2]
    for n in range(3):
        e_copies[n].wait_recv()
        grad = grad + e_recv[n].astype(F32)
    z_send[...] = grad.astype(BF16)
    z_back = remote(z_send, z_recv, z_ss.at[0], z_rs.at[0], partner)
    z_back.start()

    back(2).wait_recv()
    grad = keep[PLACE[0]] + f_recv[2].astype(F32)
    back(5).wait_recv()
    grad = grad + f_recv[5].astype(F32)
    scaled = unit[...]
    dot = jnp.sum(scaled * grad, axis=1, keepdims=True)
    final = tnorm[:, :1] * (grad - scaled * dot)
    tail = final[:, NW * MAIN :]
    for v in range(NW):
        g_send[v, :, :MAIN] = final[:, v * MAIN : (v + 1) * MAIN]
        g_send[v, :, MAIN:] = pltpu.roll(tail, MAIN - v * TAIL, 1) if v else tail
    g_copies = []
    for j in range(1, NW):
        copy = remote(g_send.at[lax.rem(w + j, NW)], g_recv.at[w], g_ss.at[j], g_rs.at[j], across(j))
        copy.start()
        g_copies.append(copy)
    g_recv[w] = g_send[w]

    grad = p_own[w]
    for n in range(3, 6):
        e_copies[n].wait_recv()
        grad = grad + e_recv[n].astype(F32)
    z_back.wait_recv()
    grad = grad + z_recv[...].astype(F32)
    img_out[...] = grad * inorm
    for copy in g_copies:
        copy.wait_recv()
    txt_out[...] = g_recv[...].reshape(COLS, COLS).T[:FEAT]

    for copy in a_copies + b_copies + e_copies + g_copies:
        copy.wait_send()
    for copy in (to1, to2, to3, to4, to5, share, pair, z_copy, z_back):
        copy.wait_send()
    for d in range(1, REACH):
        back(d).wait_send()

    @pl.when(core == 1)
    def _():
        to6.wait_send()
        back(6).wait_send()


def solution(mesh):
    chips = mesh.shape["dp"] // 2
    slots = len(ORDER)
    dma = pltpu.SemaphoreType.DMA

    def body(image_emb, text_emb, pair_offsets, log_scale, bias):
        shape = jax.ShapeDtypeStruct((FEAT, COLS), F32)
        any_space = pl.BlockSpec(memory_space=pl.ANY)
        smem = pl.BlockSpec(memory_space=pltpu.SMEM)
        vmem = pl.BlockSpec(memory_space=pltpu.VMEM)
        return pl.pallas_call(
            functools.partial(kernel, chips),
            out_shape=(shape, shape),
            in_specs=[any_space, any_space, smem, smem, smem],
            out_specs=(vmem, vmem),
            scratch_shapes=[
                pltpu.VMEM((NW, FEAT, COLS), BF16),
                pltpu.VMEM((FEAT, COLS), BF16),
                pltpu.VMEM((COLS, COLS), F32),
                pltpu.VMEM((NW, ROWS, COLS), BF16),
                pltpu.VMEM((NW, ROWS, COLS), BF16),
                pltpu.VMEM((2, D, COLS), BF16),
                pltpu.VMEM((slots * ROWS, D), BF16),
                pltpu.VMEM((ROWS, D), F32),
                pltpu.VMEM((ROWS, MAIN), F32),
                pltpu.VMEM((2, slots * ROWS, COLS), BF16),
                pltpu.VMEM((2, 8, COLS), F32),
                pltpu.VMEM((slots, ROWS, D), BF16),
                pltpu.VMEM((slots, ROWS, D), BF16),
                pltpu.VMEM((NW, FEAT, COLS), BF16),
                pltpu.VMEM((NW, FEAT, COLS), BF16),
                pltpu.VMEM((NW, FEAT, COLS), F32),
                pltpu.VMEM((NW, FEAT, COLS), BF16),
                pltpu.VMEM((6, FEAT, COLS), BF16),
                pltpu.VMEM((FEAT, COLS), BF16),
                pltpu.VMEM((FEAT, COLS), BF16),
                pltpu.VMEM((3, ROWS, D), F32),
                pltpu.VMEM((NW, ROWS, COLS), F32),
                pltpu.VMEM((NW, ROWS, COLS), F32),
                dma((2,)),
                dma((NW,)),
                dma((NW,)),
                dma((NW,)),
                dma((NW,)),
                dma((slots,)),
                dma((slots,)),
                dma((slots,)),
                dma((slots,)),
                dma((NW,)),
                dma((NW,)),
                dma((NW,)),
                dma((NW,)),
                dma((2,)),
                dma((2,)),
                dma((1,)),
                dma((1,)),
            ],
            compiler_params=pltpu.CompilerParams(
                collective_id=0, has_side_effects=True, vmem_limit_bytes=60 * 1024 * 1024
            ),
        )(image_emb, text_emb, pair_offsets, log_scale, bias)

    placed = (P("width", "dp"), P("width", "dp"), P(), P(), P())
    return jax.shard_map(
        body,
        mesh=mesh,
        in_specs=placed,
        out_specs=(P("width", "dp"), P("width", "dp")),
        check_vma=False,
    )
```

```python
import functools

import jax
import jax.numpy as jnp
from jax import lax
from jax.experimental import pallas as pl
from jax.experimental.pallas import tpu as pltpu
from jax.sharding import PartitionSpec as P

MESH = pl.DeviceIdType.MESH
F32 = jnp.float32
BF16 = jnp.bfloat16
EPSILON = 1e-06
CYCLE = 12
NW = 8
NX = 4
FEAT = 144
MAIN = 128
TAIL = FEAT - MAIN
D = NW * FEAT
COLS = 256
ROWS = COLS // NW
REACH = 6
ORDER = (0, 2, 5, 1, 3, 4, 6)
PLACE = {d: i for i, d in enumerate(ORDER)}


def rows_of(d):
    return pl.ds(PLACE[d] * ROWS, ROWS)


def kernel(
    chips,
    img_hbm,
    txt_hbm,
    offsets_hbm,
    scale_hbm,
    bias_hbm,
    out_hbm,
    offsets,
    log_scale,
    bias,
    img_raw,
    txt_in,
    txt_wide,
    a_send,
    a_recv,
    low,
    txt,
    unit,
    tnorm,
    slopes,
    dots,
    f_send,
    f_recv,
    p_send,
    p_recv,
    p_own,
    e_send,
    e_recv,
    z_send,
    z_recv,
    keep,
    g_send,
    g_recv,
    h_send,
    h_recv,
    out,
    local_sem,
    a_ss,
    a_rs,
    b_ss,
    b_rs,
    c_ss,
    c_rs,
    f_ss,
    f_rs,
    e_ss,
    e_rs,
    g_ss,
    g_rs,
    s_ss,
    s_rs,
    z_ss,
    z_rs,
    h_ss,
    h_rs,
):
    dp = lax.axis_index("dp")
    w = lax.axis_index("width")
    chip = lax.div(dp, 2)
    core = lax.rem(dp, 2)

    def along(d):
        return (lax.rem(chip + d + chips, chips) * 2 + core, w)

    def across(j):
        return (dp, lax.rem(w + j, NW))

    other = (dp + 1 - 2 * core, w)
    x = lax.rem(w, NX)
    base = w - x
    base2 = NX - base
    w2 = base2 + x
    partner = (dp, w2)

    def near(j):
        return lax.rem(x + j, NX)

    def remote(src, dst, ss, rs, to):
        return pltpu.make_async_remote_copy(
            src_ref=src, dst_ref=dst, send_sem=ss, recv_sem=rs, device_id=to, device_id_type=MESH
        )

    barrier = pltpu.get_barrier_semaphore()
    peers = [along(d) for d in (5, -5, 2, -2, 1, -1)] + [across(j) for j in range(1, NW)] + [other]
    for peer in peers:
        pl.semaphore_signal(barrier, inc=1, device_id=peer, device_id_type=MESH)

    get_txt = pltpu.make_async_copy(txt_hbm, txt_in, local_sem.at[0])
    get_img = pltpu.make_async_copy(img_hbm, img_raw.at[w], local_sem.at[1])
    get_txt.start()
    get_img.start()
    scalars = [
        pltpu.make_async_copy(src, dst, local_sem.at[2 + n])
        for n, (src, dst) in enumerate(((offsets_hbm, offsets), (scale_hbm, log_scale), (bias_hbm, bias)))
    ]
    for copy in scalars:
        copy.start()

    @pl.when(core == 0)
    def _():
        txt[rows_of(REACH), :] = jnp.zeros((ROWS, D), BF16)

    txt_wide[FEAT:, :] = jnp.zeros((COLS - FEAT, COLS), F32)
    dots[...] = jnp.zeros(dots.shape, F32)
    get_txt.wait()
    txt_wide[:FEAT, :] = txt_in[...].astype(F32)
    a_send[...] = txt_wide[...].T.astype(BF16).reshape(NW, ROWS, COLS)
    get_img.wait()
    for copy in scalars:
        copy.wait()
    pl.semaphore_wait(barrier, len(peers))

    z_copy = remote(img_raw.at[w], img_raw.at[w], b_ss.at[0], b_rs.at[0], partner)
    z_copy.start()
    a_copies = []
    for j in range(1, NW):
        copy = remote(a_send.at[lax.rem(w + j, NW)], a_recv.at[w], a_ss.at[j], a_rs.at[j], across(j))
        copy.start()
        a_copies.append(copy)
    a_recv[w] = a_send[w]
    for copy in a_copies:
        copy.wait_recv()
    b_copies = []
    for j in (1, 3, 2):
        copy = remote(img_raw.at[w], img_raw.at[w], b_ss.at[j], b_rs.at[j], (dp, base + near(j)))
        copy.start()
        b_copies.append(copy)

    tail = jnp.zeros((ROWS, MAIN), F32)
    for v in range(NW):
        piece = a_recv[v].astype(F32)
        unit[:, v * MAIN : (v + 1) * MAIN] = piece[:, :MAIN]
        rest = piece[:, MAIN:]
        tail = tail + (pltpu.roll(rest, v * TAIL, 1) if v else rest)
    unit[:, NW * MAIN :] = tail
    raw = unit[...]
    norm = lax.rsqrt(jnp.sum(raw * raw, axis=1, keepdims=True) + EPSILON)
    scaled = raw * norm
    unit[...] = scaled
    tnorm[...] = jnp.broadcast_to(norm, tnorm.shape)
    txt[rows_of(0), :] = scaled.astype(BF16)

    def pass_text(src, dst, to):
        return remote(txt.at[rows_of(src)], txt.at[rows_of(dst)], c_ss.at[dst], c_rs.at[dst], to)

    to2 = pass_text(0, 2, along(2))
    to5 = pass_text(0, 5, along(5))
    to5.start()
    to2.start()

    z_copy.wait_recv()
    for j in (1, 3, 2):
        copy = remote(img_raw.at[w2], img_raw.at[w2], b_ss.at[NX + j], b_rs.at[NX + j], (dp, base + near(j)))
        copy.start()
        b_copies.append(copy)

    to2.wait_recv()
    to1 = pass_text(2, 1, along(-1))
    to3 = pass_text(2, 3, along(1))
    to1.start()
    to3.start()
    to5.wait_recv()
    to4 = pass_text(5, 4, along(-1))
    to6 = pass_text(5, 6, along(1))
    to4.start()

    @pl.when(core == 1)
    def _():
        to6.start()

    def squares(v):
        return jnp.sum(jnp.square(img_raw[v].astype(F32)), axis=0, keepdims=True)

    total = squares(w) + squares(w2)
    for n, copy in enumerate(b_copies):
        copy.wait_recv()
        j = (1, 3, 2)[n % 3]
        total = total + squares((base if n < 3 else base2) + near(NX - j))
    inorm = lax.rsqrt(total + EPSILON)
    for v in range(NW):
        scaled = (img_raw[v].astype(F32) * inorm).astype(BF16)
        low[core, v * MAIN : (v + 1) * MAIN, :] = scaled[:MAIN]
        low[core, NW * MAIN + v * TAIL : NW * MAIN + (v + 1) * TAIL, :] = scaled[MAIN:]
    share = remote(low.at[core], low.at[core], s_ss.at[0], s_rs.at[0], other)
    share.start()

    temper = jnp.exp(jnp.full((1, COLS), log_scale[0], F32))
    shift = bias[0]
    col = lax.broadcasted_iota(jnp.int32, (ROWS, COLS), 1)
    row = lax.broadcasted_iota(jnp.int32, (ROWS, COLS), 0) + w * ROWS
    gap = col - row

    home = {1: 1, 3: -1, 4: 1, 6: -1}

    def back(d):
        return remote(f_send.at[d], f_recv.at[d], f_ss.at[d], f_rs.at[d], along(home[d]))

    def meet(ds):
        first = PLACE[ds[0]] * ROWS
        size = len(ds) * ROWS
        here = txt[first : first + size, :]
        grad = jnp.zeros((size, D), F32)
        for i in range(2):
            logits = jnp.dot(here, low[i], preferred_element_type=F32)
            parts = []
            dot = jnp.zeros((1, COLS), F32)
            for n, d in enumerate(ds):
                step = 2 * d + i - core
                met = jnp.logical_and(step >= 0, step < CYCLE).astype(F32)
                offset = offsets[jnp.clip(step, 0, CYCLE - 1)]
                own = logits[n * ROWS : (n + 1) * ROWS]
                positive = (((gap - offset) & (COLS - 1)) == 0).astype(F32)
                slope = (temper * (jax.nn.sigmoid(temper * own + shift) - positive)) * met
                slope = slope.astype(BF16)
                dot = dot + jnp.sum(slope.astype(F32) * own, axis=0, keepdims=True)
                slopes[i, (PLACE[d]) * ROWS : (PLACE[d] + 1) * ROWS, :] = slope
                parts.append(slope)
            dots[i] = dots[i] + jnp.broadcast_to(dot, dots.shape[1:])
            grad = grad + lax.dot_general(
                slopes[i, first : first + size, :], low[i], (((1,), (1,)), ((), ())), preferred_element_type=F32
            )
        for n, d in enumerate(ds):
            part = grad[n * ROWS : (n + 1) * ROWS]
            if d in (0, 2, 5):
                keep[PLACE[d]] = part
            else:
                f_send[d] = part.astype(BF16)

    share.wait_recv()
    meet((0, 2, 5))
    to1.wait_recv()
    to3.wait_recv()
    to4.wait_recv()

    @pl.when(core == 1)
    def _():
        to6.wait_recv()

    meet((1, 3, 4, 6))
    for d in (4, 3, 1):
        back(d).start()

    @pl.when(core == 1)
    def _():
        back(6).start()

    def image_part(i, store):
        third = D // 3
        dot = dots[i][:1]
        for t in range(3):
            part = lax.dot_general(
                txt[:, t * third : (t + 1) * third], slopes[i], (((0,), (0,)), ((), ())), preferred_element_type=F32
            )
            part = part - low[i, t * third : (t + 1) * third, :].astype(F32) * dot
            for u in range(3):
                v = 3 * t + u
                chunk = part[u * MAIN : (u + 1) * MAIN]
                if v < NW:
                    store(v, 0, MAIN, chunk)
                else:
                    for q in range(NW):
                        store(q, MAIN, FEAT, chunk[q * TAIL : (q + 1) * TAIL])

    def to_other(v, lo, hi, chunk):
        p_send[v, lo:hi, :] = chunk.astype(BF16)

    def to_own(v, lo, hi, chunk):
        p_own[v, lo:hi, :] = chunk

    image_part(1 - core, to_other)
    pair = remote(p_send, p_recv, s_ss.at[1], s_rs.at[1], other)
    pair.start()
    image_part(core, to_own)
    pair.wait_recv()
    for v in range(NW):
        p_own[v] = p_own[v] + p_recv[v].astype(F32)
        e_send[v] = p_own[v].astype(BF16)
    e_copies = []
    for start in (base2, base):
        for j in (1, 3, 2):
            n = len(e_copies)
            copy = remote(
                e_send.at[start + near(j)], e_recv.at[n], e_ss.at[n], e_rs.at[n], (dp, base + near(j))
            )
            copy.start()
            e_copies.append(copy)

    lane = lax.broadcasted_iota(jnp.int32, (ROWS, MAIN), 1)

    def pieces(part, fill, store):
        tail = part[:, NW * MAIN :]
        for v in range(NW):
            rest = pltpu.roll(tail, MAIN - v * TAIL, 1) if v else tail
            store(v, part[:, v * MAIN : (v + 1) * MAIN], jnp.where(lane < TAIL, rest, fill))

    def to_row(v, main, rest):
        g_send[v, :, :MAIN] = main
        g_send[v, :, MAIN:] = rest

    scaled = unit[...]
    part = keep[PLACE[0]]
    part = part - scaled * jnp.sum(scaled * part, axis=1, keepdims=True)
    pieces(part, tnorm[...], to_row)
    g_copies = []
    for j in range(1, NW):
        copy = remote(g_send.at[lax.rem(w + j, NW)], g_recv.at[w], g_ss.at[j], g_rs.at[j], across(j))
        copy.start()
        g_copies.append(copy)
    g_recv[w] = g_send[w]

    h_copies = []

    def send_home(t, d, part):
        text = txt[rows_of(d), :].astype(F32)
        part = part - text * jnp.sum(text * part, axis=1, keepdims=True)

        def to_home(v, main, rest):
            h_send[t, v, :, :MAIN] = main.astype(BF16)
            h_send[t, v, :, MAIN:] = rest.astype(BF16)

        pieces(part, 0.0, to_home)
        owner = lax.rem(chip - d + chips, chips) * 2 + core
        for j in range(NW):
            to = lax.rem(w + j, NW)
            copy = remote(h_send.at[t, to], h_recv.at[t, w], h_ss.at[t, j], h_rs.at[t, j], (owner, to))
            copy.start()
            h_copies.append(copy)

    back(4).wait_recv()
    keep[PLACE[5]] = keep[PLACE[5]] + f_recv[4].astype(F32)

    @pl.when(core == 1)
    def _():
        back(6).wait_recv()
        keep[PLACE[5]] = keep[PLACE[5]] + f_recv[6].astype(F32)

    send_home(0, 5, keep[PLACE[5]])
    back(1).wait_recv()
    back(3).wait_recv()
    send_home(1, 2, keep[PLACE[2]] + f_recv[1].astype(F32) + f_recv[3].astype(F32))

    grad = p_own[w2]
    for n in range(3):
        e_copies[n].wait_recv()
        grad = grad + e_recv[n].astype(F32)
    z_send[...] = grad.astype(BF16)
    z_back = remote(z_send, z_recv, z_ss.at[0], z_rs.at[0], partner)
    z_back.start()

    grad = p_own[w]
    for n in range(3, 6):
        e_copies[n].wait_recv()
        grad = grad + e_recv[n].astype(F32)
    z_back.wait_recv()
    grad = grad + z_recv[...].astype(F32)
    out[0] = grad * inorm
    put_img = pltpu.make_async_copy(out.at[0], out_hbm.at[pl.ds(0, FEAT), :], local_sem.at[5])
    put_img.start()
    for copy in g_copies + h_copies:
        copy.wait_recv()
    whole = g_recv[...] + h_recv[0].astype(F32) + h_recv[1].astype(F32)
    whole = whole.reshape(COLS, COLS).T
    out[1] = whole[:FEAT] * whole[FEAT : FEAT + 1]
    put_txt = pltpu.make_async_copy(out.at[1], out_hbm.at[pl.ds(FEAT, FEAT), :], local_sem.at[6])
    put_txt.start()

    for copy in a_copies + b_copies + e_copies + g_copies + h_copies:
        copy.wait_send()
    for copy in (to1, to2, to3, to4, to5, share, pair, z_copy, z_back):
        copy.wait_send()
    for d in (1, 3, 4):
        back(d).wait_send()

    @pl.when(core == 1)
    def _():
        to6.wait_send()
        back(6).wait_send()

    put_img.wait()
    put_txt.wait()


def solution(mesh):
    chips = mesh.shape["dp"] // 2
    slots = len(ORDER)
    dma = pltpu.SemaphoreType.DMA

    def body(image_emb, text_emb, pair_offsets, log_scale, bias):
        shape = jax.ShapeDtypeStruct((2 * FEAT, COLS), F32)
        hbm = pl.BlockSpec(memory_space=pltpu.HBM)
        grads = pl.pallas_call(
            functools.partial(kernel, chips),
            out_shape=shape,
            in_specs=[hbm] * 5,
            out_specs=hbm,
            scratch_shapes=[
                pltpu.SMEM((CYCLE,), jnp.int32),
                pltpu.SMEM((1,), F32),
                pltpu.SMEM((1,), F32),
                pltpu.VMEM((NW, FEAT, COLS), BF16),
                pltpu.VMEM((FEAT, COLS), BF16),
                pltpu.VMEM((COLS, COLS), F32),
                pltpu.VMEM((NW, ROWS, COLS), BF16),
                pltpu.VMEM((NW, ROWS, COLS), BF16),
                pltpu.VMEM((2, D, COLS), BF16),
                pltpu.VMEM((slots * ROWS, D), BF16),
                pltpu.VMEM((ROWS, D), F32),
                pltpu.VMEM((ROWS, MAIN), F32),
                pltpu.VMEM((2, slots * ROWS, COLS), BF16),
                pltpu.VMEM((2, 8, COLS), F32),
                pltpu.VMEM((slots, ROWS, D), BF16),
                pltpu.VMEM((slots, ROWS, D), BF16),
                pltpu.VMEM((NW, FEAT, COLS), BF16),
                pltpu.VMEM((NW, FEAT, COLS), BF16),
                pltpu.VMEM((NW, FEAT, COLS), F32),
                pltpu.VMEM((NW, FEAT, COLS), BF16),
                pltpu.VMEM((6, FEAT, COLS), BF16),
                pltpu.VMEM((FEAT, COLS), BF16),
                pltpu.VMEM((FEAT, COLS), BF16),
                pltpu.VMEM((3, ROWS, D), F32),
                pltpu.VMEM((NW, ROWS, COLS), F32),
                pltpu.VMEM((NW, ROWS, COLS), F32),
                pltpu.VMEM((2, NW, ROWS, COLS), BF16),
                pltpu.VMEM((2, NW, ROWS, COLS), BF16),
                pltpu.VMEM((2, FEAT, COLS), F32),
                dma((7,)),
                dma((NW,)),
                dma((NW,)),
                dma((NW,)),
                dma((NW,)),
                dma((slots,)),
                dma((slots,)),
                dma((slots,)),
                dma((slots,)),
                dma((NW,)),
                dma((NW,)),
                dma((NW,)),
                dma((NW,)),
                dma((2,)),
                dma((2,)),
                dma((1,)),
                dma((1,)),
                dma((2, NW)),
                dma((2, NW)),
            ],
            compiler_params=pltpu.CompilerParams(
                collective_id=0, has_side_effects=True, vmem_limit_bytes=60 * 1024 * 1024
            ),
        )(image_emb, text_emb, pair_offsets, log_scale, bias)
        return grads[:FEAT], grads[FEAT:]

    placed = (P("width", "dp"), P("width", "dp"), P(), P(), P())
    return jax.shard_map(
        body,
        mesh=mesh,
        in_specs=placed,
        out_specs=(P("width", "dp"), P("width", "dp")),
        check_vma=False,
    )
```

```python
import functools

import jax
import jax.numpy as jnp
from jax import lax
from jax.experimental import pallas as pl
from jax.experimental.pallas import tpu as pltpu
from jax.sharding import PartitionSpec as P

MESH = pl.DeviceIdType.MESH
F32 = jnp.float32
BF16 = jnp.bfloat16
EPSILON = 1e-06
CYCLE = 12
NW = 8
NX = 4
FEAT = 144
MAIN = 128
TAIL = FEAT - MAIN
D = NW * FEAT
COLS = 256
ROWS = COLS // NW
NY = 8
REACH = 6
ORDER = (0, 2, 5, 1, 3, 4, 6)
PLACE = {d: i for i, d in enumerate(ORDER)}


def rows_of(d):
    return pl.ds(PLACE[d] * ROWS, ROWS)


def kernel(
    chips,
    img_hbm,
    txt_hbm,
    offsets_hbm,
    log_scale,
    bias,
    out,
    offsets,
    img_raw,
    txt_in,
    txt_wide,
    a_send,
    a_recv,
    low,
    txt,
    unit,
    tnorm,
    slopes,
    dots,
    f_send,
    f_recv,
    p_send,
    p_recv,
    p_own,
    e_send,
    e_recv,
    z_send,
    z_recv,
    keep,
    g_send,
    g_recv,
    h_send,
    h_recv,
    local_sem,
    a_ss,
    a_rs,
    b_ss,
    b_rs,
    c_ss,
    c_rs,
    f_ss,
    f_rs,
    e_ss,
    e_rs,
    g_ss,
    g_rs,
    s_ss,
    s_rs,
    z_ss,
    z_rs,
    h_ss,
    h_rs,
):
    dp = lax.axis_index("dp")
    w = lax.axis_index("width")
    chip = lax.div(dp, 2)
    core = lax.rem(dp, 2)

    def along(d):
        return (lax.rem(chip + d + chips, chips) * 2 + core, w)

    def across(j):
        return (dp, lax.rem(w + j, NW))

    other = (dp + 1 - 2 * core, w)
    y = lax.rem(chip, NY)
    first, last = y == 0, y == NY - 1
    x = lax.rem(w, NX)
    base = w - x
    base2 = NX - base
    w2 = base2 + x
    partner = (dp, w2)

    def near(j):
        return lax.rem(x + j, NX)

    def remote(src, dst, ss, rs, to):
        return pltpu.make_async_remote_copy(
            src_ref=src, dst_ref=dst, send_sem=ss, recv_sem=rs, device_id=to, device_id_type=MESH
        )

    barrier = pltpu.get_barrier_semaphore()
    peers = [along(d) for d in (5, -5, 2, -2, 1, -1)] + [across(j) for j in range(1, NW)] + [other]
    for peer in peers:
        pl.semaphore_signal(barrier, inc=1, device_id=peer, device_id_type=MESH)

    get_txt = pltpu.make_async_copy(txt_hbm, txt_in, local_sem.at[0])
    get_img = pltpu.make_async_copy(img_hbm, img_raw.at[w], local_sem.at[1])
    get_txt.start()
    get_img.start()
    get_offsets = pltpu.make_async_copy(offsets_hbm, offsets, local_sem.at[2])
    get_offsets.start()

    @pl.when(core == 0)
    def _():
        txt[rows_of(REACH), :] = jnp.zeros((ROWS, D), BF16)

    txt_wide[FEAT:, :] = jnp.zeros((COLS - FEAT, COLS), F32)
    dots[...] = jnp.zeros(dots.shape, F32)
    get_txt.wait()
    txt_wide[:FEAT, :] = txt_in[...].astype(F32)
    a_send[...] = txt_wide[...].T.astype(BF16).reshape(NW, ROWS, COLS)
    get_img.wait()
    get_offsets.wait()
    pl.semaphore_wait(barrier, len(peers))

    z_copy = remote(img_raw.at[w], img_raw.at[w], b_ss.at[0], b_rs.at[0], partner)
    z_copy.start()
    a_copies = []
    for j in range(1, NW):
        copy = remote(a_send.at[lax.rem(w + j, NW)], a_recv.at[w], a_ss.at[j], a_rs.at[j], across(j))
        copy.start()
        a_copies.append(copy)
    a_recv[w] = a_send[w]
    for copy in a_copies:
        copy.wait_recv()
    b_copies = []
    for j in (1, 3, 2):
        copy = remote(img_raw.at[w], img_raw.at[w], b_ss.at[j], b_rs.at[j], (dp, base + near(j)))
        copy.start()
        b_copies.append(copy)

    tail = jnp.zeros((ROWS, MAIN), F32)
    for v in range(NW):
        piece = a_recv[v].astype(F32)
        unit[:, v * MAIN : (v + 1) * MAIN] = piece[:, :MAIN]
        rest = piece[:, MAIN:]
        tail = tail + (pltpu.roll(rest, v * TAIL, 1) if v else rest)
    unit[:, NW * MAIN :] = tail
    raw = unit[...]
    norm = lax.rsqrt(jnp.sum(raw * raw, axis=1, keepdims=True) + EPSILON)
    scaled = raw * norm
    unit[...] = scaled
    tnorm[...] = jnp.broadcast_to(norm, tnorm.shape)
    txt[rows_of(0), :] = scaled.astype(BF16)

    def pass_text(src, dst, to, sem=None):
        sem = dst if sem is None else sem
        return remote(txt.at[rows_of(src)], txt.at[rows_of(dst)], c_ss.at[sem], c_rs.at[dst], to)

    to2 = pass_text(0, 2, along(2))
    to5 = pass_text(0, 5, along(5))
    to5.start()
    to2.start()
    to1_last = pass_text(0, 1, along(1), 0)
    to4_last = pass_text(2, 4, along(2), 0)
    to3_first = pass_text(5, 3, along(-2), 0)

    @pl.when(y == NY - 2)
    def _():
        to1_last.start()


    z_copy.wait_recv()
    for j in (1, 3, 2):
        copy = remote(img_raw.at[w2], img_raw.at[w2], b_ss.at[NX + j], b_rs.at[NX + j], (dp, base + near(j)))
        copy.start()
        b_copies.append(copy)

    to2.wait_recv()
    to1 = pass_text(2, 1, along(-1))
    to3 = pass_text(2, 3, along(1))

    @pl.when(y != 0)
    def _():
        to1.start()

    @pl.when(y != NY - 1)
    def _():
        to3.start()

    @pl.when(y == NY - 3)
    def _():
        to4_last.start()

    to5.wait_recv()
    to4 = pass_text(5, 4, along(-1))
    to6 = pass_text(5, 6, along(1))

    @pl.when(y != 0)
    def _():
        to4.start()

    @pl.when(core == 1)
    def _():
        to6.start()

    @pl.when(y == 2)
    def _():
        to3_first.start()

    def squares(v):
        return jnp.sum(jnp.square(img_raw[v].astype(F32)), axis=0, keepdims=True)

    total = squares(w) + squares(w2)
    for n, copy in enumerate(b_copies):
        copy.wait_recv()
        j = (1, 3, 2)[n % 3]
        total = total + squares((base if n < 3 else base2) + near(NX - j))
    inorm = lax.rsqrt(total + EPSILON)
    for v in range(NW):
        scaled = (img_raw[v].astype(F32) * inorm).astype(BF16)
        low[core, v * MAIN : (v + 1) * MAIN, :] = scaled[:MAIN]
        low[core, NW * MAIN + v * TAIL : NW * MAIN + (v + 1) * TAIL, :] = scaled[MAIN:]
    share = remote(low.at[core], low.at[core], s_ss.at[0], s_rs.at[0], other)
    share.start()

    temper = jnp.exp(jnp.full((1, COLS), log_scale[0], F32))
    shift = bias[0]
    col = lax.broadcasted_iota(jnp.int32, (ROWS, COLS), 1)
    row = lax.broadcasted_iota(jnp.int32, (ROWS, COLS), 0) + w * ROWS
    gap = col - row

    home = {
        1: (jnp.where(last, -1, 1), jnp.where(last, 0, 1)),
        3: (jnp.where(first, 2, -1), jnp.where(first, 5, 3)),
        4: (jnp.where(last, -2, 1), jnp.where(last, 2, 4)),
        6: (-1, 6),
    }

    def back(d):
        to, slot = home[d]
        return remote(f_send.at[d], f_recv.at[slot], f_ss.at[d], f_rs.at[slot], along(to))

    def add_part(place, slot):
        remote(f_send.at[slot], f_recv.at[slot], f_ss.at[slot], f_rs.at[slot], other).wait_recv()
        keep[place] = keep[place] + f_recv[slot].astype(F32)

    def meet(ds):
        first = PLACE[ds[0]] * ROWS
        size = len(ds) * ROWS
        here = txt[first : first + size, :]
        grad = jnp.zeros((size, D), F32)
        for i in range(2):
            logits = jnp.dot(here, low[i], preferred_element_type=F32)
            parts = []
            dot = jnp.zeros((1, COLS), F32)
            for n, d in enumerate(ds):
                step = 2 * d + i - core
                met = jnp.logical_and(step >= 0, step < CYCLE).astype(F32)
                offset = offsets[jnp.clip(step, 0, CYCLE - 1)]
                own = logits[n * ROWS : (n + 1) * ROWS]
                positive = (((gap - offset) & (COLS - 1)) == 0).astype(F32)
                slope = (temper * (jax.nn.sigmoid(temper * own + shift) - positive)) * met
                slope = slope.astype(BF16)
                dot = dot + jnp.sum(slope.astype(F32) * own, axis=0, keepdims=True)
                slopes[i, (PLACE[d]) * ROWS : (PLACE[d] + 1) * ROWS, :] = slope
                parts.append(slope)
            dots[i] = dots[i] + jnp.broadcast_to(dot, dots.shape[1:])
            grad = grad + lax.dot_general(
                slopes[i, first : first + size, :], low[i], (((1,), (1,)), ((), ())), preferred_element_type=F32
            )
        for n, d in enumerate(ds):
            part = grad[n * ROWS : (n + 1) * ROWS]
            if d in (0, 2, 5):
                keep[PLACE[d]] = part
            else:
                f_send[d] = part.astype(BF16)

    share.wait_recv()
    meet((0, 2, 5))
    to1.wait_recv()
    to3.wait_recv()
    to4.wait_recv()

    @pl.when(core == 1)
    def _():
        to6.wait_recv()

    meet((1, 3, 4, 6))
    for d in (4, 3, 1):
        back(d).start()

    @pl.when(core == 1)
    def _():
        back(6).start()

    def image_part(i, store):
        third = D // 3
        dot = dots[i][:1]
        for t in range(3):
            part = lax.dot_general(
                txt[:, t * third : (t + 1) * third], slopes[i], (((0,), (0,)), ((), ())), preferred_element_type=F32
            )
            part = part - low[i, t * third : (t + 1) * third, :].astype(F32) * dot
            for u in range(3):
                v = 3 * t + u
                chunk = part[u * MAIN : (u + 1) * MAIN]
                if v < NW:
                    store(v, 0, MAIN, chunk)
                else:
                    for q in range(NW):
                        store(q, MAIN, FEAT, chunk[q * TAIL : (q + 1) * TAIL])

    def to_other(v, lo, hi, chunk):
        p_send[v, lo:hi, :] = chunk.astype(BF16)

    def to_own(v, lo, hi, chunk):
        p_own[v, lo:hi, :] = chunk

    image_part(1 - core, to_other)
    pair = remote(p_send, p_recv, s_ss.at[1], s_rs.at[1], other)
    pair.start()
    image_part(core, to_own)
    pair.wait_recv()
    for v in range(NW):
        p_own[v] = p_own[v] + p_recv[v].astype(F32)
        e_send[v] = p_own[v].astype(BF16)
    e_copies = []
    for start in (base2, base):
        for j in (1, 3, 2):
            n = len(e_copies)
            copy = remote(
                e_send.at[start + near(j)], e_recv.at[n], e_ss.at[n], e_rs.at[n], (dp, base + near(j))
            )
            copy.start()
            e_copies.append(copy)

    lane = lax.broadcasted_iota(jnp.int32, (ROWS, MAIN), 1)

    def pieces(part, fill, store):
        tail = part[:, NW * MAIN :]
        for v in range(NW):
            rest = pltpu.roll(tail, MAIN - v * TAIL, 1) if v else tail
            store(v, part[:, v * MAIN : (v + 1) * MAIN], jnp.where(lane < TAIL, rest, fill))

    def to_row(v, main, rest):
        g_send[v, :, :MAIN] = main
        g_send[v, :, MAIN:] = rest

    h_copies = []

    def send_home(t, d, part):
        text = txt[rows_of(d), :].astype(F32)
        part = part - text * jnp.sum(text * part, axis=1, keepdims=True)

        def to_home(v, main, rest):
            h_send[t, v, :, :MAIN] = main.astype(BF16)
            h_send[t, v, :, MAIN:] = rest.astype(BF16)

        pieces(part, 0.0, to_home)
        owner = lax.rem(chip - d + chips, chips) * 2 + core
        for j in range(NW):
            to = lax.rem(w + j, NW)
            copy = remote(h_send.at[t, to], h_recv.at[t, w], h_ss.at[t, j], h_rs.at[t, j], (owner, to))
            copy.start()
            h_copies.append(copy)

    @pl.when(y != 0)
    def _():
        add_part(PLACE[5], 4)

    @pl.when(core == 1)
    def _():
        add_part(PLACE[5], 6)

    @pl.when(y == 2)
    def _():
        add_part(PLACE[5], 5)

    send_home(0, 5, keep[PLACE[5]])

    @pl.when(y != 0)
    def _():
        add_part(PLACE[2], 1)

    @pl.when(y != NY - 1)
    def _():
        add_part(PLACE[2], 3)

    @pl.when(y == NY - 3)
    def _():
        add_part(PLACE[2], 2)

    send_home(1, 2, keep[PLACE[2]])

    @pl.when(y == NY - 2)
    def _():
        add_part(PLACE[0], 0)

    scaled = unit[...]
    part = keep[PLACE[0]]
    part = part - scaled * jnp.sum(scaled * part, axis=1, keepdims=True)
    pieces(part, tnorm[...], to_row)
    g_copies = []
    for j in range(1, NW):
        copy = remote(g_send.at[lax.rem(w + j, NW)], g_recv.at[w], g_ss.at[j], g_rs.at[j], across(j))
        copy.start()
        g_copies.append(copy)
    g_recv[w] = g_send[w]

    grad = p_own[w2]
    for n in range(3):
        e_copies[n].wait_recv()
        grad = grad + e_recv[n].astype(F32)
    z_send[...] = grad.astype(BF16)
    z_back = remote(z_send, z_recv, z_ss.at[0], z_rs.at[0], partner)
    z_back.start()

    grad = p_own[w]
    for n in range(3, 6):
        e_copies[n].wait_recv()
        grad = grad + e_recv[n].astype(F32)
    z_back.wait_recv()
    grad = grad + z_recv[...].astype(F32)
    out[:FEAT] = grad * inorm
    for copy in g_copies + h_copies:
        copy.wait_recv()
    whole = g_recv[...] + h_recv[0].astype(F32) + h_recv[1].astype(F32)
    whole = whole.reshape(COLS, COLS).T
    out[FEAT:] = whole[:FEAT] * whole[FEAT : FEAT + 1]

    for copy in a_copies + b_copies + e_copies + g_copies + h_copies:
        copy.wait_send()
    for copy in (to2, to5, share, pair, z_copy, z_back):
        copy.wait_send()
    for d in (1, 3, 4):
        back(d).wait_send()

    for here, copy in (
        (y != 0, to1),
        (y != NY - 1, to3),
        (y != 0, to4),
        (y == NY - 2, to1_last),
        (y == NY - 3, to4_last),
        (y == 2, to3_first),
    ):
        pl.when(here)(copy.wait_send)

    @pl.when(core == 1)
    def _():
        to6.wait_send()
        back(6).wait_send()


def solution(mesh):
    chips = mesh.shape["dp"] // 2
    slots = len(ORDER)
    dma = pltpu.SemaphoreType.DMA

    def body(image_emb, text_emb, pair_offsets, log_scale, bias):
        shape = jax.ShapeDtypeStruct((2 * FEAT, COLS), F32)
        smem = pl.BlockSpec(memory_space=pltpu.SMEM)
        hbm = pl.BlockSpec(memory_space=pltpu.HBM)
        grads = pl.pallas_call(
            functools.partial(kernel, chips),
            out_shape=shape,
            in_specs=[hbm, hbm, hbm, smem, smem],
            out_specs=pl.BlockSpec(memory_space=pltpu.VMEM),
            scratch_shapes=[
                pltpu.SMEM((CYCLE,), jnp.int32),
                pltpu.VMEM((NW, FEAT, COLS), BF16),
                pltpu.VMEM((FEAT, COLS), BF16),
                pltpu.VMEM((COLS, COLS), F32),
                pltpu.VMEM((NW, ROWS, COLS), BF16),
                pltpu.VMEM((NW, ROWS, COLS), BF16),
                pltpu.VMEM((2, D, COLS), BF16),
                pltpu.VMEM((slots * ROWS, D), BF16),
                pltpu.VMEM((ROWS, D), F32),
                pltpu.VMEM((ROWS, MAIN), F32),
                pltpu.VMEM((2, slots * ROWS, COLS), BF16),
                pltpu.VMEM((2, 8, COLS), F32),
                pltpu.VMEM((slots, ROWS, D), BF16),
                pltpu.VMEM((slots, ROWS, D), BF16),
                pltpu.VMEM((NW, FEAT, COLS), BF16),
                pltpu.VMEM((NW, FEAT, COLS), BF16),
                pltpu.VMEM((NW, FEAT, COLS), F32),
                pltpu.VMEM((NW, FEAT, COLS), BF16),
                pltpu.VMEM((6, FEAT, COLS), BF16),
                pltpu.VMEM((FEAT, COLS), BF16),
                pltpu.VMEM((FEAT, COLS), BF16),
                pltpu.VMEM((3, ROWS, D), F32),
                pltpu.VMEM((NW, ROWS, COLS), F32),
                pltpu.VMEM((NW, ROWS, COLS), F32),
                pltpu.VMEM((2, NW, ROWS, COLS), BF16),
                pltpu.VMEM((2, NW, ROWS, COLS), BF16),
                dma((3,)),
                dma((NW,)),
                dma((NW,)),
                dma((NW,)),
                dma((NW,)),
                dma((slots,)),
                dma((slots,)),
                dma((slots,)),
                dma((slots,)),
                dma((NW,)),
                dma((NW,)),
                dma((NW,)),
                dma((NW,)),
                dma((2,)),
                dma((2,)),
                dma((1,)),
                dma((1,)),
                dma((2, NW)),
                dma((2, NW)),
            ],
            compiler_params=pltpu.CompilerParams(
                collective_id=0, has_side_effects=True, vmem_limit_bytes=40 * 1024 * 1024
            ),
        )(
            *(pltpu.with_memory_space_constraint(v, pltpu.HBM) for v in (image_emb, text_emb, pair_offsets)), log_scale, bias
        )
        return grads[:FEAT], grads[FEAT:]

    placed = (P("width", "dp"), P("width", "dp"), P(), P(), P())
    return jax.shard_map(
        body,
        mesh=mesh,
        in_specs=placed,
        out_specs=(P("width", "dp"), P("width", "dp")),
        check_vma=False,
    )
```

```python
import functools

import jax
import jax.numpy as jnp
from jax import lax
from jax.experimental import pallas as pl
from jax.experimental.pallas import tpu as pltpu
from jax.sharding import PartitionSpec as P

MESH = pl.DeviceIdType.MESH
F32 = jnp.float32
BF16 = jnp.bfloat16
EPSILON = 1e-06
CYCLE = 12
NW = 8
NX = 4
FEAT = 144
MAIN = 128
TAIL = FEAT - MAIN
D = NW * FEAT
COLS = 256
ROWS = COLS // NW
NY = 8
REACH = 6
ORDER = (0, 2, 5, 1, 3, 4, 6)
PLACE = {d: i for i, d in enumerate(ORDER)}


def rows_of(d):
    return pl.ds(PLACE[d] * ROWS, ROWS)


def kernel(
    chips,
    img_hbm,
    txt_hbm,
    offsets_hbm,
    log_scale,
    bias,
    out,
    offsets,
    img_raw,
    txt_in,
    txt_wide,
    a_send,
    a_recv,
    low,
    txt,
    unit,
    tnorm,
    slopes,
    dots,
    f_send,
    f_recv,
    p_send,
    p_recv,
    p_own,
    e_send,
    e_recv,
    z_send,
    z_recv,
    keep,
    g_send,
    g_recv,
    h_send,
    h_recv,
    local_sem,
    a_ss,
    a_rs,
    b_ss,
    b_rs,
    c_ss,
    c_rs,
    f_ss,
    f_rs,
    e_ss,
    e_rs,
    g_ss,
    g_rs,
    s_ss,
    s_rs,
    z_ss,
    z_rs,
    h_ss,
    h_rs,
):
    dp = lax.axis_index("dp")
    w = lax.axis_index("width")
    chip = lax.div(dp, 2)
    core = lax.rem(dp, 2)

    def along(d):
        return (lax.rem(chip + d + chips, chips) * 2 + core, w)

    def across(j):
        return (dp, lax.rem(w + j, NW))

    other = (dp + 1 - 2 * core, w)
    y = lax.rem(chip, NY)
    first, last = y == 0, y == NY - 1
    x = lax.rem(w, NX)
    base = w - x
    base2 = NX - base
    w2 = base2 + x
    partner = (dp, w2)

    def near(j):
        return lax.rem(x + j, NX)

    def remote(src, dst, ss, rs, to):
        return pltpu.make_async_remote_copy(
            src_ref=src, dst_ref=dst, send_sem=ss, recv_sem=rs, device_id=to, device_id_type=MESH
        )

    barrier = pltpu.get_barrier_semaphore()
    peers = [along(d) for d in (5, -5, 2, -2, 1, -1)] + [across(j) for j in range(1, NW)] + [other]
    for peer in peers:
        pl.semaphore_signal(barrier, inc=1, device_id=peer, device_id_type=MESH)

    get_txt = pltpu.make_async_copy(txt_hbm, txt_in, local_sem.at[0])
    get_img = pltpu.make_async_copy(img_hbm, img_raw.at[w], local_sem.at[1])
    get_txt.start()
    get_img.start()
    get_offsets = pltpu.make_async_copy(offsets_hbm, offsets, local_sem.at[2])
    get_offsets.start()

    @pl.when(core == 0)
    def _():
        txt[rows_of(REACH), :] = jnp.zeros((ROWS, D), BF16)

    txt_wide[FEAT:, :] = jnp.zeros((COLS - FEAT, COLS), F32)
    dots[...] = jnp.zeros(dots.shape, F32)
    get_txt.wait()
    txt_wide[:FEAT, :] = txt_in[...].astype(F32)
    a_send[...] = txt_wide[...].T.astype(BF16).reshape(NW, ROWS, COLS)
    get_img.wait()
    get_offsets.wait()
    pl.semaphore_wait(barrier, len(peers))

    z_copy = remote(img_raw.at[w], img_raw.at[w], b_ss.at[0], b_rs.at[0], partner)
    z_copy.start()
    a_copies = []
    for j in range(1, NW):
        copy = remote(a_send.at[lax.rem(w + j, NW)], a_recv.at[w], a_ss.at[j], a_rs.at[j], across(j))
        copy.start()
        a_copies.append(copy)
    a_recv[w] = a_send[w]
    for copy in a_copies:
        copy.wait_recv()
    b_copies = []
    for j in (1, 3, 2):
        copy = remote(img_raw.at[w], img_raw.at[w], b_ss.at[j], b_rs.at[j], (dp, base + near(j)))
        copy.start()
        b_copies.append(copy)

    tail = jnp.zeros((ROWS, MAIN), F32)
    for v in range(NW):
        piece = a_recv[v].astype(F32)
        unit[:, v * MAIN : (v + 1) * MAIN] = piece[:, :MAIN]
        rest = piece[:, MAIN:]
        tail = tail + (pltpu.roll(rest, v * TAIL, 1) if v else rest)
    unit[:, NW * MAIN :] = tail
    raw = unit[...]
    norm = lax.rsqrt(jnp.sum(raw * raw, axis=1, keepdims=True) + EPSILON)
    scaled = raw * norm
    unit[...] = scaled
    tnorm[...] = jnp.broadcast_to(norm, tnorm.shape)
    txt[rows_of(0), :] = scaled.astype(BF16)

    def pass_text(src, dst, to, sem=None):
        sem = dst if sem is None else sem
        return remote(txt.at[rows_of(src)], txt.at[rows_of(dst)], c_ss.at[sem], c_rs.at[dst], to)

    to2 = pass_text(0, 2, along(2))
    to5 = pass_text(0, 5, along(5))
    to5.start()
    to2.start()
    to1_last = pass_text(0, 1, along(1), 0)
    to4_last = pass_text(2, 4, along(2), 0)
    to3_first = pass_text(5, 3, along(-2), 0)

    @pl.when(y == NY - 2)
    def _():
        to1_last.start()


    z_copy.wait_recv()
    for j in (1, 3, 2):
        copy = remote(img_raw.at[w2], img_raw.at[w2], b_ss.at[NX + j], b_rs.at[NX + j], (dp, base + near(j)))
        copy.start()
        b_copies.append(copy)

    to2.wait_recv()
    to1 = pass_text(2, 1, along(-1))
    to3 = pass_text(2, 3, along(1))

    @pl.when(y != 0)
    def _():
        to1.start()

    @pl.when(y != NY - 1)
    def _():
        to3.start()

    @pl.when(y == NY - 3)
    def _():
        to4_last.start()

    to5.wait_recv()
    to4 = pass_text(5, 4, along(-1))
    to6 = pass_text(5, 6, along(1))

    @pl.when(y != 0)
    def _():
        to4.start()

    @pl.when(core == 1)
    def _():
        to6.start()

    @pl.when(y == 2)
    def _():
        to3_first.start()

    def squares(v):
        return jnp.sum(jnp.square(img_raw[v].astype(F32)), axis=0, keepdims=True)

    total = squares(w) + squares(w2)
    for n, copy in enumerate(b_copies):
        copy.wait_recv()
        j = (1, 3, 2)[n % 3]
        total = total + squares((base if n < 3 else base2) + near(NX - j))
    inorm = lax.rsqrt(total + EPSILON)
    for v in range(NW):
        scaled = (img_raw[v].astype(F32) * inorm).astype(BF16)
        low[core, v * MAIN : (v + 1) * MAIN, :] = scaled[:MAIN]
        low[core, NW * MAIN + v * TAIL : NW * MAIN + (v + 1) * TAIL, :] = scaled[MAIN:]
    share = remote(low.at[core], low.at[core], s_ss.at[0], s_rs.at[0], other)
    share.start()

    temper = jnp.exp(jnp.full((1, COLS), log_scale[0], F32))
    shift = bias[0]
    col = lax.broadcasted_iota(jnp.int32, (ROWS, COLS), 1)
    row = lax.broadcasted_iota(jnp.int32, (ROWS, COLS), 0) + w * ROWS
    gap = col - row

    home = {
        1: (jnp.where(last, -1, 1), jnp.where(last, 0, 1)),
        3: (jnp.where(first, 2, -1), jnp.where(first, 5, 3)),
        4: (jnp.where(last, -2, 1), jnp.where(last, 2, 4)),
        6: (-1, 6),
    }

    def back(d):
        to, slot = home[d]
        return remote(f_send.at[d], f_recv.at[slot], f_ss.at[d], f_rs.at[slot], along(to))

    def add_part(place, slot):
        remote(f_send.at[slot], f_recv.at[slot], f_ss.at[slot], f_rs.at[slot], other).wait_recv()
        keep[place] = keep[place] + f_recv[slot].astype(F32)

    def meet(ds):
        first = PLACE[ds[0]] * ROWS
        size = len(ds) * ROWS
        here = txt[first : first + size, :]
        grad = jnp.zeros((size, D), F32)
        for i in range(2):
            logits = jnp.dot(here, low[i], preferred_element_type=F32)
            parts = []
            dot = jnp.zeros((1, COLS), F32)
            for n, d in enumerate(ds):
                step = 2 * d + i - core
                met = jnp.logical_and(step >= 0, step < CYCLE).astype(F32)
                offset = offsets[jnp.clip(step, 0, CYCLE - 1)]
                own = logits[n * ROWS : (n + 1) * ROWS]
                positive = (((gap - offset) & (COLS - 1)) == 0).astype(F32)
                slope = (temper * (jax.nn.sigmoid(temper * own + shift) - positive)) * met
                slope = slope.astype(BF16)
                dot = dot + jnp.sum(slope.astype(F32) * own, axis=0, keepdims=True)
                slopes[i, (PLACE[d]) * ROWS : (PLACE[d] + 1) * ROWS, :] = slope
                parts.append(slope)
            dots[i] = dots[i] + jnp.broadcast_to(dot, dots.shape[1:])
            grad = grad + lax.dot_general(
                slopes[i, first : first + size, :], low[i], (((1,), (1,)), ((), ())), preferred_element_type=F32
            )
        for n, d in enumerate(ds):
            part = grad[n * ROWS : (n + 1) * ROWS]
            if d in (0, 2, 5):
                keep[PLACE[d]] = part
            else:
                f_send[d] = part.astype(BF16)

    share.wait_recv()
    meet((0, 2, 5))
    to1.wait_recv()
    to3.wait_recv()
    to4.wait_recv()

    @pl.when(core == 1)
    def _():
        to6.wait_recv()

    meet((1, 3, 4, 6))
    for d in (4, 3, 1):
        back(d).start()

    @pl.when(core == 1)
    def _():
        back(6).start()

    def image_part(i, store):
        third = D // 3
        dot = dots[i][:1]
        for t in range(3):
            part = lax.dot_general(
                txt[:, t * third : (t + 1) * third], slopes[i], (((0,), (0,)), ((), ())), preferred_element_type=F32
            )
            part = part - low[i, t * third : (t + 1) * third, :].astype(F32) * dot
            for u in range(3):
                v = 3 * t + u
                chunk = part[u * MAIN : (u + 1) * MAIN]
                if v < NW:
                    store(v, 0, MAIN, chunk)
                else:
                    for q in range(NW):
                        store(q, MAIN, FEAT, chunk[q * TAIL : (q + 1) * TAIL])

    def to_other(v, lo, hi, chunk):
        p_send[v, lo:hi, :] = chunk.astype(BF16)

    def to_own(v, lo, hi, chunk):
        p_own[v, lo:hi, :] = chunk

    image_part(1 - core, to_other)
    pair = remote(p_send, p_recv, s_ss.at[1], s_rs.at[1], other)
    pair.start()
    image_part(core, to_own)

    lane = lax.broadcasted_iota(jnp.int32, (8, MAIN), 1)

    def pieces(part, more, store):
        tail = part[:, NW * MAIN :]
        for v in range(NW):
            packed = more
            for q in range(4):
                shift = (32 * q - v * TAIL) % MAIN
                rest = tail[8 * q : 8 * q + 8]
                rest = pltpu.roll(rest, shift, 1) if shift else rest
                packed = jnp.where((lane >= 32 * q) & (lane < 32 * q + TAIL), rest, packed)
            rest = jnp.concatenate([packed, jnp.zeros((8, MAIN), F32)], axis=0)
            store(v, part[:, v * MAIN : (v + 1) * MAIN].astype(BF16), rest.astype(BF16))

    def to_row(v, main, rest):
        g_send[v, :ROWS, :] = main
        g_send[v, ROWS:, :] = rest

    g_copies = [
        remote(g_send.at[lax.rem(w + j, NW)], g_recv.at[w], g_ss.at[j], g_rs.at[j], across(j)) for j in range(1, NW)
    ]

    def send_own():
        scaled = unit[...]
        part = keep[PLACE[0]]
        part = part - scaled * jnp.sum(scaled * part, axis=1, keepdims=True)
        norm = tnorm[...]
        high = norm.astype(BF16).astype(F32)
        norms = jnp.zeros((8, MAIN), F32)
        for q in range(4):
            norms = jnp.where(lane == 32 * q + TAIL, high[8 * q : 8 * q + 8], norms)
            norms = jnp.where(lane == 32 * q + TAIL + 1, (norm - high)[8 * q : 8 * q + 8], norms)
        pieces(part, norms, to_row)
        for copy in g_copies:
            copy.start()
        g_recv[w] = g_send[w]

    pl.when(y != NY - 2)(send_own)

    pair.wait_recv()
    for v in range(NW):
        p_own[v] = p_own[v] + p_recv[v].astype(F32)
        e_send[v] = p_own[v].astype(BF16)
    e_copies = [
        remote(e_send.at[start + near(j)], e_recv.at[n + j], e_ss.at[n + j], e_rs.at[n + j], (dp, base + near(j)))
        for n, start in ((NX, base2), (0, base))
        for j in (1, 3, 2)
    ]
    for copy in e_copies[:3]:
        copy.start()

    h_copies = []

    def send_home(t, d, part):
        text = txt[rows_of(d), :].astype(F32)
        part = part - text * jnp.sum(text * part, axis=1, keepdims=True)

        def to_home(v, main, rest):
            h_send[t, v, :ROWS, :] = main
            h_send[t, v, ROWS:, :] = rest

        pieces(part, jnp.zeros((8, MAIN), F32), to_home)
        owner = lax.rem(chip - d + chips, chips) * 2 + core
        for j in range(NW):
            to = lax.rem(w + j, NW)
            copy = remote(h_send.at[t, to], h_recv.at[t, w], h_ss.at[t, j], h_rs.at[t, j], (owner, to))
            copy.start()
            h_copies.append(copy)

    @pl.when(y != 0)
    def _():
        add_part(PLACE[5], 4)

    @pl.when(core == 1)
    def _():
        add_part(PLACE[5], 6)

    @pl.when(y == 2)
    def _():
        add_part(PLACE[5], 5)

    send_home(0, 5, keep[PLACE[5]])

    @pl.when(y != 0)
    def _():
        add_part(PLACE[2], 1)

    @pl.when(y != NY - 1)
    def _():
        add_part(PLACE[2], 3)

    @pl.when(y == NY - 3)
    def _():
        add_part(PLACE[2], 2)

    send_home(1, 2, keep[PLACE[2]])

    @pl.when(y == NY - 2)
    def _():
        add_part(PLACE[0], 0)
        send_own()

    grad = p_own[w2]
    for j, copy in zip((1, 3, 2), e_copies[:3]):
        copy.wait_recv()
        grad = grad + e_recv[NX + j].astype(F32)
    z_send[...] = grad.astype(BF16)
    z_back = remote(z_send, z_recv, z_ss.at[0], z_rs.at[0], partner)
    z_back.start()
    for copy in e_copies[3:]:
        copy.start()
    grad = p_own[w]
    for j, copy in zip((1, 3, 2), e_copies[3:]):
        copy.wait_recv()
        grad = grad + e_recv[j].astype(F32)
    z_back.wait_recv()
    grad = grad + z_recv[...].astype(F32)
    out[:FEAT] = grad * inorm
    for copy in g_copies + h_copies:
        copy.wait_recv()
    whole = g_recv[...].astype(F32) + h_recv[0].astype(F32) + h_recv[1].astype(F32)
    txt_wide[:, :MAIN] = whole[:, :ROWS].reshape(COLS, MAIN)
    packed = whole[:, ROWS : ROWS + 8].reshape(NW * 8, MAIN)
    for q in range(4):
        rest = pltpu.roll(packed, MAIN - 32 * q, 1) if q else packed
        for v in range(NW):
            at = v * ROWS + 8 * q
            txt_wide[at : at + 8, MAIN:] = rest[8 * v : 8 * v + 8]
    whole = txt_wide[...].T
    out[FEAT:] = whole[:FEAT] * (whole[FEAT : FEAT + 1] + whole[FEAT + 1 : FEAT + 2])

    for copy in a_copies + b_copies + e_copies + g_copies + h_copies:
        copy.wait_send()
    for copy in (to2, to5, share, pair, z_copy, z_back):
        copy.wait_send()
    for d in (1, 3, 4):
        back(d).wait_send()

    for here, copy in (
        (y != 0, to1),
        (y != NY - 1, to3),
        (y != 0, to4),
        (y == NY - 2, to1_last),
        (y == NY - 3, to4_last),
        (y == 2, to3_first),
    ):
        pl.when(here)(copy.wait_send)

    @pl.when(core == 1)
    def _():
        to6.wait_send()
        back(6).wait_send()


def solution(mesh):
    chips = mesh.shape["dp"] // 2
    slots = len(ORDER)
    dma = pltpu.SemaphoreType.DMA

    def body(image_emb, text_emb, pair_offsets, log_scale, bias):
        shape = jax.ShapeDtypeStruct((2 * FEAT, COLS), F32)
        smem = pl.BlockSpec(memory_space=pltpu.SMEM)
        hbm = pl.BlockSpec(memory_space=pltpu.HBM)
        grads = pl.pallas_call(
            functools.partial(kernel, chips),
            out_shape=shape,
            in_specs=[hbm, hbm, hbm, smem, smem],
            out_specs=pl.BlockSpec(memory_space=pltpu.VMEM),
            scratch_shapes=[
                pltpu.SMEM((CYCLE,), jnp.int32),
                pltpu.VMEM((NW, FEAT, COLS), BF16),
                pltpu.VMEM((FEAT, COLS), BF16),
                pltpu.VMEM((COLS, COLS), F32),
                pltpu.VMEM((NW, ROWS, COLS), BF16),
                pltpu.VMEM((NW, ROWS, COLS), BF16),
                pltpu.VMEM((2, D, COLS), BF16),
                pltpu.VMEM((slots * ROWS, D), BF16),
                pltpu.VMEM((ROWS, D), F32),
                pltpu.VMEM((ROWS, MAIN), F32),
                pltpu.VMEM((2, slots * ROWS, COLS), BF16),
                pltpu.VMEM((2, 8, COLS), F32),
                pltpu.VMEM((slots, ROWS, D), BF16),
                pltpu.VMEM((slots, ROWS, D), BF16),
                pltpu.VMEM((NW, FEAT, COLS), BF16),
                pltpu.VMEM((NW, FEAT, COLS), BF16),
                pltpu.VMEM((NW, FEAT, COLS), F32),
                pltpu.VMEM((NW, FEAT, COLS), BF16),
                pltpu.VMEM((NW, FEAT, COLS), BF16),
                pltpu.VMEM((FEAT, COLS), BF16),
                pltpu.VMEM((FEAT, COLS), BF16),
                pltpu.VMEM((3, ROWS, D), F32),
                pltpu.VMEM((NW, ROWS + 16, MAIN), BF16),
                pltpu.VMEM((NW, ROWS + 16, MAIN), BF16),
                pltpu.VMEM((2, NW, ROWS + 16, MAIN), BF16),
                pltpu.VMEM((2, NW, ROWS + 16, MAIN), BF16),
                dma((3,)),
                dma((NW,)),
                dma((NW,)),
                dma((NW,)),
                dma((NW,)),
                dma((slots,)),
                dma((slots,)),
                dma((slots,)),
                dma((slots,)),
                dma((NW,)),
                dma((NW,)),
                dma((NW,)),
                dma((NW,)),
                dma((2,)),
                dma((2,)),
                dma((1,)),
                dma((1,)),
                dma((2, NW)),
                dma((2, NW)),
            ],
            compiler_params=pltpu.CompilerParams(
                collective_id=0, has_side_effects=True, vmem_limit_bytes=40 * 1024 * 1024
            ),
        )(
            *(pltpu.with_memory_space_constraint(v, pltpu.HBM) for v in (image_emb, text_emb, pair_offsets)), log_scale, bias
        )
        return grads[:FEAT], grads[FEAT:]

    placed = (P("width", "dp"), P("width", "dp"), P(), P(), P())
    return jax.shard_map(
        body,
        mesh=mesh,
        in_specs=placed,
        out_specs=(P("width", "dp"), P("width", "dp")),
        check_vma=False,
    )
```

```python
import functools

import jax
import jax.numpy as jnp
from jax import lax
from jax.experimental import pallas as pl
from jax.experimental.pallas import tpu as pltpu
from jax.sharding import PartitionSpec as P

MESH = pl.DeviceIdType.MESH
F32 = jnp.float32
BF16 = jnp.bfloat16
EPSILON = 1e-06
CYCLE = 12
NW = 8
NX = 4
FEAT = 144
MAIN = 128
TAIL = FEAT - MAIN
D = NW * FEAT
COLS = 256
ROWS = COLS // NW
NY = 8
REACH = 6
ORDER = (0, 2, 5, 1, 3, 4, 6)
PLACE = {d: i for i, d in enumerate(ORDER)}


def rows_of(d):
    return pl.ds(PLACE[d] * ROWS, ROWS)


def kernel(
    chips,
    img_hbm,
    txt_hbm,
    offsets_hbm,
    log_scale,
    bias,
    out,
    offsets,
    img_raw,
    txt_in,
    txt_wide,
    a_send,
    a_recv,
    low,
    txt,
    unit,
    tnorm,
    slopes,
    dots,
    f_send,
    f_recv,
    p_send,
    p_recv,
    p_own,
    e_send,
    e_recv,
    z_send,
    z_recv,
    keep,
    g_send,
    g_recv,
    h_send,
    h_recv,
    local_sem,
    a_ss,
    a_rs,
    b_ss,
    b_rs,
    c_ss,
    c_rs,
    f_ss,
    f_rs,
    e_ss,
    e_rs,
    g_ss,
    g_rs,
    s_ss,
    s_rs,
    z_ss,
    z_rs,
    h_ss,
    h_rs,
):
    dp = lax.axis_index("dp")
    w = lax.axis_index("width")
    chip = lax.div(dp, 2)
    core = lax.rem(dp, 2)

    def along(d):
        return (lax.rem(chip + d + chips, chips) * 2 + core, w)

    def across(j):
        return (dp, lax.rem(w + j, NW))

    other = (dp + 1 - 2 * core, w)
    y = lax.rem(chip, NY)
    first, last = y == 0, y == NY - 1
    x = lax.rem(w, NX)
    base = w - x
    base2 = NX - base
    w2 = base2 + x
    partner = (dp, w2)

    def near(j):
        return lax.rem(x + j, NX)

    def remote(src, dst, ss, rs, to):
        return pltpu.make_async_remote_copy(
            src_ref=src, dst_ref=dst, send_sem=ss, recv_sem=rs, device_id=to, device_id_type=MESH
        )

    barrier = pltpu.get_barrier_semaphore()

    def arrive(peer):
        pl.semaphore_signal(barrier, inc=1, device_id=peer, device_id_type=MESH)

    for d in (-5, -2, -1):
        arrive(along(d))
    for j in range(1, NW):
        arrive(across(j))
    arrive(other)

    @pl.when(y != NY - 1)
    def _():
        arrive(along(1))

    get_txt = pltpu.make_async_copy(txt_hbm, txt_in, local_sem.at[0])
    get_img = pltpu.make_async_copy(img_hbm, img_raw.at[w], local_sem.at[1])
    get_txt.start()
    get_img.start()
    get_offsets = pltpu.make_async_copy(offsets_hbm, offsets, local_sem.at[2])
    get_offsets.start()

    @pl.when(core == 0)
    def _():
        txt[rows_of(REACH), :] = jnp.zeros((ROWS, D), BF16)

    txt_wide[FEAT:, :] = jnp.zeros((COLS - FEAT, COLS), F32)
    dots[...] = jnp.zeros(dots.shape, F32)
    get_txt.wait()
    txt_wide[:FEAT, :] = txt_in[...].astype(F32)
    a_send[...] = txt_wide[...].T.astype(BF16).reshape(NW, ROWS, COLS)
    get_img.wait()
    get_offsets.wait()
    pl.semaphore_wait(barrier, jnp.where(first, NW + 3, NW + 4))

    z_copy = remote(img_raw.at[w], img_raw.at[w], b_ss.at[0], b_rs.at[0], partner)
    z_copy.start()
    a_copies = []
    for j in range(1, NW):
        copy = remote(a_send.at[lax.rem(w + j, NW)], a_recv.at[w], a_ss.at[j], a_rs.at[j], across(j))
        copy.start()
        a_copies.append(copy)
    a_recv[w] = a_send[w]
    for copy in a_copies:
        copy.wait_recv()
    b_copies = []
    for j in (1, 3, 2):
        copy = remote(img_raw.at[w], img_raw.at[w], b_ss.at[j], b_rs.at[j], (dp, base + near(j)))
        copy.start()
        b_copies.append(copy)

    tail = jnp.zeros((ROWS, MAIN), F32)
    for v in range(NW):
        piece = a_recv[v].astype(F32)
        unit[:, v * MAIN : (v + 1) * MAIN] = piece[:, :MAIN]
        rest = piece[:, MAIN:]
        tail = tail + (pltpu.roll(rest, v * TAIL, 1) if v else rest)
    unit[:, NW * MAIN :] = tail
    raw = unit[...]
    norm = lax.rsqrt(jnp.sum(raw * raw, axis=1, keepdims=True) + EPSILON)
    scaled = raw * norm
    unit[...] = scaled
    tnorm[...] = jnp.broadcast_to(norm, tnorm.shape)
    txt[rows_of(0), :] = scaled.astype(BF16)

    def pass_text(src, dst, to, sem=None):
        sem = dst if sem is None else sem
        return remote(txt.at[rows_of(src)], txt.at[rows_of(dst)], c_ss.at[sem], c_rs.at[dst], to)

    to2 = pass_text(0, 2, along(2))
    to5 = pass_text(0, 5, along(5))
    to5.start()
    to2.start()
    to1_last = pass_text(0, 1, along(1), 0)
    to4_last = pass_text(2, 4, along(2), 0)
    to3_first = pass_text(5, 3, along(-2), 0)

    @pl.when(y == NY - 2)
    def _():
        to1_last.start()


    z_copy.wait_recv()
    for j in (1, 3, 2):
        copy = remote(img_raw.at[w2], img_raw.at[w2], b_ss.at[NX + j], b_rs.at[NX + j], (dp, base + near(j)))
        copy.start()
        b_copies.append(copy)

    to1 = pass_text(2, 1, along(-1))
    to3 = pass_text(2, 3, along(1))
    to4 = pass_text(5, 4, along(-1))
    to6 = pass_text(5, 6, along(1))

    def forward():
        to2.wait_recv()

        @pl.when(y != 0)
        def _():
            to1.start()

        @pl.when(y != NY - 1)
        def _():
            to3.start()

        @pl.when(y == NY - 3)
        def _():
            to4_last.start()

        to5.wait_recv()

        @pl.when(y != 0)
        def _():
            to4.start()

        @pl.when(core == 1)
        def _():
            to6.start()

        @pl.when(y == 2)
        def _():
            to3_first.start()

    pl.when(core == 1)(forward)

    def squares(v):
        return jnp.sum(jnp.square(img_raw[v].astype(F32)), axis=0, keepdims=True)

    total = squares(w) + squares(w2)
    for n, copy in enumerate(b_copies):
        copy.wait_recv()
        j = (1, 3, 2)[n % 3]
        total = total + squares((base if n < 3 else base2) + near(NX - j))
    inorm = lax.rsqrt(total + EPSILON)
    for v in range(NW):
        scaled = (img_raw[v].astype(F32) * inorm).astype(BF16)
        low[core, v * MAIN : (v + 1) * MAIN, :] = scaled[:MAIN]
        low[core, NW * MAIN + v * TAIL : NW * MAIN + (v + 1) * TAIL, :] = scaled[MAIN:]
    share = remote(low.at[core], low.at[core], s_ss.at[0], s_rs.at[0], other)
    share.start()

    pl.when(core == 0)(forward)

    temper = jnp.exp(jnp.full((1, COLS), log_scale[0], F32))
    shift = bias[0]
    col = lax.broadcasted_iota(jnp.int32, (ROWS, COLS), 1)
    row = lax.broadcasted_iota(jnp.int32, (ROWS, COLS), 0) + w * ROWS
    gap = col - row

    home = {
        1: (jnp.where(last, -1, 1), jnp.where(last, 0, 1)),
        3: (jnp.where(first, 2, -1), jnp.where(first, 5, 3)),
        4: (jnp.where(last, -2, 1), jnp.where(last, 2, 4)),
        6: (-1, 6),
    }

    def back(d):
        to, slot = home[d]
        return remote(f_send.at[d], f_recv.at[slot], f_ss.at[d], f_rs.at[slot], along(to))

    def add_part(place, slot):
        remote(f_send.at[slot], f_recv.at[slot], f_ss.at[slot], f_rs.at[slot], other).wait_recv()
        keep[place] = keep[place] + f_recv[slot].astype(F32)

    def meet(ds):
        first = PLACE[ds[0]] * ROWS
        size = len(ds) * ROWS
        here = txt[first : first + size, :]
        grad = jnp.zeros((size, D), F32)
        for i in range(2):
            logits = jnp.dot(here, low[i], preferred_element_type=F32)
            parts = []
            dot = jnp.zeros((1, COLS), F32)
            for n, d in enumerate(ds):
                step = 2 * d + i - core
                met = jnp.logical_and(step >= 0, step < CYCLE).astype(F32)
                offset = offsets[jnp.clip(step, 0, CYCLE - 1)]
                own = logits[n * ROWS : (n + 1) * ROWS]
                positive = (((gap - offset) & (COLS - 1)) == 0).astype(F32)
                slope = (temper * (jax.nn.sigmoid(temper * own + shift) - positive)) * met
                slope = slope.astype(BF16)
                dot = dot + jnp.sum(slope.astype(F32) * own, axis=0, keepdims=True)
                slopes[i, (PLACE[d]) * ROWS : (PLACE[d] + 1) * ROWS, :] = slope
                parts.append(slope)
            dots[i] = dots[i] + jnp.broadcast_to(dot, dots.shape[1:])
            grad = grad + lax.dot_general(
                slopes[i, first : first + size, :], low[i], (((1,), (1,)), ((), ())), preferred_element_type=F32
            )
        for n, d in enumerate(ds):
            part = grad[n * ROWS : (n + 1) * ROWS]
            if d in (0, 2, 5):
                keep[PLACE[d]] = part
            else:
                f_send[d] = part.astype(BF16)

    share.wait_recv()
    meet((0, 2, 5))
    to1.wait_recv()
    to3.wait_recv()
    to4.wait_recv()

    @pl.when(core == 1)
    def _():
        to6.wait_recv()

    meet((1, 3, 4, 6))
    for d in (4, 3, 1):
        back(d).start()

    @pl.when(core == 1)
    def _():
        back(6).start()

    def image_part(i, store):
        third = D // 3
        dot = dots[i][:1]
        for t in range(3):
            part = lax.dot_general(
                txt[:, t * third : (t + 1) * third], slopes[i], (((0,), (0,)), ((), ())), preferred_element_type=F32
            )
            part = part - low[i, t * third : (t + 1) * third, :].astype(F32) * dot
            for u in range(3):
                v = 3 * t + u
                chunk = part[u * MAIN : (u + 1) * MAIN]
                if v < NW:
                    store(v, 0, MAIN, chunk)
                else:
                    for q in range(NW):
                        store(q, MAIN, FEAT, chunk[q * TAIL : (q + 1) * TAIL])

    def to_other(v, lo, hi, chunk):
        p_send[v, lo:hi, :] = chunk.astype(BF16)

    def to_own(v, lo, hi, chunk):
        p_own[v, lo:hi, :] = chunk

    image_part(1 - core, to_other)
    pair = remote(p_send, p_recv, s_ss.at[1], s_rs.at[1], other)
    pair.start()
    image_part(core, to_own)

    lane = lax.broadcasted_iota(jnp.int32, (8, MAIN), 1)

    def pieces(part, more, store):
        tail = part[:, NW * MAIN :]
        for v in range(NW):
            packed = more
            for q in range(4):
                shift = (32 * q - v * TAIL) % MAIN
                rest = tail[8 * q : 8 * q + 8]
                rest = pltpu.roll(rest, shift, 1) if shift else rest
                packed = jnp.where((lane >= 32 * q) & (lane < 32 * q + TAIL), rest, packed)
            rest = jnp.concatenate([packed, jnp.zeros((8, MAIN), F32)], axis=0)
            store(v, part[:, v * MAIN : (v + 1) * MAIN].astype(BF16), rest.astype(BF16))

    def to_row(v, main, rest):
        g_send[v, :ROWS, :] = main
        g_send[v, ROWS:, :] = rest

    g_copies = [
        remote(g_send.at[lax.rem(w + j, NW)], g_recv.at[w], g_ss.at[j], g_rs.at[j], across(j)) for j in range(1, NW)
    ]

    def send_own():
        scaled = unit[...]
        part = keep[PLACE[0]]
        part = part - scaled * jnp.sum(scaled * part, axis=1, keepdims=True)
        norm = tnorm[...]
        high = norm.astype(BF16).astype(F32)
        norms = jnp.zeros((8, MAIN), F32)
        for q in range(4):
            norms = jnp.where(lane == 32 * q + TAIL, high[8 * q : 8 * q + 8], norms)
            norms = jnp.where(lane == 32 * q + TAIL + 1, (norm - high)[8 * q : 8 * q + 8], norms)
        pieces(part, norms, to_row)
        for copy in g_copies:
            copy.start()
        g_recv[w] = g_send[w]

    pl.when(y != NY - 2)(send_own)

    pair.wait_recv()
    for v in range(NW):
        p_own[v] = p_own[v] + p_recv[v].astype(F32)
        e_send[v] = p_own[v].astype(BF16)
    e_copies = [
        remote(e_send.at[start + near(j)], e_recv.at[n + j], e_ss.at[n + j], e_rs.at[n + j], (dp, base + near(j)))
        for n, start in ((NX, base2), (0, base))
        for j in (1, 3, 2)
    ]
    for copy in e_copies:
        copy.start()

    h_copies = []
    for t, d in ((0, 5), (1, 2)):
        owner = lax.rem(chip - d + chips, chips) * 2 + core
        for j in range(NW):
            to = lax.rem(w + j, NW)
            h_copies.append(
                remote(h_send.at[t, to], h_recv.at[t, w], h_ss.at[t, j], h_rs.at[t, j], (owner, to))
            )

    def send_home(t, d, part):
        text = txt[rows_of(d), :].astype(F32)
        part = part - text * jnp.sum(text * part, axis=1, keepdims=True)

        def to_home(v, main, rest):
            h_send[t, v, :ROWS, :] = main
            h_send[t, v, ROWS:, :] = rest

        pieces(part, jnp.zeros((8, MAIN), F32), to_home)
        for copy in h_copies[t * NW : (t + 1) * NW]:
            copy.start()

    def text_sums():
        @pl.when(y != 0)
        def _():
            add_part(PLACE[5], 4)

        @pl.when(core == 1)
        def _():
            add_part(PLACE[5], 6)

        @pl.when(y == 2)
        def _():
            add_part(PLACE[5], 5)

        send_home(0, 5, keep[PLACE[5]])

        @pl.when(y != 0)
        def _():
            add_part(PLACE[2], 1)

        @pl.when(y != NY - 1)
        def _():
            add_part(PLACE[2], 3)

        @pl.when(y == NY - 3)
        def _():
            add_part(PLACE[2], 2)

        send_home(1, 2, keep[PLACE[2]])

    z_back = remote(z_send, z_recv, z_ss.at[0], z_rs.at[0], partner)

    def image_sums():
        grad = p_own[w2]
        for j, copy in zip((1, 3, 2), e_copies[:3]):
            copy.wait_recv()
            grad = grad + e_recv[NX + j].astype(F32)
        z_send[...] = grad.astype(BF16)
        z_back.start()

    pl.when(core == 1)(image_sums)
    text_sums()
    pl.when(core == 0)(image_sums)

    @pl.when(y == NY - 2)
    def _():
        add_part(PLACE[0], 0)
        send_own()

    grad = p_own[w]
    for j, copy in zip((1, 3, 2), e_copies[3:]):
        copy.wait_recv()
        grad = grad + e_recv[j].astype(F32)
    z_back.wait_recv()
    grad = grad + z_recv[...].astype(F32)
    out[:FEAT] = grad * inorm
    for copy in g_copies + h_copies:
        copy.wait_recv()
    whole = g_recv[...].astype(F32) + h_recv[0].astype(F32) + h_recv[1].astype(F32)
    txt_wide[:, :MAIN] = whole[:, :ROWS].reshape(COLS, MAIN)
    packed = whole[:, ROWS : ROWS + 8].reshape(NW * 8, MAIN)
    for q in range(4):
        rest = pltpu.roll(packed, MAIN - 32 * q, 1) if q else packed
        for v in range(NW):
            at = v * ROWS + 8 * q
            txt_wide[at : at + 8, MAIN:] = rest[8 * v : 8 * v + 8]
    whole = txt_wide[...].T
    out[FEAT:] = whole[:FEAT] * (whole[FEAT : FEAT + 1] + whole[FEAT + 1 : FEAT + 2])

    for copy in a_copies + b_copies + e_copies + g_copies + h_copies:
        copy.wait_send()
    for copy in (to2, to5, share, pair, z_copy, z_back):
        copy.wait_send()
    for d in (1, 3, 4):
        back(d).wait_send()

    for here, copy in (
        (y != 0, to1),
        (y != NY - 1, to3),
        (y != 0, to4),
        (y == NY - 2, to1_last),
        (y == NY - 3, to4_last),
        (y == 2, to3_first),
    ):
        pl.when(here)(copy.wait_send)

    @pl.when(core == 1)
    def _():
        to6.wait_send()
        back(6).wait_send()


def solution(mesh):
    chips = mesh.shape["dp"] // 2
    slots = len(ORDER)
    dma = pltpu.SemaphoreType.DMA

    def body(image_emb, text_emb, pair_offsets, log_scale, bias):
        shape = jax.ShapeDtypeStruct((2 * FEAT, COLS), F32)
        smem = pl.BlockSpec(memory_space=pltpu.SMEM)
        hbm = pl.BlockSpec(memory_space=pltpu.HBM)
        grads = pl.pallas_call(
            functools.partial(kernel, chips),
            out_shape=shape,
            in_specs=[hbm, hbm, hbm, smem, smem],
            out_specs=pl.BlockSpec(memory_space=pltpu.VMEM),
            scratch_shapes=[
                pltpu.SMEM((CYCLE,), jnp.int32),
                pltpu.VMEM((NW, FEAT, COLS), BF16),
                pltpu.VMEM((FEAT, COLS), BF16),
                pltpu.VMEM((COLS, COLS), F32),
                pltpu.VMEM((NW, ROWS, COLS), BF16),
                pltpu.VMEM((NW, ROWS, COLS), BF16),
                pltpu.VMEM((2, D, COLS), BF16),
                pltpu.VMEM((slots * ROWS, D), BF16),
                pltpu.VMEM((ROWS, D), F32),
                pltpu.VMEM((ROWS, MAIN), F32),
                pltpu.VMEM((2, slots * ROWS, COLS), BF16),
                pltpu.VMEM((2, 8, COLS), F32),
                pltpu.VMEM((slots, ROWS, D), BF16),
                pltpu.VMEM((slots, ROWS, D), BF16),
                pltpu.VMEM((NW, FEAT, COLS), BF16),
                pltpu.VMEM((NW, FEAT, COLS), BF16),
                pltpu.VMEM((NW, FEAT, COLS), F32),
                pltpu.VMEM((NW, FEAT, COLS), BF16),
                pltpu.VMEM((NW, FEAT, COLS), BF16),
                pltpu.VMEM((FEAT, COLS), BF16),
                pltpu.VMEM((FEAT, COLS), BF16),
                pltpu.VMEM((3, ROWS, D), F32),
                pltpu.VMEM((NW, ROWS + 16, MAIN), BF16),
                pltpu.VMEM((NW, ROWS + 16, MAIN), BF16),
                pltpu.VMEM((2, NW, ROWS + 16, MAIN), BF16),
                pltpu.VMEM((2, NW, ROWS + 16, MAIN), BF16),
                dma((3,)),
                dma((NW,)),
                dma((NW,)),
                dma((NW,)),
                dma((NW,)),
                dma((slots,)),
                dma((slots,)),
                dma((slots,)),
                dma((slots,)),
                dma((NW,)),
                dma((NW,)),
                dma((NW,)),
                dma((NW,)),
                dma((2,)),
                dma((2,)),
                dma((1,)),
                dma((1,)),
                dma((2, NW)),
                dma((2, NW)),
            ],
            compiler_params=pltpu.CompilerParams(
                collective_id=0, has_side_effects=True, vmem_limit_bytes=40 * 1024 * 1024
            ),
        )(
            *(pltpu.with_memory_space_constraint(v, pltpu.HBM) for v in (image_emb, text_emb, pair_offsets)), log_scale, bias
        )
        return grads[:FEAT], grads[FEAT:]

    placed = (P("width", "dp"), P("width", "dp"), P(), P(), P())
    return jax.shard_map(
        body,
        mesh=mesh,
        in_specs=placed,
        out_specs=(P("width", "dp"), P("width", "dp")),
        check_vma=False,
    )
```

```python
import functools

import jax
import jax.numpy as jnp
from jax import lax
from jax.experimental import pallas as pl
from jax.experimental.pallas import tpu as pltpu
from jax.sharding import PartitionSpec as P

MESH = pl.DeviceIdType.MESH
F32 = jnp.float32
BF16 = jnp.bfloat16
EPSILON = 1e-06
CYCLE = 12
NW = 8
NX = 4
FEAT = 144
MAIN = 128
TAIL = FEAT - MAIN
D = NW * FEAT
COLS = 256
ROWS = COLS // NW
NY = 8
REACH = 6
ORDER = (0, 2, 5, 1, 3, 4, 6)
PLACE = {d: i for i, d in enumerate(ORDER)}


def rows_of(d):
    return pl.ds(PLACE[d] * ROWS, ROWS)


def kernel(
    chips,
    img_hbm,
    txt_hbm,
    offsets_hbm,
    log_scale,
    bias,
    out,
    offsets,
    img_raw,
    txt_in,
    txt_wide,
    a_send,
    a_recv,
    low,
    txt,
    unit,
    tnorm,
    slopes,
    dots,
    f_send,
    f_recv,
    p_send,
    p_recv,
    p_own,
    e_send,
    e_recv,
    z_send,
    z_recv,
    keep,
    g_send,
    g_recv,
    h_send,
    h_recv,
    local_sem,
    a_ss,
    a_rs,
    b_ss,
    b_rs,
    c_ss,
    c_rs,
    f_ss,
    f_rs,
    e_ss,
    e_rs,
    g_ss,
    g_rs,
    s_ss,
    s_rs,
    z_ss,
    z_rs,
    h_ss,
    h_rs,
):
    dp = lax.axis_index("dp")
    w = lax.axis_index("width")
    chip = lax.div(dp, 2)
    core = lax.rem(dp, 2)

    def along(d):
        return (lax.rem(chip + d + chips, chips) * 2 + core, w)

    def across(j):
        return (dp, lax.rem(w + j, NW))

    other = (dp + 1 - 2 * core, w)
    y = lax.rem(chip, NY)
    first, last = y == 0, y == NY - 1
    x = lax.rem(w, NX)
    base = w - x
    base2 = NX - base
    w2 = base2 + x
    partner = (dp, w2)

    def near(j):
        return lax.rem(x + j, NX)

    def remote(src, dst, ss, rs, to):
        return pltpu.make_async_remote_copy(
            src_ref=src, dst_ref=dst, send_sem=ss, recv_sem=rs, device_id=to, device_id_type=MESH
        )

    barrier = pltpu.get_barrier_semaphore()

    def arrive(peer):
        pl.semaphore_signal(barrier, inc=1, device_id=peer, device_id_type=MESH)

    for d in (-5, -2, -1):
        arrive(along(d))
    for j in range(1, NW):
        arrive(across(j))
    arrive(other)

    @pl.when(y != NY - 1)
    def _():
        arrive(along(1))

    get_txt = pltpu.make_async_copy(txt_hbm, txt_in, local_sem.at[0])
    get_img = pltpu.make_async_copy(img_hbm, img_raw.at[w], local_sem.at[1])
    get_txt.start()
    get_img.start()
    get_offsets = pltpu.make_async_copy(offsets_hbm, offsets, local_sem.at[2])
    get_offsets.start()

    @pl.when(core == 0)
    def _():
        txt[rows_of(REACH), :] = jnp.zeros((ROWS, D), BF16)

    txt_wide[FEAT:, :] = jnp.zeros((COLS - FEAT, COLS), F32)
    dots[...] = jnp.zeros(dots.shape, F32)
    get_txt.wait()
    txt_wide[:FEAT, :] = txt_in[...].astype(F32)
    a_send[...] = txt_wide[...].T.astype(BF16).reshape(NW, ROWS, COLS)
    get_img.wait()
    get_offsets.wait()
    pl.semaphore_wait(barrier, jnp.where(first, NW + 3, NW + 4))

    z_copy = remote(img_raw.at[w], img_raw.at[w], b_ss.at[0], b_rs.at[0], partner)
    z_copy.start()
    a_copies = []
    for j in range(1, NW):
        copy = remote(a_send.at[lax.rem(w + j, NW)], a_recv.at[w], a_ss.at[j], a_rs.at[j], across(j))
        copy.start()
        a_copies.append(copy)
    a_recv[w] = a_send[w]
    for copy in a_copies:
        copy.wait_recv()
    b_copies = []
    for j in (1, 3, 2):
        copy = remote(img_raw.at[w], img_raw.at[w], b_ss.at[j], b_rs.at[j], (dp, base + near(j)))
        copy.start()
        b_copies.append(copy)

    tail = jnp.zeros((ROWS, MAIN), F32)
    for v in range(NW):
        piece = a_recv[v].astype(F32)
        unit[:, v * MAIN : (v + 1) * MAIN] = piece[:, :MAIN]
        rest = piece[:, MAIN:]
        tail = tail + (pltpu.roll(rest, v * TAIL, 1) if v else rest)
    unit[:, NW * MAIN :] = tail
    raw = unit[...]
    norm = lax.rsqrt(jnp.sum(raw * raw, axis=1, keepdims=True) + EPSILON)
    scaled = raw * norm
    unit[...] = scaled
    tnorm[...] = jnp.broadcast_to(norm, tnorm.shape)
    txt[rows_of(0), :] = scaled.astype(BF16)

    def pass_text(src, dst, to, sem=None):
        sem = dst if sem is None else sem
        return remote(txt.at[rows_of(src)], txt.at[rows_of(dst)], c_ss.at[sem], c_rs.at[dst], to)

    to2 = pass_text(0, 2, along(2))
    to5 = pass_text(0, 5, along(5))
    to5.start()
    to2.start()
    to1_last = pass_text(0, 1, along(1), 0)
    to4_last = pass_text(2, 4, along(2), 0)

    @pl.when(y == NY - 2)
    def _():
        to1_last.start()


    z_copy.wait_recv()
    for j in (1, 3, 2):
        copy = remote(img_raw.at[w2], img_raw.at[w2], b_ss.at[NX + j], b_rs.at[NX + j], (dp, base + near(j)))
        copy.start()
        b_copies.append(copy)

    to1 = pass_text(2, 1, along(-1))
    to3 = pass_text(2, 3, along(1))
    to4 = pass_text(5, 4, along(-1))
    to6 = pass_text(5, 6, along(1))

    def forward():
        to2.wait_recv()

        @pl.when(y != 0)
        def _():
            to1.start()

        to3.start()

        @pl.when(y == NY - 3)
        def _():
            to4_last.start()

        to5.wait_recv()

        @pl.when(y != 0)
        def _():
            to4.start()

        @pl.when(core == 1)
        def _():
            to6.start()

    pl.when(core == 1)(forward)

    def squares(v):
        return jnp.sum(jnp.square(img_raw[v].astype(F32)), axis=0, keepdims=True)

    total = squares(w) + squares(w2)
    for n, copy in enumerate(b_copies):
        copy.wait_recv()
        j = (1, 3, 2)[n % 3]
        total = total + squares((base if n < 3 else base2) + near(NX - j))
    inorm = lax.rsqrt(total + EPSILON)
    for v in range(NW):
        scaled = (img_raw[v].astype(F32) * inorm).astype(BF16)
        low[core, v * MAIN : (v + 1) * MAIN, :] = scaled[:MAIN]
        low[core, NW * MAIN + v * TAIL : NW * MAIN + (v + 1) * TAIL, :] = scaled[MAIN:]
    share = remote(low.at[core], low.at[core], s_ss.at[0], s_rs.at[0], other)
    share.start()

    pl.when(core == 0)(forward)

    temper = jnp.exp(jnp.full((1, COLS), log_scale[0], F32))
    shift = bias[0]
    col = lax.broadcasted_iota(jnp.int32, (ROWS, COLS), 1)
    row = lax.broadcasted_iota(jnp.int32, (ROWS, COLS), 0) + w * ROWS
    gap = col - row

    home = {
        1: (jnp.where(last, -1, 1), jnp.where(last, 0, 1)),
        3: (jnp.where(first, 2, -1), jnp.where(first, 5, 3)),
        4: (jnp.where(last, -2, 1), jnp.where(last, 2, 4)),
        6: (-1, 6),
    }

    def back(d):
        to, slot = home[d]
        return remote(f_send.at[d], f_recv.at[slot], f_ss.at[d], f_rs.at[slot], along(to))

    def add_part(place, slot):
        remote(f_send.at[slot], f_recv.at[slot], f_ss.at[slot], f_rs.at[slot], other).wait_recv()
        keep[place] = keep[place] + f_recv[slot].astype(F32)

    def meet(ds):
        first = PLACE[ds[0]] * ROWS
        size = len(ds) * ROWS
        here = txt[first : first + size, :]
        grad = jnp.zeros((size, D), F32)
        for i in range(2):
            logits = jnp.dot(here, low[i], preferred_element_type=F32)
            parts = []
            dot = jnp.zeros((1, COLS), F32)
            for n, d in enumerate(ds):
                step = 2 * d + i - core
                met = jnp.logical_and(step >= 0, step < CYCLE).astype(F32)
                offset = offsets[jnp.clip(step, 0, CYCLE - 1)]
                own = logits[n * ROWS : (n + 1) * ROWS]
                positive = (((gap - offset) & (COLS - 1)) == 0).astype(F32)
                slope = (temper * (jax.nn.sigmoid(temper * own + shift) - positive)) * met
                slope = slope.astype(BF16)
                dot = dot + jnp.sum(slope.astype(F32) * own, axis=0, keepdims=True)
                slopes[i, (PLACE[d]) * ROWS : (PLACE[d] + 1) * ROWS, :] = slope
                parts.append(slope)
            dots[i] = dots[i] + jnp.broadcast_to(dot, dots.shape[1:])
            grad = grad + lax.dot_general(
                slopes[i, first : first + size, :], low[i], (((1,), (1,)), ((), ())), preferred_element_type=F32
            )
        for n, d in enumerate(ds):
            part = grad[n * ROWS : (n + 1) * ROWS]
            if d in (0, 2, 5):
                keep[PLACE[d]] = part
            else:
                f_send[d] = part.astype(BF16)

    share.wait_recv()
    meet((0, 2, 5))
    to1.wait_recv()
    to3.wait_recv()
    to4.wait_recv()

    @pl.when(core == 1)
    def _():
        to6.wait_recv()

    meet((1, 3, 4, 6))
    for d in (4, 3, 1):
        back(d).start()

    @pl.when(core == 1)
    def _():
        back(6).start()

    def image_part(i, store):
        third = D // 3
        dot = dots[i][:1]
        for t in range(3):
            part = lax.dot_general(
                txt[:, t * third : (t + 1) * third], slopes[i], (((0,), (0,)), ((), ())), preferred_element_type=F32
            )
            part = part - low[i, t * third : (t + 1) * third, :].astype(F32) * dot
            for u in range(3):
                v = 3 * t + u
                chunk = part[u * MAIN : (u + 1) * MAIN]
                if v < NW:
                    store(v, 0, MAIN, chunk)
                else:
                    for q in range(NW):
                        store(q, MAIN, FEAT, chunk[q * TAIL : (q + 1) * TAIL])

    def to_other(v, lo, hi, chunk):
        p_send[v, lo:hi, :] = chunk.astype(BF16)

    def to_own(v, lo, hi, chunk):
        p_own[v, lo:hi, :] = chunk

    image_part(1 - core, to_other)
    pair = remote(p_send, p_recv, s_ss.at[1], s_rs.at[1], other)
    pair.start()
    image_part(core, to_own)

    lane = lax.broadcasted_iota(jnp.int32, (8, MAIN), 1)

    def pieces(part, more, store):
        tail = part[:, NW * MAIN :]
        for v in range(NW):
            packed = more
            for q in range(4):
                shift = (32 * q - v * TAIL) % MAIN
                rest = tail[8 * q : 8 * q + 8]
                rest = pltpu.roll(rest, shift, 1) if shift else rest
                packed = jnp.where((lane >= 32 * q) & (lane < 32 * q + TAIL), rest, packed)
            rest = jnp.concatenate([packed, jnp.zeros((8, MAIN), F32)], axis=0)
            store(v, part[:, v * MAIN : (v + 1) * MAIN].astype(BF16), rest.astype(BF16))

    def to_row(v, main, rest):
        g_send[v, :ROWS, :] = main
        g_send[v, ROWS:, :] = rest

    g_copies = [
        remote(g_send.at[lax.rem(w + j, NW)], g_recv.at[w], g_ss.at[j], g_rs.at[j], across(j)) for j in range(1, NW)
    ]

    def send_own():
        scaled = unit[...]
        part = keep[PLACE[0]]
        part = part - scaled * jnp.sum(scaled * part, axis=1, keepdims=True)
        norm = tnorm[...]
        high = norm.astype(BF16).astype(F32)
        norms = jnp.zeros((8, MAIN), F32)
        for q in range(4):
            norms = jnp.where(lane == 32 * q + TAIL, high[8 * q : 8 * q + 8], norms)
            norms = jnp.where(lane == 32 * q + TAIL + 1, (norm - high)[8 * q : 8 * q + 8], norms)
        pieces(part, norms, to_row)
        for copy in g_copies:
            copy.start()
        g_recv[w] = g_send[w]

    pl.when(y != NY - 2)(send_own)

    pair.wait_recv()
    for v in range(NW):
        p_own[v] = p_own[v] + p_recv[v].astype(F32)
        e_send[v] = p_own[v].astype(BF16)
    e_copies = [
        remote(e_send.at[start + near(j)], e_recv.at[n + j], e_ss.at[n + j], e_rs.at[n + j], (dp, base + near(j)))
        for n, start in ((NX, base2), (0, base))
        for j in (1, 3, 2)
    ]
    for copy in e_copies:
        copy.start()

    h_copies = []
    for t, d in ((0, 5), (1, 2)):
        owner = lax.rem(chip - d + chips, chips) * 2 + core
        for j in range(NW):
            to = lax.rem(w + j, NW)
            h_copies.append(
                remote(h_send.at[t, to], h_recv.at[t, w], h_ss.at[t, j], h_rs.at[t, j], (owner, to))
            )

    def send_home(t, d, part):
        text = txt[rows_of(d), :].astype(F32)
        part = part - text * jnp.sum(text * part, axis=1, keepdims=True)

        def to_home(v, main, rest):
            h_send[t, v, :ROWS, :] = main
            h_send[t, v, ROWS:, :] = rest

        pieces(part, jnp.zeros((8, MAIN), F32), to_home)
        for copy in h_copies[t * NW : (t + 1) * NW]:
            copy.start()

    def text_sums():
        @pl.when(y != 0)
        def _():
            add_part(PLACE[5], 4)

        @pl.when(core == 1)
        def _():
            add_part(PLACE[5], 6)

        @pl.when(y == 2)
        def _():
            add_part(PLACE[5], 5)

        send_home(0, 5, keep[PLACE[5]])

        @pl.when(y != 0)
        def _():
            add_part(PLACE[2], 1)

        @pl.when(y != NY - 1)
        def _():
            add_part(PLACE[2], 3)

        @pl.when(y == NY - 3)
        def _():
            add_part(PLACE[2], 2)

        send_home(1, 2, keep[PLACE[2]])

    z_back = remote(z_send, z_recv, z_ss.at[0], z_rs.at[0], partner)

    def image_sums():
        grad = p_own[w2]
        for j, copy in zip((1, 3, 2), e_copies[:3]):
            copy.wait_recv()
            grad = grad + e_recv[NX + j].astype(F32)
        z_send[...] = grad.astype(BF16)
        z_back.start()

    pl.when(core == 1)(image_sums)
    text_sums()
    pl.when(core == 0)(image_sums)

    @pl.when(y == NY - 2)
    def _():
        add_part(PLACE[0], 0)
        send_own()

    grad = p_own[w]
    for j, copy in zip((1, 3, 2), e_copies[3:]):
        copy.wait_recv()
        grad = grad + e_recv[j].astype(F32)
    z_back.wait_recv()
    grad = grad + z_recv[...].astype(F32)
    out[:FEAT] = grad * inorm
    for copy in g_copies + h_copies:
        copy.wait_recv()
    whole = g_recv[...].astype(F32) + h_recv[0].astype(F32) + h_recv[1].astype(F32)
    txt_wide[:, :MAIN] = whole[:, :ROWS].reshape(COLS, MAIN)
    packed = whole[:, ROWS : ROWS + 8].reshape(NW * 8, MAIN)
    for q in range(4):
        rest = pltpu.roll(packed, MAIN - 32 * q, 1) if q else packed
        for v in range(NW):
            at = v * ROWS + 8 * q
            txt_wide[at : at + 8, MAIN:] = rest[8 * v : 8 * v + 8]
    whole = txt_wide[...].T
    out[FEAT:] = whole[:FEAT] * (whole[FEAT : FEAT + 1] + whole[FEAT + 1 : FEAT + 2])

    for copy in a_copies + b_copies + e_copies + g_copies + h_copies:
        copy.wait_send()
    for copy in (to2, to3, to5, share, pair, z_copy, z_back):
        copy.wait_send()
    for d in (1, 3, 4):
        back(d).wait_send()

    for here, copy in (
        (y != 0, to1),
        (y != 0, to4),
        (y == NY - 2, to1_last),
        (y == NY - 3, to4_last),
    ):
        pl.when(here)(copy.wait_send)

    @pl.when(core == 1)
    def _():
        to6.wait_send()
        back(6).wait_send()


def solution(mesh):
    chips = mesh.shape["dp"] // 2
    slots = len(ORDER)
    dma = pltpu.SemaphoreType.DMA

    def body(image_emb, text_emb, pair_offsets, log_scale, bias):
        shape = jax.ShapeDtypeStruct((2 * FEAT, COLS), F32)
        smem = pl.BlockSpec(memory_space=pltpu.SMEM)
        hbm = pl.BlockSpec(memory_space=pltpu.HBM)
        grads = pl.pallas_call(
            functools.partial(kernel, chips),
            out_shape=shape,
            in_specs=[hbm, hbm, hbm, smem, smem],
            out_specs=pl.BlockSpec(memory_space=pltpu.VMEM),
            scratch_shapes=[
                pltpu.SMEM((CYCLE,), jnp.int32),
                pltpu.VMEM((NW, FEAT, COLS), BF16),
                pltpu.VMEM((FEAT, COLS), BF16),
                pltpu.VMEM((COLS, COLS), F32),
                pltpu.VMEM((NW, ROWS, COLS), BF16),
                pltpu.VMEM((NW, ROWS, COLS), BF16),
                pltpu.VMEM((2, D, COLS), BF16),
                pltpu.VMEM((slots * ROWS, D), BF16),
                pltpu.VMEM((ROWS, D), F32),
                pltpu.VMEM((ROWS, MAIN), F32),
                pltpu.VMEM((2, slots * ROWS, COLS), BF16),
                pltpu.VMEM((2, 8, COLS), F32),
                pltpu.VMEM((slots, ROWS, D), BF16),
                pltpu.VMEM((slots, ROWS, D), BF16),
                pltpu.VMEM((NW, FEAT, COLS), BF16),
                pltpu.VMEM((NW, FEAT, COLS), BF16),
                pltpu.VMEM((NW, FEAT, COLS), F32),
                pltpu.VMEM((NW, FEAT, COLS), BF16),
                pltpu.VMEM((NW, FEAT, COLS), BF16),
                pltpu.VMEM((FEAT, COLS), BF16),
                pltpu.VMEM((FEAT, COLS), BF16),
                pltpu.VMEM((3, ROWS, D), F32),
                pltpu.VMEM((NW, ROWS + 16, MAIN), BF16),
                pltpu.VMEM((NW, ROWS + 16, MAIN), BF16),
                pltpu.VMEM((2, NW, ROWS + 16, MAIN), BF16),
                pltpu.VMEM((2, NW, ROWS + 16, MAIN), BF16),
                dma((3,)),
                dma((NW,)),
                dma((NW,)),
                dma((NW,)),
                dma((NW,)),
                dma((slots,)),
                dma((slots,)),
                dma((slots,)),
                dma((slots,)),
                dma((NW,)),
                dma((NW,)),
                dma((NW,)),
                dma((NW,)),
                dma((2,)),
                dma((2,)),
                dma((1,)),
                dma((1,)),
                dma((2, NW)),
                dma((2, NW)),
            ],
            compiler_params=pltpu.CompilerParams(
                collective_id=0, has_side_effects=True, vmem_limit_bytes=40 * 1024 * 1024
            ),
        )(
            *(pltpu.with_memory_space_constraint(v, pltpu.HBM) for v in (image_emb, text_emb, pair_offsets)), log_scale, bias
        )
        return grads[:FEAT], grads[FEAT:]

    placed = (P("width", "dp"), P("width", "dp"), P(), P(), P())
    return jax.shard_map(
        body,
        mesh=mesh,
        in_specs=placed,
        out_specs=(P("width", "dp"), P("width", "dp")),
        check_vma=False,
    )
```

```python
import functools

import jax
import jax.numpy as jnp
from jax import lax
from jax.experimental import pallas as pl
from jax.experimental.pallas import tpu as pltpu
from jax.sharding import PartitionSpec as P

MESH = pl.DeviceIdType.MESH
F32 = jnp.float32
BF16 = jnp.bfloat16
EPSILON = 1e-06
CYCLE = 12
NW = 8
NX = 4
FEAT = 144
MAIN = 128
TAIL = FEAT - MAIN
D = NW * FEAT
COLS = 256
ROWS = COLS // NW
NY = 8
REACH = 6
ORDER = (0, 2, 5, 1, 3, 4, 6)
PLACE = {d: i for i, d in enumerate(ORDER)}


def rows_of(d):
    return pl.ds(PLACE[d] * ROWS, ROWS)


def kernel(
    chips,
    img_hbm,
    txt_hbm,
    offsets_hbm,
    log_scale,
    bias,
    out,
    offsets,
    img_raw,
    txt_in,
    txt_wide,
    a_send,
    a_recv,
    low,
    txt,
    unit,
    tnorm,
    slopes,
    dots,
    f_send,
    f_recv,
    p_send,
    p_recv,
    p_own,
    e_send,
    e_recv,
    z_send,
    z_recv,
    keep,
    g_send,
    g_recv,
    h_send,
    h_recv,
    local_sem,
    a_ss,
    a_rs,
    b_ss,
    b_rs,
    c_ss,
    c_rs,
    f_ss,
    f_rs,
    e_ss,
    e_rs,
    g_ss,
    g_rs,
    s_ss,
    s_rs,
    z_ss,
    z_rs,
    h_ss,
    h_rs,
):
    dp = lax.axis_index("dp")
    w = lax.axis_index("width")
    chip = lax.div(dp, 2)
    core = lax.rem(dp, 2)

    def along(d):
        return (lax.rem(chip + d + chips, chips) * 2 + core, w)

    def across(j):
        return (dp, lax.rem(w + j, NW))

    other = (dp + 1 - 2 * core, w)
    y = lax.rem(chip, NY)
    first, last = y == 0, y == NY - 1
    x = lax.rem(w, NX)
    base = w - x
    base2 = NX - base
    w2 = base2 + x
    partner = (dp, w2)

    def near(j):
        return lax.rem(x + j, NX)

    def remote(src, dst, ss, rs, to):
        return pltpu.make_async_remote_copy(
            src_ref=src, dst_ref=dst, send_sem=ss, recv_sem=rs, device_id=to, device_id_type=MESH
        )

    get_txt = pltpu.make_async_copy(txt_hbm, txt_in, local_sem.at[0])
    get_img = pltpu.make_async_copy(img_hbm, img_raw.at[w], local_sem.at[1])
    get_txt.start()
    get_img.start()

    barrier = pltpu.get_barrier_semaphore()

    def arrive(peer):
        pl.semaphore_signal(barrier, inc=1, device_id=peer, device_id_type=MESH)

    for d in (-5, -2, -1):
        arrive(along(d))
    for j in range(1, NW):
        arrive(across(j))
    arrive(other)

    @pl.when(y != NY - 1)
    def _():
        arrive(along(1))

    get_offsets = pltpu.make_async_copy(offsets_hbm, offsets, local_sem.at[2])
    get_offsets.start()

    @pl.when(core == 0)
    def _():
        txt[rows_of(REACH), :] = jnp.zeros((ROWS, D), BF16)

    txt_wide[FEAT:, :] = jnp.zeros((COLS - FEAT, COLS), F32)
    dots[...] = jnp.zeros(dots.shape, F32)
    get_txt.wait()
    txt_wide[:FEAT, :] = txt_in[...].astype(F32)
    a_send[...] = txt_wide[...].T.astype(BF16).reshape(NW, ROWS, COLS)
    get_img.wait()
    get_offsets.wait()
    pl.semaphore_wait(barrier, jnp.where(first, NW + 3, NW + 4))

    z_copy = remote(img_raw.at[w], img_raw.at[w], b_ss.at[0], b_rs.at[0], partner)
    z_copy.start()
    a_copies = []
    for j in range(1, NW):
        copy = remote(a_send.at[lax.rem(w + j, NW)], a_recv.at[w], a_ss.at[j], a_rs.at[j], across(j))
        copy.start()
        a_copies.append(copy)
    a_recv[w] = a_send[w]
    for copy in a_copies:
        copy.wait_recv()
    b_copies = []
    for j in (1, 3, 2):
        copy = remote(img_raw.at[w], img_raw.at[w], b_ss.at[j], b_rs.at[j], (dp, base + near(j)))
        copy.start()
        b_copies.append(copy)

    tail = jnp.zeros((ROWS, MAIN), F32)
    for v in range(NW):
        piece = a_recv[v].astype(F32)
        unit[:, v * MAIN : (v + 1) * MAIN] = piece[:, :MAIN]
        rest = piece[:, MAIN:]
        tail = tail + (pltpu.roll(rest, v * TAIL, 1) if v else rest)
    unit[:, NW * MAIN :] = tail
    raw = unit[...]
    norm = lax.rsqrt(jnp.sum(raw * raw, axis=1, keepdims=True) + EPSILON)
    scaled = raw * norm
    unit[...] = scaled
    tnorm[...] = jnp.broadcast_to(norm, tnorm.shape)
    txt[rows_of(0), :] = scaled.astype(BF16)

    def pass_text(src, dst, to, sem=None):
        sem = dst if sem is None else sem
        return remote(txt.at[rows_of(src)], txt.at[rows_of(dst)], c_ss.at[sem], c_rs.at[dst], to)

    to2 = pass_text(0, 2, along(2))
    to5 = pass_text(0, 5, along(5))
    to5.start()
    to2.start()
    to1_last = pass_text(0, 1, along(1), 0)
    to4_last = pass_text(2, 4, along(2), 0)

    @pl.when(y == NY - 2)
    def _():
        to1_last.start()


    z_copy.wait_recv()
    for j in (1, 3, 2):
        copy = remote(img_raw.at[w2], img_raw.at[w2], b_ss.at[NX + j], b_rs.at[NX + j], (dp, base + near(j)))
        copy.start()
        b_copies.append(copy)

    to1 = pass_text(2, 1, along(-1))
    to3 = pass_text(2, 3, along(1))
    to4 = pass_text(5, 4, along(-1))
    to6 = pass_text(5, 6, along(1))

    def forward():
        to2.wait_recv()

        @pl.when(y != 0)
        def _():
            to1.start()

        to3.start()

        @pl.when(y == NY - 3)
        def _():
            to4_last.start()

        to5.wait_recv()

        @pl.when(y != 0)
        def _():
            to4.start()

        @pl.when(core == 1)
        def _():
            to6.start()

    pl.when(core == 1)(forward)

    def squares(v):
        return jnp.sum(jnp.square(img_raw[v].astype(F32)), axis=0, keepdims=True)

    total = squares(w) + squares(w2)
    for n, copy in enumerate(b_copies):
        copy.wait_recv()
        j = (1, 3, 2)[n % 3]
        total = total + squares((base if n < 3 else base2) + near(NX - j))
    inorm = lax.rsqrt(total + EPSILON)
    for v in range(NW):
        scaled = (img_raw[v].astype(F32) * inorm).astype(BF16)
        low[core, v * MAIN : (v + 1) * MAIN, :] = scaled[:MAIN]
        low[core, NW * MAIN + v * TAIL : NW * MAIN + (v + 1) * TAIL, :] = scaled[MAIN:]
    share = remote(low.at[core], low.at[core], s_ss.at[0], s_rs.at[0], other)
    share.start()

    pl.when(core == 0)(forward)

    temper = jnp.exp(jnp.full((1, COLS), log_scale[0], F32))
    shift = bias[0]
    col = lax.broadcasted_iota(jnp.int32, (ROWS, COLS), 1)
    row = lax.broadcasted_iota(jnp.int32, (ROWS, COLS), 0) + w * ROWS
    gap = col - row

    home = {
        1: (jnp.where(last, -1, 1), jnp.where(last, 0, 1)),
        3: (jnp.where(first, 2, -1), jnp.where(first, 5, 3)),
        4: (jnp.where(last, -2, 1), jnp.where(last, 2, 4)),
        6: (-1, 6),
    }

    def back(d):
        to, slot = home[d]
        return remote(f_send.at[d], f_recv.at[slot], f_ss.at[d], f_rs.at[slot], along(to))

    def add_part(place, slot):
        remote(f_send.at[slot], f_recv.at[slot], f_ss.at[slot], f_rs.at[slot], other).wait_recv()
        keep[place] = keep[place] + f_recv[slot].astype(F32)

    def meet(ds):
        first = PLACE[ds[0]] * ROWS
        size = len(ds) * ROWS
        here = txt[first : first + size, :]
        grad = jnp.zeros((size, D), F32)
        for i in range(2):
            logits = jnp.dot(here, low[i], preferred_element_type=F32)
            parts = []
            dot = jnp.zeros((1, COLS), F32)
            for n, d in enumerate(ds):
                step = 2 * d + i - core
                met = jnp.logical_and(step >= 0, step < CYCLE).astype(F32)
                offset = offsets[jnp.clip(step, 0, CYCLE - 1)]
                own = logits[n * ROWS : (n + 1) * ROWS]
                positive = (((gap - offset) & (COLS - 1)) == 0).astype(F32)
                slope = (temper * (jax.nn.sigmoid(temper * own + shift) - positive)) * met
                slope = slope.astype(BF16)
                dot = dot + jnp.sum(slope.astype(F32) * own, axis=0, keepdims=True)
                slopes[i, (PLACE[d]) * ROWS : (PLACE[d] + 1) * ROWS, :] = slope
                parts.append(slope)
            dots[i] = dots[i] + jnp.broadcast_to(dot, dots.shape[1:])
            grad = grad + lax.dot_general(
                slopes[i, first : first + size, :], low[i], (((1,), (1,)), ((), ())), preferred_element_type=F32
            )
        for n, d in enumerate(ds):
            part = grad[n * ROWS : (n + 1) * ROWS]
            if d in (0, 2, 5):
                keep[PLACE[d]] = part
            else:
                f_send[d] = part.astype(BF16)

    share.wait_recv()
    meet((0, 2, 5))
    to1.wait_recv()
    to3.wait_recv()
    to4.wait_recv()

    @pl.when(core == 1)
    def _():
        to6.wait_recv()

    meet((1, 3, 4, 6))
    for d in (4, 3, 1):
        back(d).start()

    @pl.when(core == 1)
    def _():
        back(6).start()

    def image_part(i, store):
        third = D // 3
        dot = dots[i][:1]
        for t in range(3):
            part = lax.dot_general(
                txt[:, t * third : (t + 1) * third], slopes[i], (((0,), (0,)), ((), ())), preferred_element_type=F32
            )
            part = part - low[i, t * third : (t + 1) * third, :].astype(F32) * dot
            for u in range(3):
                v = 3 * t + u
                chunk = part[u * MAIN : (u + 1) * MAIN]
                if v < NW:
                    store(v, 0, MAIN, chunk)
                else:
                    for q in range(NW):
                        store(q, MAIN, FEAT, chunk[q * TAIL : (q + 1) * TAIL])

    def to_other(v, lo, hi, chunk):
        p_send[v, lo:hi, :] = chunk.astype(BF16)

    def to_own(v, lo, hi, chunk):
        p_own[v, lo:hi, :] = chunk

    image_part(1 - core, to_other)
    pair = remote(p_send, p_recv, s_ss.at[1], s_rs.at[1], other)
    pair.start()
    image_part(core, to_own)

    lane = lax.broadcasted_iota(jnp.int32, (8, MAIN), 1)

    def pieces(part, more, store):
        tail = part[:, NW * MAIN :]
        for v in range(NW):
            packed = more
            for q in range(4):
                shift = (32 * q - v * TAIL) % MAIN
                rest = tail[8 * q : 8 * q + 8]
                rest = pltpu.roll(rest, shift, 1) if shift else rest
                packed = jnp.where((lane >= 32 * q) & (lane < 32 * q + TAIL), rest, packed)
            rest = jnp.concatenate([packed, jnp.zeros((8, MAIN), F32)], axis=0)
            store(v, part[:, v * MAIN : (v + 1) * MAIN].astype(BF16), rest.astype(BF16))

    def to_row(v, main, rest):
        g_send[v, :ROWS, :] = main
        g_send[v, ROWS:, :] = rest

    g_copies = [
        remote(g_send.at[lax.rem(w + j, NW)], g_recv.at[w], g_ss.at[j], g_rs.at[j], across(j)) for j in range(1, NW)
    ]

    def send_own():
        scaled = unit[...]
        part = keep[PLACE[0]]
        part = part - scaled * jnp.sum(scaled * part, axis=1, keepdims=True)
        norm = tnorm[...]
        high = norm.astype(BF16).astype(F32)
        norms = jnp.zeros((8, MAIN), F32)
        for q in range(4):
            norms = jnp.where(lane == 32 * q + TAIL, high[8 * q : 8 * q + 8], norms)
            norms = jnp.where(lane == 32 * q + TAIL + 1, (norm - high)[8 * q : 8 * q + 8], norms)
        pieces(part, norms, to_row)
        for copy in g_copies:
            copy.start()
        g_recv[w] = g_send[w]

    pl.when(y != NY - 2)(send_own)

    pair.wait_recv()
    for v in range(NW):
        p_own[v] = p_own[v] + p_recv[v].astype(F32)
        e_send[v] = p_own[v].astype(BF16)
    def along_x(piece, slot, j):
        return remote(e_send.at[piece], e_recv.at[slot], e_ss.at[slot], e_rs.at[slot], (dp, base + near(j)))

    e_copies = [along_x(base2 + near(j), NX + j, j) for j in (1, 3, 2)]
    e_copies += [along_x(base + near(1), 1, 1), along_x(base + near(2), 2, 3)]
    e_last = along_x(base + near(3), 3, 3)
    for copy in e_copies:
        copy.start()

    h_copies = []
    for t, d in ((0, 5), (1, 2)):
        owner = lax.rem(chip - d + chips, chips) * 2 + core
        for j in range(NW):
            to = lax.rem(w + j, NW)
            h_copies.append(
                remote(h_send.at[t, to], h_recv.at[t, w], h_ss.at[t, j], h_rs.at[t, j], (owner, to))
            )

    def send_home(t, d, part):
        text = txt[rows_of(d), :].astype(F32)
        part = part - text * jnp.sum(text * part, axis=1, keepdims=True)

        def to_home(v, main, rest):
            h_send[t, v, :ROWS, :] = main
            h_send[t, v, ROWS:, :] = rest

        pieces(part, jnp.zeros((8, MAIN), F32), to_home)
        for copy in h_copies[t * NW : (t + 1) * NW]:
            copy.start()

    def text_sums():
        @pl.when(y != 0)
        def _():
            add_part(PLACE[5], 4)

        @pl.when(core == 1)
        def _():
            add_part(PLACE[5], 6)

        @pl.when(y == 2)
        def _():
            add_part(PLACE[5], 5)

        send_home(0, 5, keep[PLACE[5]])

        @pl.when(y != 0)
        def _():
            add_part(PLACE[2], 1)

        @pl.when(y != NY - 1)
        def _():
            add_part(PLACE[2], 3)

        @pl.when(y == NY - 3)
        def _():
            add_part(PLACE[2], 2)

        send_home(1, 2, keep[PLACE[2]])

    z_back = remote(z_send, z_recv, z_ss.at[0], z_rs.at[0], partner)

    def image_sums():
        grad = p_own[w2]
        for j, copy in zip((1, 3, 2), e_copies[:3]):
            copy.wait_recv()
            grad = grad + e_recv[NX + j].astype(F32)
        z_send[...] = grad.astype(BF16)
        z_back.start()

    pl.when(core == 1)(image_sums)
    text_sums()
    pl.when(core == 0)(image_sums)
    e_copies[4].wait_recv()
    e_send[base + near(3)] = (p_own[base + near(3)] + e_recv[2].astype(F32)).astype(BF16)
    e_last.start()

    @pl.when(y == NY - 2)
    def _():
        add_part(PLACE[0], 0)
        send_own()

    grad = p_own[w]
    for j, copy in ((1, e_copies[3]), (3, e_last)):
        copy.wait_recv()
        grad = grad + e_recv[j].astype(F32)
    z_back.wait_recv()
    grad = grad + z_recv[...].astype(F32)
    out[:FEAT] = grad * inorm
    for copy in g_copies + h_copies:
        copy.wait_recv()
    whole = g_recv[...].astype(F32) + h_recv[0].astype(F32) + h_recv[1].astype(F32)
    txt_wide[:, :MAIN] = whole[:, :ROWS].reshape(COLS, MAIN)
    packed = whole[:, ROWS : ROWS + 8].reshape(NW * 8, MAIN)
    for q in range(4):
        rest = pltpu.roll(packed, MAIN - 32 * q, 1) if q else packed
        for v in range(NW):
            at = v * ROWS + 8 * q
            txt_wide[at : at + 8, MAIN:] = rest[8 * v : 8 * v + 8]
    whole = txt_wide[...].T
    out[FEAT:] = whole[:FEAT] * (whole[FEAT : FEAT + 1] + whole[FEAT + 1 : FEAT + 2])

    for copy in a_copies + b_copies + e_copies + g_copies + h_copies:
        copy.wait_send()
    for copy in (to2, to3, to5, share, pair, z_copy, z_back, e_last):
        copy.wait_send()
    for d in (1, 3, 4):
        back(d).wait_send()

    for here, copy in (
        (y != 0, to1),
        (y != 0, to4),
        (y == NY - 2, to1_last),
        (y == NY - 3, to4_last),
    ):
        pl.when(here)(copy.wait_send)

    @pl.when(core == 1)
    def _():
        to6.wait_send()
        back(6).wait_send()


def solution(mesh):
    chips = mesh.shape["dp"] // 2
    slots = len(ORDER)
    dma = pltpu.SemaphoreType.DMA

    def body(image_emb, text_emb, pair_offsets, log_scale, bias):
        shape = jax.ShapeDtypeStruct((2 * FEAT, COLS), F32)
        smem = pl.BlockSpec(memory_space=pltpu.SMEM)
        hbm = pl.BlockSpec(memory_space=pltpu.HBM)
        grads = pl.pallas_call(
            functools.partial(kernel, chips),
            out_shape=shape,
            in_specs=[hbm, hbm, hbm, smem, smem],
            out_specs=pl.BlockSpec(memory_space=pltpu.VMEM),
            scratch_shapes=[
                pltpu.SMEM((CYCLE,), jnp.int32),
                pltpu.VMEM((NW, FEAT, COLS), BF16),
                pltpu.VMEM((FEAT, COLS), BF16),
                pltpu.VMEM((COLS, COLS), F32),
                pltpu.VMEM((NW, ROWS, COLS), BF16),
                pltpu.VMEM((NW, ROWS, COLS), BF16),
                pltpu.VMEM((2, D, COLS), BF16),
                pltpu.VMEM((slots * ROWS, D), BF16),
                pltpu.VMEM((ROWS, D), F32),
                pltpu.VMEM((ROWS, MAIN), F32),
                pltpu.VMEM((2, slots * ROWS, COLS), BF16),
                pltpu.VMEM((2, 8, COLS), F32),
                pltpu.VMEM((slots, ROWS, D), BF16),
                pltpu.VMEM((slots, ROWS, D), BF16),
                pltpu.VMEM((NW, FEAT, COLS), BF16),
                pltpu.VMEM((NW, FEAT, COLS), BF16),
                pltpu.VMEM((NW, FEAT, COLS), F32),
                pltpu.VMEM((NW, FEAT, COLS), BF16),
                pltpu.VMEM((NW, FEAT, COLS), BF16),
                pltpu.VMEM((FEAT, COLS), BF16),
                pltpu.VMEM((FEAT, COLS), BF16),
                pltpu.VMEM((3, ROWS, D), F32),
                pltpu.VMEM((NW, ROWS + 16, MAIN), BF16),
                pltpu.VMEM((NW, ROWS + 16, MAIN), BF16),
                pltpu.VMEM((2, NW, ROWS + 16, MAIN), BF16),
                pltpu.VMEM((2, NW, ROWS + 16, MAIN), BF16),
                dma((3,)),
                dma((NW,)),
                dma((NW,)),
                dma((NW,)),
                dma((NW,)),
                dma((slots,)),
                dma((slots,)),
                dma((slots,)),
                dma((slots,)),
                dma((NW,)),
                dma((NW,)),
                dma((NW,)),
                dma((NW,)),
                dma((2,)),
                dma((2,)),
                dma((1,)),
                dma((1,)),
                dma((2, NW)),
                dma((2, NW)),
            ],
            compiler_params=pltpu.CompilerParams(
                collective_id=0, has_side_effects=True, vmem_limit_bytes=40 * 1024 * 1024
            ),
        )(
            *(pltpu.with_memory_space_constraint(v, pltpu.HBM) for v in (image_emb, text_emb, pair_offsets)), log_scale, bias
        )
        return grads[:FEAT], grads[FEAT:]

    placed = (P("width", "dp"), P("width", "dp"), P(), P(), P())
    return jax.shard_map(
        body,
        mesh=mesh,
        in_specs=placed,
        out_specs=(P("width", "dp"), P("width", "dp")),
        check_vma=False,
    )
```

```python
import functools

import jax
import jax.numpy as jnp
from jax import lax
from jax.experimental import pallas as pl
from jax.experimental.pallas import tpu as pltpu
from jax.sharding import PartitionSpec as P

MESH = pl.DeviceIdType.MESH
F32 = jnp.float32
BF16 = jnp.bfloat16
EPSILON = 1e-06
CYCLE = 12
NW = 8
NX = 4
FEAT = 144
MAIN = 128
TAIL = FEAT - MAIN
D = NW * FEAT
COLS = 256
ROWS = COLS // NW
NY = 8
REACH = 6
ORDER = (0, 2, 5, 1, 3, 4, 6)
PLACE = {d: i for i, d in enumerate(ORDER)}


def rows_of(d):
    return pl.ds(PLACE[d] * ROWS, ROWS)


def kernel(
    chips,
    img_hbm,
    txt_hbm,
    offsets_hbm,
    log_scale,
    bias,
    out,
    offsets,
    img_raw,
    txt_in,
    txt_wide,
    a_send,
    a_recv,
    low,
    txt,
    unit,
    tnorm,
    slopes,
    dots,
    f_send,
    f_recv,
    p_send,
    p_recv,
    p_own,
    e_send,
    e_recv,
    z_send,
    z_recv,
    keep,
    g_send,
    g_recv,
    h_send,
    h_recv,
    local_sem,
    a_ss,
    a_rs,
    b_ss,
    b_rs,
    c_ss,
    c_rs,
    f_ss,
    f_rs,
    e_ss,
    e_rs,
    g_ss,
    g_rs,
    s_ss,
    s_rs,
    z_ss,
    z_rs,
    h_ss,
    h_rs,
):
    dp = lax.axis_index("dp")
    w = lax.axis_index("width")
    chip = lax.div(dp, 2)
    core = lax.rem(dp, 2)

    def along(d):
        return (lax.rem(chip + d + chips, chips) * 2 + core, w)

    def across(j):
        return (dp, lax.rem(w + j, NW))

    other = (dp + 1 - 2 * core, w)
    y = lax.rem(chip, NY)
    first, last = y == 0, y == NY - 1
    x = lax.rem(w, NX)
    base = w - x
    base2 = NX - base
    w2 = base2 + x
    partner = (dp, w2)

    def near(j):
        return lax.rem(x + j, NX)

    def remote(src, dst, ss, rs, to):
        return pltpu.make_async_remote_copy(
            src_ref=src, dst_ref=dst, send_sem=ss, recv_sem=rs, device_id=to, device_id_type=MESH
        )

    get_txt = pltpu.make_async_copy(txt_hbm, txt_in, local_sem.at[0])
    get_img = pltpu.make_async_copy(img_hbm, img_raw.at[w], local_sem.at[1])
    get_txt.start()
    get_img.start()

    barrier = pltpu.get_barrier_semaphore()

    def arrive(peer):
        pl.semaphore_signal(barrier, inc=1, device_id=peer, device_id_type=MESH)

    for d in (-5, -2, -1):
        arrive(along(d))
    for j in range(1, NW):
        arrive(across(j))
    arrive(other)

    @pl.when(y != NY - 1)
    def _():
        arrive(along(1))

    get_offsets = pltpu.make_async_copy(offsets_hbm, offsets, local_sem.at[2])
    get_offsets.start()

    @pl.when(core == 0)
    def _():
        txt[rows_of(REACH), :] = jnp.zeros((ROWS, D), BF16)

    txt_wide[FEAT:, :] = jnp.zeros((COLS - FEAT, COLS), F32)
    dots[...] = jnp.zeros(dots.shape, F32)
    get_txt.wait()
    txt_wide[:FEAT, :] = txt_in[...].astype(F32)
    a_send[...] = txt_wide[...].T.astype(BF16).reshape(NW, ROWS, COLS)
    get_img.wait()
    get_offsets.wait()
    pl.semaphore_wait(barrier, jnp.where(first, NW + 3, NW + 4))

    z_copy = remote(img_raw.at[w], img_raw.at[w], b_ss.at[0], b_rs.at[0], partner)
    z_copy.start()
    a_copies = []
    for j in range(1, NW):
        copy = remote(a_send.at[lax.rem(w + j, NW)], a_recv.at[w], a_ss.at[j], a_rs.at[j], across(j))
        copy.start()
        a_copies.append(copy)
    a_recv[w] = a_send[w]
    for copy in a_copies:
        copy.wait_recv()
    b_copies = []
    for j in (1, 3, 2):
        copy = remote(img_raw.at[w], img_raw.at[w], b_ss.at[j], b_rs.at[j], (dp, base + near(j)))
        copy.start()
        b_copies.append(copy)

    tail = jnp.zeros((ROWS, MAIN), F32)
    for v in range(NW):
        piece = a_recv[v].astype(F32)
        unit[:, v * MAIN : (v + 1) * MAIN] = piece[:, :MAIN]
        rest = piece[:, MAIN:]
        tail = tail + (pltpu.roll(rest, v * TAIL, 1) if v else rest)
    unit[:, NW * MAIN :] = tail
    raw = unit[...]
    norm = lax.rsqrt(jnp.sum(raw * raw, axis=1, keepdims=True) + EPSILON)
    scaled = raw * norm
    unit[...] = scaled
    tnorm[...] = jnp.broadcast_to(norm, tnorm.shape)
    txt[rows_of(0), :] = scaled.astype(BF16)

    def pass_text(src, dst, to, sem=None):
        sem = dst if sem is None else sem
        return remote(txt.at[rows_of(src)], txt.at[rows_of(dst)], c_ss.at[sem], c_rs.at[dst], to)

    to2 = pass_text(0, 2, along(2))
    to5 = pass_text(0, 5, along(5))
    to5.start()
    to2.start()
    to1_last = pass_text(0, 1, along(1), 0)
    to4_last = pass_text(2, 4, along(2), 0)

    @pl.when(y == NY - 2)
    def _():
        to1_last.start()


    z_copy.wait_recv()
    for j in (1, 3, 2):
        copy = remote(img_raw.at[w2], img_raw.at[w2], b_ss.at[NX + j], b_rs.at[NX + j], (dp, base + near(j)))
        copy.start()
        b_copies.append(copy)

    to1 = pass_text(2, 1, along(-1))
    to3 = pass_text(2, 3, along(1))
    to4 = pass_text(5, 4, along(-1))
    to6 = pass_text(5, 6, along(1))

    def forward():
        to2.wait_recv()

        @pl.when(y != 0)
        def _():
            to1.start()

        to3.start()

        @pl.when(y == NY - 3)
        def _():
            to4_last.start()

        to5.wait_recv()

        @pl.when(y != 0)
        def _():
            to4.start()

        @pl.when(core == 1)
        def _():
            to6.start()

    pl.when(core == 1)(forward)

    def squares(v):
        return jnp.sum(jnp.square(img_raw[v].astype(F32)), axis=0, keepdims=True)

    total = squares(w) + squares(w2)
    for n, copy in enumerate(b_copies):
        copy.wait_recv()
        j = (1, 3, 2)[n % 3]
        total = total + squares((base if n < 3 else base2) + near(NX - j))
    inorm = lax.rsqrt(total + EPSILON)
    for v in range(NW):
        scaled = (img_raw[v].astype(F32) * inorm).astype(BF16)
        low[core, v * MAIN : (v + 1) * MAIN, :] = scaled[:MAIN]
        low[core, NW * MAIN + v * TAIL : NW * MAIN + (v + 1) * TAIL, :] = scaled[MAIN:]
    share = remote(low.at[core], low.at[core], s_ss.at[0], s_rs.at[0], other)
    share.start()

    pl.when(core == 0)(forward)

    temper = jnp.exp(jnp.full((1, COLS), log_scale[0], F32))
    shift = bias[0]
    col = lax.broadcasted_iota(jnp.int32, (ROWS, COLS), 1)
    row = lax.broadcasted_iota(jnp.int32, (ROWS, COLS), 0) + w * ROWS
    gap = col - row

    home = {
        1: (jnp.where(last, -1, 1), jnp.where(last, 0, 1)),
        3: (jnp.where(first, 2, -1), jnp.where(first, 5, 3)),
        4: (jnp.where(last, -2, 1), jnp.where(last, 2, 4)),
        6: (-1, 6),
    }

    def back(d):
        to, slot = home[d]
        return remote(f_send.at[d], f_recv.at[slot], f_ss.at[d], f_rs.at[slot], along(to))

    def add_part(place, slot):
        remote(f_send.at[slot], f_recv.at[slot], f_ss.at[slot], f_rs.at[slot], other).wait_recv()
        keep[place] = keep[place] + f_recv[slot].astype(F32)

    def meet(ds):
        first = PLACE[ds[0]] * ROWS
        size = len(ds) * ROWS
        here = txt[first : first + size, :]
        grad = jnp.zeros((size, D), F32)
        for i in range(2):
            logits = jnp.dot(here, low[i], preferred_element_type=F32)
            parts = []
            dot = jnp.zeros((1, COLS), F32)
            for n, d in enumerate(ds):
                step = 2 * d + i - core
                met = jnp.logical_and(step >= 0, step < CYCLE).astype(F32)
                offset = offsets[jnp.clip(step, 0, CYCLE - 1)]
                own = logits[n * ROWS : (n + 1) * ROWS]
                positive = (((gap - offset) & (COLS - 1)) == 0).astype(F32)
                slope = (temper * (jax.nn.sigmoid(temper * own + shift) - positive)) * met
                slope = slope.astype(BF16)
                dot = dot + jnp.sum(slope.astype(F32) * own, axis=0, keepdims=True)
                slopes[i, (PLACE[d]) * ROWS : (PLACE[d] + 1) * ROWS, :] = slope
                parts.append(slope)
            dots[i] = dots[i] + jnp.broadcast_to(dot, dots.shape[1:])
            grad = grad + lax.dot_general(
                slopes[i, first : first + size, :], low[i], (((1,), (1,)), ((), ())), preferred_element_type=F32
            )
        for n, d in enumerate(ds):
            part = grad[n * ROWS : (n + 1) * ROWS]
            if d in (0, 2, 5):
                keep[PLACE[d]] = part
            else:
                f_send[d] = part.astype(BF16)

    share.wait_recv()
    meet((0, 2, 5))
    to1.wait_recv()
    to3.wait_recv()
    to4.wait_recv()

    @pl.when(core == 1)
    def _():
        to6.wait_recv()

    meet((1, 3, 4, 6))
    for d in (4, 3, 1):
        back(d).start()

    @pl.when(core == 1)
    def _():
        back(6).start()

    def image_part(i, store):
        third = D // 3
        dot = dots[i][:1]
        for t in range(3):
            part = lax.dot_general(
                txt[:, t * third : (t + 1) * third], slopes[i], (((0,), (0,)), ((), ())), preferred_element_type=F32
            )
            part = part - low[i, t * third : (t + 1) * third, :].astype(F32) * dot
            for u in range(3):
                v = 3 * t + u
                chunk = part[u * MAIN : (u + 1) * MAIN]
                if v < NW:
                    store(v, 0, MAIN, chunk)
                else:
                    for q in range(NW):
                        store(q, MAIN, FEAT, chunk[q * TAIL : (q + 1) * TAIL])

    def to_other(v, lo, hi, chunk):
        p_send[v, lo:hi, :] = chunk.astype(BF16)

    def to_own(v, lo, hi, chunk):
        p_own[v, lo:hi, :] = chunk

    image_part(1 - core, to_other)
    pair = remote(p_send, p_recv, s_ss.at[1], s_rs.at[1], other)
    pair.start()
    image_part(core, to_own)

    lane = lax.broadcasted_iota(jnp.int32, (8, MAIN), 1)

    def pieces(part, more, store):
        tail = part[:, NW * MAIN :]
        for v in range(NW):
            packed = more
            for q in range(4):
                shift = (32 * q - v * TAIL) % MAIN
                rest = tail[8 * q : 8 * q + 8]
                rest = pltpu.roll(rest, shift, 1) if shift else rest
                packed = jnp.where((lane >= 32 * q) & (lane < 32 * q + TAIL), rest, packed)
            rest = jnp.concatenate([packed, jnp.zeros((8, MAIN), F32)], axis=0)
            store(v, part[:, v * MAIN : (v + 1) * MAIN].astype(BF16), rest.astype(BF16))

    def to_row(v, main, rest):
        g_send[v, :ROWS, :] = main
        g_send[v, ROWS:, :] = rest

    g_copies = [
        remote(g_send.at[lax.rem(w + j, NW)], g_recv.at[w], g_ss.at[j], g_rs.at[j], across(j)) for j in range(1, NW)
    ]

    def send_own():
        scaled = unit[...]
        part = keep[PLACE[0]]
        part = part - scaled * jnp.sum(scaled * part, axis=1, keepdims=True)
        norm = tnorm[...]
        high = norm.astype(BF16).astype(F32)
        norms = jnp.zeros((8, MAIN), F32)
        for q in range(4):
            norms = jnp.where(lane == 32 * q + TAIL, high[8 * q : 8 * q + 8], norms)
            norms = jnp.where(lane == 32 * q + TAIL + 1, (norm - high)[8 * q : 8 * q + 8], norms)
        pieces(part, norms, to_row)
        for copy in g_copies:
            copy.start()
        g_recv[w] = g_send[w]

    pl.when(y != NY - 2)(send_own)

    pair.wait_recv()
    for v in range(NW):
        p_own[v] = p_own[v] + p_recv[v].astype(F32)
        e_send[v] = p_own[v].astype(BF16)
    def along_x(piece, slot, j):
        return remote(e_send.at[piece], e_recv.at[slot], e_ss.at[slot], e_rs.at[slot], (dp, base + near(j)))

    e_copies = [along_x(base2 + near(j), NX + j, j) for j in (1, 3, 2)]
    e_copies += [along_x(base + near(1), 1, 1), along_x(base + near(2), 2, 3)]
    e_last = along_x(base + near(3), 3, 3)
    for copy in e_copies:
        copy.start()

    h_copies = []
    for t, d in ((0, 5), (1, 2)):
        owner = lax.rem(chip - d + chips, chips) * 2 + core
        for j in range(NW):
            to = lax.rem(w + j, NW)
            h_copies.append(
                remote(h_send.at[t, to], h_recv.at[t, w], h_ss.at[t, j], h_rs.at[t, j], (owner, to))
            )

    def send_home(t, d, part):
        text = txt[rows_of(d), :].astype(F32)
        part = part - text * jnp.sum(text * part, axis=1, keepdims=True)

        def to_home(v, main, rest):
            h_send[t, v, :ROWS, :] = main
            h_send[t, v, ROWS:, :] = rest

        pieces(part, jnp.zeros((8, MAIN), F32), to_home)
        for copy in h_copies[t * NW : (t + 1) * NW]:
            copy.start()

    def far_sums():
        @pl.when(y != 0)
        def _():
            add_part(PLACE[5], 4)

        @pl.when(core == 1)
        def _():
            add_part(PLACE[5], 6)

        @pl.when(y == 2)
        def _():
            add_part(PLACE[5], 5)

        send_home(0, 5, keep[PLACE[5]])

    def near_sums():
        @pl.when(y != 0)
        def _():
            add_part(PLACE[2], 1)

        @pl.when(y != NY - 1)
        def _():
            add_part(PLACE[2], 3)

        @pl.when(y == NY - 3)
        def _():
            add_part(PLACE[2], 2)

        send_home(1, 2, keep[PLACE[2]])

    z_back = remote(z_send, z_recv, z_ss.at[0], z_rs.at[0], partner)

    def image_sums():
        grad = p_own[w2]
        for j, copy in zip((1, 3, 2), e_copies[:3]):
            copy.wait_recv()
            grad = grad + e_recv[NX + j].astype(F32)
        z_send[...] = grad.astype(BF16)
        z_back.start()

    far_sums()
    pl.when(core == 1)(image_sums)
    near_sums()
    pl.when(core == 0)(image_sums)
    e_copies[4].wait_recv()
    e_send[base + near(3)] = (p_own[base + near(3)] + e_recv[2].astype(F32)).astype(BF16)
    e_last.start()

    @pl.when(y == NY - 2)
    def _():
        add_part(PLACE[0], 0)
        send_own()

    grad = p_own[w]
    for j, copy in ((1, e_copies[3]), (3, e_last)):
        copy.wait_recv()
        grad = grad + e_recv[j].astype(F32)
    z_back.wait_recv()
    grad = grad + z_recv[...].astype(F32)
    out[:FEAT] = grad * inorm
    for copy in g_copies + h_copies:
        copy.wait_recv()
    whole = g_recv[...].astype(F32) + h_recv[0].astype(F32) + h_recv[1].astype(F32)
    txt_wide[:, :MAIN] = whole[:, :ROWS].reshape(COLS, MAIN)
    packed = whole[:, ROWS : ROWS + 8].reshape(NW * 8, MAIN)
    for q in range(4):
        rest = pltpu.roll(packed, MAIN - 32 * q, 1) if q else packed
        for v in range(NW):
            at = v * ROWS + 8 * q
            txt_wide[at : at + 8, MAIN:] = rest[8 * v : 8 * v + 8]
    whole = txt_wide[...].T
    out[FEAT:] = whole[:FEAT] * (whole[FEAT : FEAT + 1] + whole[FEAT + 1 : FEAT + 2])

    for copy in a_copies + b_copies + e_copies + g_copies + h_copies:
        copy.wait_send()
    for copy in (to2, to3, to5, share, pair, z_copy, z_back, e_last):
        copy.wait_send()
    for d in (1, 3, 4):
        back(d).wait_send()

    for here, copy in (
        (y != 0, to1),
        (y != 0, to4),
        (y == NY - 2, to1_last),
        (y == NY - 3, to4_last),
    ):
        pl.when(here)(copy.wait_send)

    @pl.when(core == 1)
    def _():
        to6.wait_send()
        back(6).wait_send()


def solution(mesh):
    chips = mesh.shape["dp"] // 2
    slots = len(ORDER)
    dma = pltpu.SemaphoreType.DMA

    def body(image_emb, text_emb, pair_offsets, log_scale, bias):
        shape = jax.ShapeDtypeStruct((2 * FEAT, COLS), F32)
        smem = pl.BlockSpec(memory_space=pltpu.SMEM)
        hbm = pl.BlockSpec(memory_space=pltpu.HBM)
        grads = pl.pallas_call(
            functools.partial(kernel, chips),
            out_shape=shape,
            in_specs=[hbm, hbm, hbm, smem, smem],
            out_specs=pl.BlockSpec(memory_space=pltpu.VMEM),
            scratch_shapes=[
                pltpu.SMEM((CYCLE,), jnp.int32),
                pltpu.VMEM((NW, FEAT, COLS), BF16),
                pltpu.VMEM((FEAT, COLS), BF16),
                pltpu.VMEM((COLS, COLS), F32),
                pltpu.VMEM((NW, ROWS, COLS), BF16),
                pltpu.VMEM((NW, ROWS, COLS), BF16),
                pltpu.VMEM((2, D, COLS), BF16),
                pltpu.VMEM((slots * ROWS, D), BF16),
                pltpu.VMEM((ROWS, D), F32),
                pltpu.VMEM((ROWS, MAIN), F32),
                pltpu.VMEM((2, slots * ROWS, COLS), BF16),
                pltpu.VMEM((2, 8, COLS), F32),
                pltpu.VMEM((slots, ROWS, D), BF16),
                pltpu.VMEM((slots, ROWS, D), BF16),
                pltpu.VMEM((NW, FEAT, COLS), BF16),
                pltpu.VMEM((NW, FEAT, COLS), BF16),
                pltpu.VMEM((NW, FEAT, COLS), F32),
                pltpu.VMEM((NW, FEAT, COLS), BF16),
                pltpu.VMEM((NW, FEAT, COLS), BF16),
                pltpu.VMEM((FEAT, COLS), BF16),
                pltpu.VMEM((FEAT, COLS), BF16),
                pltpu.VMEM((3, ROWS, D), F32),
                pltpu.VMEM((NW, ROWS + 16, MAIN), BF16),
                pltpu.VMEM((NW, ROWS + 16, MAIN), BF16),
                pltpu.VMEM((2, NW, ROWS + 16, MAIN), BF16),
                pltpu.VMEM((2, NW, ROWS + 16, MAIN), BF16),
                dma((3,)),
                dma((NW,)),
                dma((NW,)),
                dma((NW,)),
                dma((NW,)),
                dma((slots,)),
                dma((slots,)),
                dma((slots,)),
                dma((slots,)),
                dma((NW,)),
                dma((NW,)),
                dma((NW,)),
                dma((NW,)),
                dma((2,)),
                dma((2,)),
                dma((1,)),
                dma((1,)),
                dma((2, NW)),
                dma((2, NW)),
            ],
            compiler_params=pltpu.CompilerParams(
                collective_id=0, has_side_effects=True, vmem_limit_bytes=40 * 1024 * 1024
            ),
        )(
            *(pltpu.with_memory_space_constraint(v, pltpu.HBM) for v in (image_emb, text_emb, pair_offsets)), log_scale, bias
        )
        return grads[:FEAT], grads[FEAT:]

    placed = (P("width", "dp"), P("width", "dp"), P(), P(), P())
    return jax.shard_map(
        body,
        mesh=mesh,
        in_specs=placed,
        out_specs=(P("width", "dp"), P("width", "dp")),
        check_vma=False,
    )
```

```python
import functools

import jax
import jax.numpy as jnp
from jax import lax
from jax.experimental import pallas as pl
from jax.experimental.pallas import tpu as pltpu
from jax.sharding import PartitionSpec as P

MESH = pl.DeviceIdType.MESH
F32 = jnp.float32
BF16 = jnp.bfloat16
EPSILON = 1e-06
CYCLE = 12
NW = 8
NX = 4
FEAT = 144
MAIN = 128
TAIL = FEAT - MAIN
D = NW * FEAT
COLS = 256
ROWS = COLS // NW
NY = 8
REACH = 6
ORDER = (0, 2, 5, 1, 3, 4, 6)
PLACE = {d: i for i, d in enumerate(ORDER)}


def rows_of(d):
    return pl.ds(PLACE[d] * ROWS, ROWS)


def kernel(
    chips,
    img_hbm,
    txt_hbm,
    offsets_hbm,
    log_scale,
    bias,
    out,
    offsets,
    img_raw,
    txt_in,
    txt_wide,
    a_send,
    a_recv,
    low,
    txt,
    unit,
    tnorm,
    slopes,
    dots,
    f_send,
    f_recv,
    p_send,
    p_recv,
    p_own,
    e_send,
    e_recv,
    z_send,
    z_recv,
    keep,
    g_send,
    g_recv,
    h_send,
    h_recv,
    local_sem,
    a_ss,
    a_rs,
    b_ss,
    b_rs,
    c_ss,
    c_rs,
    f_ss,
    f_rs,
    e_ss,
    e_rs,
    g_ss,
    g_rs,
    s_ss,
    s_rs,
    z_ss,
    z_rs,
    h_ss,
    h_rs,
):
    dp = lax.axis_index("dp")
    w = lax.axis_index("width")
    chip = lax.div(dp, 2)
    core = lax.rem(dp, 2)

    def along(d):
        return (lax.rem(chip + d + chips, chips) * 2 + core, w)

    def across(j):
        return (dp, lax.rem(w + j, NW))

    other = (dp + 1 - 2 * core, w)
    y = lax.rem(chip, NY)
    first, last = y == 0, y == NY - 1
    x = lax.rem(w, NX)
    base = w - x
    base2 = NX - base
    w2 = base2 + x
    partner = (dp, w2)

    def near(j):
        return lax.rem(x + j, NX)

    def remote(src, dst, ss, rs, to):
        return pltpu.make_async_remote_copy(
            src_ref=src, dst_ref=dst, send_sem=ss, recv_sem=rs, device_id=to, device_id_type=MESH
        )

    get_txt = pltpu.make_async_copy(txt_hbm, txt_in, local_sem.at[0])
    get_img = pltpu.make_async_copy(img_hbm, img_raw.at[w], local_sem.at[1])
    get_txt.start()
    get_img.start()

    barrier = pltpu.get_barrier_semaphore()

    def arrive(peer):
        pl.semaphore_signal(barrier, inc=1, device_id=peer, device_id_type=MESH)

    for d in (-5, -2, -1):
        arrive(along(d))
    for j in range(1, NW):
        arrive(across(j))
    arrive(other)

    @pl.when(y != NY - 1)
    def _():
        arrive(along(1))

    get_offsets = pltpu.make_async_copy(offsets_hbm, offsets, local_sem.at[2])
    get_offsets.start()

    @pl.when(core == 0)
    def _():
        txt[rows_of(REACH), :] = jnp.zeros((ROWS, D), BF16)

    txt_wide[FEAT:, :] = jnp.zeros((COLS - FEAT, COLS), F32)
    dots[...] = jnp.zeros(dots.shape, F32)
    get_txt.wait()
    txt_wide[:FEAT, :] = txt_in[...].astype(F32)
    a_send[...] = txt_wide[...].T.astype(BF16).reshape(NW, ROWS, COLS)
    get_img.wait()
    get_offsets.wait()
    pl.semaphore_wait(barrier, jnp.where(first, NW + 3, NW + 4))

    z_copy = remote(img_raw.at[w], img_raw.at[w], b_ss.at[0], b_rs.at[0], partner)
    z_copy.start()
    a_copies = []
    for j in range(1, NW):
        copy = remote(a_send.at[lax.rem(w + j, NW)], a_recv.at[w], a_ss.at[j], a_rs.at[j], across(j))
        copy.start()
        a_copies.append(copy)
    a_recv[w] = a_send[w]
    for copy in a_copies:
        copy.wait_recv()
    b_copies = []
    for j in (1, 3, 2):
        copy = remote(img_raw.at[w], img_raw.at[w], b_ss.at[j], b_rs.at[j], (dp, base + near(j)))
        copy.start()
        b_copies.append(copy)

    tail = jnp.zeros((ROWS, MAIN), F32)
    for v in range(NW):
        piece = a_recv[v].astype(F32)
        unit[:, v * MAIN : (v + 1) * MAIN] = piece[:, :MAIN]
        rest = piece[:, MAIN:]
        tail = tail + (pltpu.roll(rest, v * TAIL, 1) if v else rest)
    unit[:, NW * MAIN :] = tail
    raw = unit[...]
    norm = lax.rsqrt(jnp.sum(raw * raw, axis=1, keepdims=True) + EPSILON)
    scaled = raw * norm
    unit[...] = scaled
    tnorm[...] = jnp.broadcast_to(norm, tnorm.shape)
    txt[rows_of(0), :] = scaled.astype(BF16)

    def pass_text(src, dst, to, sem=None):
        sem = dst if sem is None else sem
        return remote(txt.at[rows_of(src)], txt.at[rows_of(dst)], c_ss.at[sem], c_rs.at[dst], to)

    to2 = pass_text(0, 2, along(2))
    to5 = pass_text(0, 5, along(5))
    to5.start()
    to2.start()
    to1_last = pass_text(0, 1, along(1), 0)
    to4_last = pass_text(2, 4, along(2), 0)

    @pl.when(y == NY - 2)
    def _():
        to1_last.start()


    z_copy.wait_recv()
    for j in (1, 3, 2):
        copy = remote(img_raw.at[w2], img_raw.at[w2], b_ss.at[NX + j], b_rs.at[NX + j], (dp, base + near(j)))
        copy.start()
        b_copies.append(copy)

    to1 = pass_text(2, 1, along(-1))
    to3 = pass_text(2, 3, along(1))
    to4 = pass_text(5, 4, along(-1))
    to6 = pass_text(5, 6, along(1))

    def forward():
        to2.wait_recv()

        @pl.when(y != 0)
        def _():
            to1.start()

        to3.start()

        @pl.when(y == NY - 3)
        def _():
            to4_last.start()

        to5.wait_recv()

        @pl.when(y != 0)
        def _():
            to4.start()

        @pl.when(core == 1)
        def _():
            to6.start()

    pl.when(core == 1)(forward)

    def squares(v):
        return jnp.sum(jnp.square(img_raw[v].astype(F32)), axis=0, keepdims=True)

    total = squares(w) + squares(w2)
    for n, copy in enumerate(b_copies):
        copy.wait_recv()
        j = (1, 3, 2)[n % 3]
        total = total + squares((base if n < 3 else base2) + near(NX - j))
    inorm = lax.rsqrt(total + EPSILON)
    for v in range(NW):
        scaled = (img_raw[v].astype(F32) * inorm).astype(BF16)
        low[core, v * MAIN : (v + 1) * MAIN, :] = scaled[:MAIN]
        low[core, NW * MAIN + v * TAIL : NW * MAIN + (v + 1) * TAIL, :] = scaled[MAIN:]
    share = remote(low.at[core], low.at[core], s_ss.at[0], s_rs.at[0], other)
    share.start()

    pl.when(core == 0)(forward)

    temper = jnp.exp(jnp.full((1, COLS), log_scale[0], F32))
    shift = bias[0]
    col = lax.broadcasted_iota(jnp.int32, (ROWS, COLS), 1)
    row = lax.broadcasted_iota(jnp.int32, (ROWS, COLS), 0) + w * ROWS
    gap = col - row

    home = {
        1: (jnp.where(last, -1, 1), jnp.where(last, 0, 1)),
        3: (-1, 3),
        4: (jnp.where(last, -2, 1), jnp.where(last, 2, 4)),
        6: (-1, 6),
    }

    def back(d):
        to, slot = home[d]
        return remote(f_send.at[d], f_recv.at[slot], f_ss.at[d], f_rs.at[slot], along(to))

    def add_part(place, slot):
        remote(f_send.at[slot], f_recv.at[slot], f_ss.at[slot], f_rs.at[slot], other).wait_recv()
        keep[place] = keep[place] + f_recv[slot].astype(F32)

    def meet(ds):
        first = PLACE[ds[0]] * ROWS
        size = len(ds) * ROWS
        here = txt[first : first + size, :]
        grad = jnp.zeros((size, D), F32)
        for i in range(2):
            logits = jnp.dot(here, low[i], preferred_element_type=F32)
            parts = []
            dot = jnp.zeros((1, COLS), F32)
            for n, d in enumerate(ds):
                step = 2 * d + i - core
                met = jnp.logical_and(step >= 0, step < CYCLE).astype(F32)
                offset = offsets[jnp.clip(step, 0, CYCLE - 1)]
                own = logits[n * ROWS : (n + 1) * ROWS]
                positive = (((gap - offset) & (COLS - 1)) == 0).astype(F32)
                slope = (temper * (jax.nn.sigmoid(temper * own + shift) - positive)) * met
                slope = slope.astype(BF16)
                dot = dot + jnp.sum(slope.astype(F32) * own, axis=0, keepdims=True)
                slopes[i, (PLACE[d]) * ROWS : (PLACE[d] + 1) * ROWS, :] = slope
                parts.append(slope)
            dots[i] = dots[i] + jnp.broadcast_to(dot, dots.shape[1:])
            grad = grad + lax.dot_general(
                slopes[i, first : first + size, :], low[i], (((1,), (1,)), ((), ())), preferred_element_type=F32
            )
        for n, d in enumerate(ds):
            part = grad[n * ROWS : (n + 1) * ROWS]
            if d in (0, 2, 5):
                keep[PLACE[d]] = part
            else:
                f_send[d] = part.astype(BF16)

    share.wait_recv()
    meet((0, 2, 5))
    to1.wait_recv()
    to3.wait_recv()
    to4.wait_recv()

    @pl.when(core == 1)
    def _():
        to6.wait_recv()

    meet((1, 3, 4, 6))
    for d in (4, 3, 1):
        back(d).start()

    @pl.when(core == 1)
    def _():
        back(6).start()

    def image_part(i, store):
        third = D // 3
        dot = dots[i][:1]
        for t in range(3):
            part = lax.dot_general(
                txt[:, t * third : (t + 1) * third], slopes[i], (((0,), (0,)), ((), ())), preferred_element_type=F32
            )
            part = part - low[i, t * third : (t + 1) * third, :].astype(F32) * dot
            for u in range(3):
                v = 3 * t + u
                chunk = part[u * MAIN : (u + 1) * MAIN]
                if v < NW:
                    store(v, 0, MAIN, chunk)
                else:
                    for q in range(NW):
                        store(q, MAIN, FEAT, chunk[q * TAIL : (q + 1) * TAIL])

    def to_other(v, lo, hi, chunk):
        p_send[v, lo:hi, :] = chunk.astype(BF16)

    def to_own(v, lo, hi, chunk):
        p_own[v, lo:hi, :] = chunk

    image_part(1 - core, to_other)
    pair = remote(p_send, p_recv, s_ss.at[1], s_rs.at[1], other)
    pair.start()
    image_part(core, to_own)

    lane = lax.broadcasted_iota(jnp.int32, (8, MAIN), 1)

    def pieces(part, more, store):
        tail = part[:, NW * MAIN :]
        for v in range(NW):
            packed = more
            for q in range(4):
                shift = (32 * q - v * TAIL) % MAIN
                rest = tail[8 * q : 8 * q + 8]
                rest = pltpu.roll(rest, shift, 1) if shift else rest
                packed = jnp.where((lane >= 32 * q) & (lane < 32 * q + TAIL), rest, packed)
            rest = jnp.concatenate([packed, jnp.zeros((8, MAIN), F32)], axis=0)
            store(v, part[:, v * MAIN : (v + 1) * MAIN].astype(BF16), rest.astype(BF16))

    def to_row(v, main, rest):
        g_send[v, :ROWS, :] = main
        g_send[v, ROWS:, :] = rest

    g_copies = [
        remote(g_send.at[lax.rem(w + j, NW)], g_recv.at[w], g_ss.at[j], g_rs.at[j], across(j)) for j in range(1, NW)
    ]

    def send_own():
        scaled = unit[...]
        part = keep[PLACE[0]]
        part = part - scaled * jnp.sum(scaled * part, axis=1, keepdims=True)
        norm = tnorm[...]
        high = norm.astype(BF16).astype(F32)
        norms = jnp.zeros((8, MAIN), F32)
        for q in range(4):
            norms = jnp.where(lane == 32 * q + TAIL, high[8 * q : 8 * q + 8], norms)
            norms = jnp.where(lane == 32 * q + TAIL + 1, (norm - high)[8 * q : 8 * q + 8], norms)
        pieces(part, norms, to_row)
        for copy in g_copies:
            copy.start()
        g_recv[w] = g_send[w]

    pl.when(y != NY - 2)(send_own)

    pair.wait_recv()
    for v in range(NW):
        p_own[v] = p_own[v] + p_recv[v].astype(F32)
        e_send[v] = p_own[v].astype(BF16)
    def along_x(piece, slot, j):
        return remote(e_send.at[piece], e_recv.at[slot], e_ss.at[slot], e_rs.at[slot], (dp, base + near(j)))

    e_copies = [along_x(base2 + near(j), NX + j, j) for j in (1, 3, 2)]
    e_copies += [along_x(base + near(1), 1, 1), along_x(base + near(2), 2, 3)]
    e_last = along_x(base + near(3), 3, 3)
    for copy in e_copies:
        copy.start()

    h_copies = []
    for t, d in ((0, 5), (1, 2)):
        owner = lax.rem(chip - d + chips, chips) * 2 + core
        for j in range(NW):
            to = lax.rem(w + j, NW)
            h_copies.append(
                remote(h_send.at[t, to], h_recv.at[t, w], h_ss.at[t, j], h_rs.at[t, j], (owner, to))
            )

    def send_home(t, d, part):
        text = txt[rows_of(d), :].astype(F32)
        part = part - text * jnp.sum(text * part, axis=1, keepdims=True)

        def to_home(v, main, rest):
            h_send[t, v, :ROWS, :] = main
            h_send[t, v, ROWS:, :] = rest

        pieces(part, jnp.zeros((8, MAIN), F32), to_home)
        for copy in h_copies[t * NW : (t + 1) * NW]:
            copy.start()

    def far_sums():
        @pl.when(y != 0)
        def _():
            add_part(PLACE[5], 4)

        @pl.when(core == 1)
        def _():
            add_part(PLACE[5], 6)

        send_home(0, 5, keep[PLACE[5]])

    def near_sums():
        @pl.when(y != 0)
        def _():
            add_part(PLACE[2], 1)

        add_part(PLACE[2], 3)

        @pl.when(y == NY - 3)
        def _():
            add_part(PLACE[2], 2)

        send_home(1, 2, keep[PLACE[2]])

    z_back = remote(z_send, z_recv, z_ss.at[0], z_rs.at[0], partner)

    def image_sums():
        grad = p_own[w2]
        for j, copy in zip((1, 3, 2), e_copies[:3]):
            copy.wait_recv()
            grad = grad + e_recv[NX + j].astype(F32)
        z_send[...] = grad.astype(BF16)
        z_back.start()

    far_sums()
    pl.when(core == 1)(image_sums)
    near_sums()
    pl.when(core == 0)(image_sums)
    e_copies[4].wait_recv()
    e_send[base + near(3)] = (p_own[base + near(3)] + e_recv[2].astype(F32)).astype(BF16)
    e_last.start()

    @pl.when(y == NY - 2)
    def _():
        add_part(PLACE[0], 0)
        send_own()

    grad = p_own[w]
    for j, copy in ((1, e_copies[3]), (3, e_last)):
        copy.wait_recv()
        grad = grad + e_recv[j].astype(F32)
    z_back.wait_recv()
    grad = grad + z_recv[...].astype(F32)
    out[:FEAT] = grad * inorm
    for copy in g_copies + h_copies:
        copy.wait_recv()
    whole = g_recv[...].astype(F32) + h_recv[0].astype(F32) + h_recv[1].astype(F32)
    txt_wide[:, :MAIN] = whole[:, :ROWS].reshape(COLS, MAIN)
    packed = whole[:, ROWS : ROWS + 8].reshape(NW * 8, MAIN)
    for q in range(4):
        rest = pltpu.roll(packed, MAIN - 32 * q, 1) if q else packed
        for v in range(NW):
            at = v * ROWS + 8 * q
            txt_wide[at : at + 8, MAIN:] = rest[8 * v : 8 * v + 8]
    whole = txt_wide[...].T
    out[FEAT:] = whole[:FEAT] * (whole[FEAT : FEAT + 1] + whole[FEAT + 1 : FEAT + 2])

    for copy in a_copies + b_copies + e_copies + g_copies + h_copies:
        copy.wait_send()
    for copy in (to2, to3, to5, share, pair, z_copy, z_back, e_last):
        copy.wait_send()
    for d in (1, 3, 4):
        back(d).wait_send()

    for here, copy in (
        (y != 0, to1),
        (y != 0, to4),
        (y == NY - 2, to1_last),
        (y == NY - 3, to4_last),
    ):
        pl.when(here)(copy.wait_send)

    @pl.when(core == 1)
    def _():
        to6.wait_send()
        back(6).wait_send()


def solution(mesh):
    chips = mesh.shape["dp"] // 2
    slots = len(ORDER)
    dma = pltpu.SemaphoreType.DMA

    def body(image_emb, text_emb, pair_offsets, log_scale, bias):
        shape = jax.ShapeDtypeStruct((2 * FEAT, COLS), F32)
        smem = pl.BlockSpec(memory_space=pltpu.SMEM)
        hbm = pl.BlockSpec(memory_space=pltpu.HBM)
        grads = pl.pallas_call(
            functools.partial(kernel, chips),
            out_shape=shape,
            in_specs=[hbm, hbm, hbm, smem, smem],
            out_specs=pl.BlockSpec(memory_space=pltpu.VMEM),
            scratch_shapes=[
                pltpu.SMEM((CYCLE,), jnp.int32),
                pltpu.VMEM((NW, FEAT, COLS), BF16),
                pltpu.VMEM((FEAT, COLS), BF16),
                pltpu.VMEM((COLS, COLS), F32),
                pltpu.VMEM((NW, ROWS, COLS), BF16),
                pltpu.VMEM((NW, ROWS, COLS), BF16),
                pltpu.VMEM((2, D, COLS), BF16),
                pltpu.VMEM((slots * ROWS, D), BF16),
                pltpu.VMEM((ROWS, D), F32),
                pltpu.VMEM((ROWS, MAIN), F32),
                pltpu.VMEM((2, slots * ROWS, COLS), BF16),
                pltpu.VMEM((2, 8, COLS), F32),
                pltpu.VMEM((slots, ROWS, D), BF16),
                pltpu.VMEM((slots, ROWS, D), BF16),
                pltpu.VMEM((NW, FEAT, COLS), BF16),
                pltpu.VMEM((NW, FEAT, COLS), BF16),
                pltpu.VMEM((NW, FEAT, COLS), F32),
                pltpu.VMEM((NW, FEAT, COLS), BF16),
                pltpu.VMEM((NW, FEAT, COLS), BF16),
                pltpu.VMEM((FEAT, COLS), BF16),
                pltpu.VMEM((FEAT, COLS), BF16),
                pltpu.VMEM((3, ROWS, D), F32),
                pltpu.VMEM((NW, ROWS + 16, MAIN), BF16),
                pltpu.VMEM((NW, ROWS + 16, MAIN), BF16),
                pltpu.VMEM((2, NW, ROWS + 16, MAIN), BF16),
                pltpu.VMEM((2, NW, ROWS + 16, MAIN), BF16),
                dma((3,)),
                dma((NW,)),
                dma((NW,)),
                dma((NW,)),
                dma((NW,)),
                dma((slots,)),
                dma((slots,)),
                dma((slots,)),
                dma((slots,)),
                dma((NW,)),
                dma((NW,)),
                dma((NW,)),
                dma((NW,)),
                dma((2,)),
                dma((2,)),
                dma((1,)),
                dma((1,)),
                dma((2, NW)),
                dma((2, NW)),
            ],
            compiler_params=pltpu.CompilerParams(
                collective_id=0, has_side_effects=True, vmem_limit_bytes=40 * 1024 * 1024
            ),
        )(
            *(pltpu.with_memory_space_constraint(v, pltpu.HBM) for v in (image_emb, text_emb, pair_offsets)), log_scale, bias
        )
        return grads[:FEAT], grads[FEAT:]

    placed = (P("width", "dp"), P("width", "dp"), P(), P(), P())
    return jax.shard_map(
        body,
        mesh=mesh,
        in_specs=placed,
        out_specs=(P("width", "dp"), P("width", "dp")),
        check_vma=False,
    )
```
